32 devices in a mesh: dp: 8 (over z, x), head: 4 (over y, core).
Axes of the slice: x: 2, y: 2, z: 4, core: 2. Of those that a mesh axis runs over, the one named last changes fastest.
Arguments:
- activations: bfloat16 [16384, 768], P(('dp', 'head')), may hold values from -6 to 6
- first_gain: float32 [768], replicated, may hold values from 0.5 to 1.5
- first_shift: float32 [768], replicated, may hold values from -3 to 3
- query_weight: bfloat16 [768, 768], P(None, 'head'), may hold values from -0.21875 to 0.21875
- key_weight: bfloat16 [768, 768], P(None, 'head'), may hold values from -0.21875 to 0.21875
- value_weight: bfloat16 [768, 768], P(None, 'head'), may hold values from -0.21875 to 0.21875
- output_weight: bfloat16 [768, 768], P('head'), may hold values from -1.75 to 1.75
- second_gain: float32 [768], replicated, may hold values from 0.5 to 1.5
- second_shift: float32 [768], replicated, may hold values from -3 to 3
- router_weight: bfloat16 [768, 8], replicated, may hold values from -0.15625 to 0.15625
- expert_in: bfloat16 [8, 768, 3072], P('dp', None, 'head'), may hold values from -0.21875 to 0.21875
- expert_out: bfloat16 [8, 768, 3072], P('dp', None, 'head'), may hold values from -0.109375 to 0.109375
- expert_ids: int32 [16384, 2], P(('dp', 'head')), may hold values from 0 to 7, all different within a row
- capacity: int32 [8], replicated, may hold values from 96 to 192, as said below
- new_mask: int32 [8], replicated, may hold values from 0 to 1, as said below
- cotangent: bfloat16 [16384, 768], P(('dp', 'head')), may hold values from -6 to 6
Outputs:
- block_out: bfloat16 [16384, 768], P(('dp', 'head'))
- grad_input: float32 [16384, 768], P(('dp', 'head'))
- grad_first_gain: float32 [768], replicated
- grad_first_shift: float32 [768], replicated
- grad_query_weight: float32 [768, 768], P(None, 'head')
- grad_key_weight: float32 [768, 768], P(None, 'head')
- grad_value_weight: float32 [768, 768], P(None, 'head')
- grad_output_weight: float32 [768, 768], P('head')
- grad_second_gain: float32 [768], replicated
- grad_second_shift: float32 [768], replicated
- grad_router: float32 [768, 8], replicated
- grad_expert_in: float32 [8, 768, 3072], P('dp', None, 'head')
- grad_expert_out: float32 [8, 768, 3072], P('dp', None, 'head')
The draws below stay inside these ranges and needn't reach their ends.
Inputs may be any that keep to these rules, and one draw needn't show every extreme that they name: `expert_ids`: each token names two different experts. `capacity`: some expert has exactly 192. `new_mask`: both values occur.
All inputs are finite; a program needn't handle non-finite values.
Results may differ from the reference program's by a relative error of at most 0.017.
Values may be sent and summed in bfloat16 or wider, within the bound.
No kernel may reach another device: no remote copies, remote signals or barrier semaphores. Data moves between devices by JAX's collectives and lax.ppermute only.
A program may use at most 192 MiB of HBM per device.

```python
import jax
import jax.numpy as jnp
from jax import lax

D = 768
H = 12
HD = 64
FF = 3072
LENGTH = 1024
EXPERTS = 8
TOK_DEV = 512
TOKENS = 16384
CAP = 192


def draw_capacity(key, part):
    key = jax.random.fold_in(key, 11)
    value_key, upper_key, lower_key = jax.random.split(key, 3)
    lower_cap = (CAP + 1) // 2
    limits = jax.random.randint(value_key, (EXPERTS,), lower_cap, CAP + 1)
    upper_at = jax.random.randint(upper_key, (), 0, EXPERTS)
    lower_at = (upper_at + jax.random.randint(lower_key, (), 1, EXPERTS)) % EXPERTS
    return limits.at[upper_at].set(CAP).at[lower_at].set(lower_cap).astype(jnp.int32)


def draw_new_mask(key, part):
    key = jax.random.fold_in(key, 23)
    bit_key, order_key = jax.random.split(key)
    flag_bits = jax.random.randint(bit_key, (EXPERTS,), 0, 2)
    shuffled = jax.random.permutation(order_key, EXPERTS)
    return flag_bits.at[shuffled[0]].set(1).at[shuffled[1]].set(0).astype(jnp.int32)


def block_levels(stream_key, shape, cuts, low, largest):
    gain, own = 1.0, jax.random.fold_in(stream_key, 6)
    for dim, parts in cuts:
        heights = jnp.exp(jax.random.uniform(jax.random.fold_in(own, dim), (parts,), jnp.float32, low / len(cuts), largest / len(cuts)))
        gain = gain * jnp.repeat(heights, shape[dim] // parts).reshape([-1 if axis == dim else 1 for axis in range(len(shape))])
    return gain


def distinct(own_key, rows, number_of, top, lift):
    order = jax.random.permutation(jax.random.fold_in(own_key, 1), number_of)
    boost = order
    for power in range(3):
        boost = boost * boost // number_of
    boost = boost * lift // number_of
    lots = jax.random.randint(jax.random.fold_in(own_key, 2), (rows, number_of), 0, 4096) + boost
    sure = jax.random.permutation(jax.random.fold_in(own_key, 3), rows)[jnp.arange(number_of) % rows]
    lots = jnp.where(jnp.arange(rows)[:, None] == sure[None, :], 1 << 14, lots)
    score = lots * number_of + jnp.arange(number_of)
    return lax.top_k(score.astype(jnp.int32), top)[1].astype(jnp.int32)


def noise(rng, dims, scale, most, pieces=(), kind=jnp.bfloat16):
    array = scale * jax.random.normal(rng, dims, jnp.float32)
    if pieces:
        array = array * block_levels(rng, dims, pieces, -0.22, 0.18)
    return jnp.clip(array, -most, most).astype(kind)


def setup_inputs(seed: int = 0) -> dict:
    key_of = jax.random.split(jax.random.key(seed), 17)
    activations = noise(key_of[0], (TOKENS, D), 1.0, 6.0, ((0, 32),))
    first_gain = jnp.clip(1.0 + 0.1 * jax.random.normal(key_of[1], (D,), jnp.float32), 0.5, 1.5)
    first_shift = noise(key_of[2], (D,), 0.3, 3.0, (), jnp.float32)
    query_weight = noise(key_of[3], (D, H * HD), D ** -0.5, 0.21875, ((1, 4),))
    key_weight = noise(key_of[4], (D, H * HD), D ** -0.5, 0.21875, ((1, 4),))
    value_weight = noise(key_of[5], (D, H * HD), D ** -0.5, 0.21875, ((1, 4),))
    output_weight = noise(key_of[6], (H * HD, D), (H * HD // 64) ** -0.5, 1.75, ((0, 4),))
    second_gain = jnp.clip(1.0 + 0.1 * jax.random.normal(key_of[7], (D,), jnp.float32), 0.5, 1.5)
    second_shift = noise(key_of[8], (D,), 0.3, 3.0, (), jnp.float32)
    router_weight = noise(key_of[9], (D, EXPERTS), (2 * D) ** -0.5, 0.15625)
    expert_in = noise(key_of[10], (EXPERTS, D, FF), D ** -0.5, 0.21875, ((0, 8), (2, 4)))
    expert_out = noise(key_of[11], (EXPERTS, D, FF), FF ** -0.5, 0.109375, ((0, 8), (2, 4)))
    expert_ids = distinct(key_of[12], TOKENS, EXPERTS, 2, 4096)
    capacity = draw_capacity(jax.random.fold_in(key_of[16], 71), 0)
    new_mask = draw_new_mask(jax.random.fold_in(key_of[16], 71), 0)
    cotangent = noise(key_of[15], (TOKENS, D), 1.0, 6.0, ((0, 32),))
    return {"activations": activations, "first_gain": first_gain, "first_shift": first_shift, "query_weight": query_weight, "key_weight": key_weight, "value_weight": value_weight, "output_weight": output_weight, "second_gain": second_gain, "second_shift": second_shift, "router_weight": router_weight, "expert_in": expert_in, "expert_out": expert_out, "expert_ids": expert_ids, "capacity": capacity, "new_mask": new_mask, "cotangent": cotangent}


@jax.custom_vjp
def low(v):
    return lax.optimization_barrier(v.astype(jnp.bfloat16)).astype(jnp.float32)

@jax.custom_vjp
def low_back(v):
    return v

def low_keep(v):
    return (low(v), None)

def low_pass(kept, grad):
    return (grad,)

def back_keep(v):
    return (v, None)

def back_low(kept, grad):
    return (low(grad),)
low.defvjp(low_keep, low_pass)
low_back.defvjp(back_keep, back_low)
NORM_EPSILON = 1e-05
HIGHEST_PRECISION = lax.Precision.HIGHEST
MASKED_SCORE = -1e+30

def layer_norm(values, gain_vector, shift_vector):
    center = lax.optimization_barrier(jnp.mean(values, axis=-1, keepdims=True))
    centered = values - center
    spread = lax.optimization_barrier(jnp.mean(centered * centered, axis=-1, keepdims=True))
    return centered * lax.rsqrt(spread + NORM_EPSILON) * gain_vector + shift_vector

def routing(expert_ids, capacity):
    blocks = TOKENS // TOK_DEV
    picks_flat = expert_ids.reshape(blocks, 2 * TOK_DEV).astype(jnp.int32)
    expert_range = jnp.arange(EXPERTS, dtype=jnp.int32)
    one_hot = (picks_flat[:, :, None] == expert_range[None, None, :]).astype(jnp.int32)
    earlier = (jnp.cumsum(one_hot, axis=1) - one_hot).astype(jnp.int32)
    position = lax.optimization_barrier(jnp.sum(earlier * one_hot, axis=2)).astype(jnp.int32)
    limit_of = lax.optimization_barrier(jnp.sum(one_hot * capacity[None, None, :], axis=2)).astype(jnp.int32)
    block_index = jnp.arange(blocks, dtype=jnp.int32)[:, None]
    slot_index = ((picks_flat * blocks + block_index) * CAP + position).astype(jnp.int32)
    dump_slot = EXPERTS * blocks * CAP
    slot_index = jnp.where(position < limit_of, slot_index, dump_slot).astype(jnp.int32)
    token_index = (block_index * TOK_DEV + jnp.arange(2 * TOK_DEV, dtype=jnp.int32)[None, :] // 2).astype(jnp.int32)
    owners = jnp.full((dump_slot + 1,), TOKENS, jnp.int32).at[slot_index.reshape(-1)].set(token_index.reshape(-1))
    return (slot_index.reshape(TOKENS, 2), owners[:dump_slot].reshape(EXPERTS, blocks * CAP))

def attend_sequence(packed):
    queries, key_rows, value_rows = packed
    scores = low_back(jnp.einsum('qhd,khd->hqk', queries, key_rows, precision=HIGHEST_PRECISION))
    causal = jnp.arange(LENGTH)[:, None] >= jnp.arange(LENGTH)[None, :]
    scores = jnp.where(causal[None], scores, MASKED_SCORE)
    row_top = lax.optimization_barrier(jnp.max(scores, axis=-1, keepdims=True))
    weights = jnp.exp(scores - row_top)
    attn_probs = low(weights / lax.optimization_barrier(jnp.sum(weights, axis=-1, keepdims=True)))
    return jnp.einsum('hqk,khd->qhd', attn_probs, value_rows, precision=HIGHEST_PRECISION)

def reference(activations, first_gain, first_shift, query_weight, key_weight, value_weight, output_weight, second_gain, second_shift, router_weight, expert_in, expert_out, expert_ids, capacity, new_mask, cotangent):
    slot_index, owners = routing(expert_ids, capacity)
    seq_count = TOKENS // LENGTH
    shape_seq = (seq_count, LENGTH, H, HD)

    def forward(act_in, gain_one, shift_one, query_w, key_w, value_w, output_w, gain_two, shift_two, router_w, inner_w, outer_w):
        normed_first = low(layer_norm(act_in, gain_one, shift_one))
        queries = low(low_back(jnp.dot(normed_first, query_w, precision=HIGHEST_PRECISION) * HD ** (-0.5)))
        key_rows = low(low_back(jnp.dot(normed_first, key_w, precision=HIGHEST_PRECISION)))
        value_rows = low(low_back(jnp.dot(normed_first, value_w, precision=HIGHEST_PRECISION)))
        attended = lax.map(jax.checkpoint(attend_sequence), (queries.reshape(shape_seq), key_rows.reshape(shape_seq), value_rows.reshape(shape_seq)))
        mixed = low(low_back(attended.reshape(TOKENS, H * HD)))
        branch = low_back(jnp.dot(mixed, output_w, precision=HIGHEST_PRECISION))
        residual = act_in + branch
        normed_second = low(layer_norm(residual, gain_two, shift_two))
        logits = low_back(jnp.dot(normed_second, router_w, precision=HIGHEST_PRECISION))
        pair_logits = jnp.take_along_axis(logits, expert_ids, axis=1)
        pair_top = lax.optimization_barrier(jnp.max(pair_logits, axis=1, keepdims=True))
        pair_exp = jnp.exp(pair_logits - pair_top)
        gate_values = pair_exp / lax.optimization_barrier(jnp.sum(pair_exp, axis=1, keepdims=True))
        padded = jnp.concatenate([normed_second, jnp.zeros((1, D), jnp.float32)], axis=0)

        def expert_pass(packed):
            owner_rows, inner_one, outer_one = packed
            inputs_e = low_back(padded[owner_rows])
            before_act = low_back(jnp.dot(inputs_e, inner_one, precision=HIGHEST_PRECISION))
            activated = low(jax.nn.gelu(before_act, approximate=True))
            return low(low_back(jnp.dot(activated, outer_one.T, precision=HIGHEST_PRECISION)))
        expert_rows = lax.map(jax.checkpoint(expert_pass), (owners, inner_w, outer_w))
        flat_rows = jnp.concatenate([expert_rows.reshape(-1, D), jnp.zeros((1, D), jnp.float32)], axis=0)
        picked = flat_rows[slot_index]
        moe_part = lax.optimization_barrier(jnp.sum(gate_values[:, :, None] * picked, axis=1))
        return residual + moe_part
    result, pullback = jax.vjp(forward, activations.astype(jnp.float32), first_gain, first_shift, query_weight.astype(jnp.float32), key_weight.astype(jnp.float32), value_weight.astype(jnp.float32), output_weight.astype(jnp.float32), second_gain, second_shift, router_weight.astype(jnp.float32), expert_in.astype(jnp.float32), expert_out.astype(jnp.float32))
    grads = pullback(cotangent.astype(jnp.float32))
    mask_float = new_mask.astype(jnp.float32)
    return (result.astype(jnp.bfloat16), grads[0], grads[1], grads[2], grads[3], grads[4], grads[5], grads[6], grads[7], grads[8], grads[9] * mask_float[None, :], grads[10] * mask_float[:, None, None], grads[11] * mask_float[:, None, None])
```

```python
import functools

import jax
import jax.numpy as jnp
import numpy as np
from jax import lax
from jax.experimental import pallas as pl
from jax.experimental.pallas import tpu as pltpu
from jax.sharding import PartitionSpec as P

HD = 64
LENGTH = 1024
NORM_EPSILON = 1e-05
MASKED_SCORE = -1e30
QUERY_ROWS = 256
STRIDE = 256
PAYLOAD = 16
MIB = 1 << 20
F32 = jnp.float32
BF16 = jnp.bfloat16
GELU_A = 0.7978845608028654
GELU_B = 0.044715


def dot_nn(left, right):
    return lax.dot_general(left, right, (((1,), (0,)), ((), ())), preferred_element_type=F32)


def dot_nt(left, right):
    return lax.dot_general(left, right, (((1,), (1,)), ((), ())), preferred_element_type=F32)


def dot_tn(left, right):
    return lax.dot_general(left, right, (((0,), (0,)), ((), ())), preferred_element_type=F32)


def iota(shape, axis):
    return lax.broadcasted_iota(jnp.int32, shape, axis)


def call(body, outs, name, ins, flops=0, vmem=40, scratch=(), smem=(), hbm=(), copies=0):
    specs = []
    for index in range(len(ins)):
        if index in smem:
            specs.append(pl.BlockSpec(memory_space=pltpu.SMEM))
        elif index in hbm:
            specs.append(pl.BlockSpec(memory_space=pl.ANY))
        else:
            specs.append(pl.BlockSpec(memory_space=pltpu.VMEM))
    moved = sum(int(np.prod(o.shape)) * o.dtype.itemsize for o in outs)
    moved += sum(int(np.prod(i.shape)) * i.dtype.itemsize for i in ins)
    return pl.pallas_call(
        body,
        out_shape=outs,
        in_specs=specs,
        out_specs=[pl.BlockSpec(memory_space=pltpu.VMEM)] * len(outs),
        scratch_shapes=list(scratch),
        compiler_params=pltpu.CompilerParams(vmem_limit_bytes=vmem * MIB),
        cost_estimate=pl.CostEstimate(flops=int(flops), bytes_accessed=moved, transcendentals=0),
        name=name,
    )(*ins)


def sds(shape, dtype):
    return jax.ShapeDtypeStruct(shape, dtype)


def norm_parts(values):
    center = jnp.mean(values, axis=1, keepdims=True)
    centered = values - center
    rate = lax.rsqrt(jnp.mean(centered * centered, axis=1, keepdims=True) + NORM_EPSILON)
    return centered * rate, rate


def norm_back(normal, rate, gain, grad):
    scaled = grad * gain
    first = jnp.mean(scaled, axis=1, keepdims=True)
    second = jnp.mean(scaled * normal, axis=1, keepdims=True)
    return rate * (scaled - first - normal * second)


def first_norm_body(x_ref, gain_ref, shift_ref, out_ref):
    normal, _ = norm_parts(x_ref[...].astype(F32))
    out_ref[...] = (normal * gain_ref[...] + shift_ref[...]).astype(BF16)


def slot_hits(slot_row, experts, start, count):
    tokens = slot_row.shape[1]
    parts = []
    for e in range(experts):
        codes = iota((count, tokens), 0) + (e * STRIDE + start)
        hit = (slot_row[0:1] == codes) | (slot_row[1:2] == codes)
        parts.append(jnp.where(hit, 1.0, 0.0))
    return jnp.concatenate(parts, axis=0).astype(BF16)


def route_body(experts, slots, ids_ref, ids_row_ref, cap_row_ref, cap_col_ref, grad_ref, col_ref, row_ref, send_ref):
    tokens = ids_ref.shape[0]
    lower = jnp.where(iota((tokens, tokens), 0) > iota((tokens, tokens), 1), 1.0, 0.0).astype(BF16)
    upper = jnp.where(iota((tokens, tokens), 0) < iota((tokens, tokens), 1), 1.0, 0.0).astype(BF16)
    lanes = iota((tokens, experts), 1)
    hot = [jnp.where(ids_ref[:, k : k + 1] == lanes, 1.0, 0.0) for k in range(2)]
    earlier = dot_nn(lower, (hot[0] + hot[1]).astype(BF16))
    limit = cap_row_ref[...].astype(F32)
    columns = []
    for k in range(2):
        place = jnp.sum(hot[k] * earlier, axis=1, keepdims=True)
        top = jnp.sum(hot[k] * limit, axis=1, keepdims=True)
        code = ids_ref[:, k : k + 1] * STRIDE + place.astype(jnp.int32)
        columns.append(jnp.where(place < top, code, -1))
    col_ref[:, 0:1] = columns[0]
    col_ref[:, 1:2] = columns[1]
    rows_e = iota((experts, tokens), 0)
    hot_row = [jnp.where(ids_row_ref[k : k + 1, :] == rows_e, 1.0, 0.0) for k in range(2)]
    earlier_row = dot_nn((hot_row[0] + hot_row[1]).astype(BF16), upper)
    limit_col = cap_col_ref[...].astype(F32)
    rows = []
    for k in range(2):
        place = jnp.sum(hot_row[k] * earlier_row, axis=0, keepdims=True)
        top = jnp.sum(hot_row[k] * limit_col, axis=0, keepdims=True)
        code = ids_row_ref[k : k + 1, :] * STRIDE + place.astype(jnp.int32)
        rows.append(jnp.where(place < top, code, -1))
    slot_row = jnp.concatenate(rows, axis=0)
    row_ref[...] = slot_row
    hits = slot_hits(slot_row, experts, 0, slots)
    sent = dot_nn(hits, grad_ref[...]).astype(BF16)
    send_ref[...] = sent.reshape(send_ref.shape)


def attend_body(half, where_ref, own_ref, other_ref, wq_ref, wk_ref, wv_ref,
                q_ref, k_ref, v_ref, log_ref, mine_ref, theirs_ref, rows, mixed, keys, vals):
    core = where_ref[0]
    mine = pl.multiple_of(core * half, half)
    theirs = pl.multiple_of((1 - core) * half, half)
    rows[pl.ds(mine, half), :] = own_ref[...]
    rows[pl.ds(theirs, half), :] = other_ref[...]
    length, width = q_ref.shape
    for part in range(2):
        block = slice(part * half, (part + 1) * half)
        source = rows[block, :]
        q_ref[block, :] = (dot_nn(source, wq_ref[...]) * HD ** (-0.5)).astype(BF16)
        k_ref[block, :] = dot_nn(source, wk_ref[...]).astype(BF16)
        v_ref[block, :] = dot_nn(source, wv_ref[...]).astype(BF16)
    heads = width // HD
    lane = iota((1, width), 1)
    triangle = iota((QUERY_ROWS, QUERY_ROWS), 0) >= iota((QUERY_ROWS, QUERY_ROWS), 1)
    for h in range(heads):
        keep = (lane >= h * HD) & (lane < (h + 1) * HD)
        keys[...] = jnp.where(keep, k_ref[...], 0)
        vals[...] = jnp.where(keep, v_ref[...], 0)
        for block in range(length // QUERY_ROWS):
            low = block * QUERY_ROWS
            here = slice(low, low + QUERY_ROWS)
            query = q_ref[here, :]
            diag = jnp.where(triangle, dot_nt(query, keys[here, :]), MASKED_SCORE)
            top = jnp.max(diag, axis=1, keepdims=True)
            if block:
                wide = dot_nt(query, keys[0:low, :])
                top = jnp.maximum(top, jnp.max(wide, axis=1, keepdims=True))
            diag = jnp.exp(diag - top)
            total = jnp.sum(diag, axis=1, keepdims=True)
            result = dot_nn(diag.astype(BF16), vals[here, :])
            if block:
                wide = jnp.exp(wide - top)
                total = total + jnp.sum(wide, axis=1, keepdims=True)
                result = result + dot_nn(wide.astype(BF16), vals[0:low, :])
            result = result / total
            log_ref[here, h : h + 1] = top + jnp.log(total)
            if h:
                result = result + mixed[here, :]
            mixed[here, :] = result
    mine_ref[...] = mixed[pl.ds(mine, half), :].astype(BF16)
    theirs_ref[...] = mixed[pl.ds(theirs, half), :].astype(BF16)


def gates_of(logits, ids_ref, lanes):
    hot = [ids_ref[:, k : k + 1] == lanes for k in range(2)]
    pair = [jnp.sum(jnp.where(hot[k], logits, 0.0), axis=1, keepdims=True) for k in range(2)]
    top = jnp.maximum(pair[0], pair[1])
    raised = [jnp.exp(p - top) for p in pair]
    total = raised[0] + raised[1]
    return [r / total for r in raised]


def split_rows(row, lines):
    high = row.astype(BF16).astype(F32)
    low = row - high
    both = jnp.concatenate([high, low], axis=1)
    return jnp.where(iota((lines, both.shape[1]), 0) == 0, both, 0.0).astype(BF16)


def post_body(experts, chunk_sizes, x_ref, m0, m1, m2, m3, w0, w1, w2, w3, gain_ref, shift_ref, router_ref,
              ids_ref, col_ref, row_ref, resid_ref, normed_ref, gates_ref, *send_refs):
    branch = dot_nn(m0[...], w0[...]) + dot_nn(m1[...], w1[...])
    branch = branch + (dot_nn(m2[...], w2[...]) + dot_nn(m3[...], w3[...]))
    residual = x_ref[...].astype(F32) + branch
    resid_ref[...] = residual
    normal, _ = norm_parts(residual)
    normed = (normal * gain_ref[...] + shift_ref[...]).astype(BF16)
    normed_ref[...] = normed
    tokens, width = normed.shape
    slot_row = row_ref[...]
    start = 0
    for size, ref in zip(chunk_sizes[:-1], send_refs[:-1]):
        hits = slot_hits(slot_row, experts, start, size)
        ref[...] = dot_nn(hits, normed).astype(BF16).reshape(ref.shape)
        start += size
    logits = dot_nn(normed, router_ref[...])
    gates = gates_of(logits, ids_ref, iota((tokens, experts), 1))
    gates_ref[:, 0:1] = gates[0]
    gates_ref[:, 1:2] = gates[1]
    size, ref = chunk_sizes[-1], send_refs[-1]
    hits = slot_hits(slot_row, experts, start, size)
    ref[:, 0:size, :] = dot_nn(hits, normed).astype(BF16).reshape(experts, size, width)
    for e in range(experts):
        codes = iota((tokens, STRIDE), 1) + e * STRIDE
        picked = [jnp.where(col_ref[:, k : k + 1] == codes, gates[k], 0.0) for k in range(2)]
        row = jnp.sum(picked[0] + picked[1], axis=0, keepdims=True)
        ref[e, size : size + PAYLOAD, 0 : 2 * STRIDE] = split_rows(row, PAYLOAD)
        ref[e, size : size + PAYLOAD, 2 * STRIDE :] = jnp.zeros((PAYLOAD, width - 2 * STRIDE), BF16)


def gelu_pair(values):
    square = values * values
    inner = values * (GELU_A + (GELU_A * GELU_B) * square)
    tanh = jnp.tanh(inner)
    half = 0.5 * tanh + 0.5
    slope = half + 0.5 * values * (1.0 - tanh * tanh) * (GELU_A + (3.0 * GELU_A * GELU_B) * square)
    return values * half, slope


def expert_body(shards, sources, start, size, last, *refs):
    refs = list(refs)
    x_ref, g_ref = refs.pop(0), refs.pop(0)
    win, wout = refs[:shards], refs[shards : 2 * shards]
    del refs[: 2 * shards]
    carry_ref = refs.pop(0) if last and start else None
    if last:
        hidden_ref, pre_ref, back_ref = refs[:3]
        del refs[:3]
    else:
        hidden_ref, pre_ref, back_ref, carry_out = refs[:4]
        del refs[:4]
    win_v, wout_v, sems = refs
    copies = []
    for r in range(shards):
        pair = (pltpu.make_async_copy(win[r], win_v.at[r], sems.at[2 * r]),
                pltpu.make_async_copy(wout[r], wout_v.at[r], sems.at[2 * r + 1]))
        for copy in pair:
            copy.start()
        copies.append(pair)
    width = x_ref.shape[2]
    rows = sources * size
    x = x_ref[:, 0:size, :].reshape(rows, width)
    g = g_ref[:, start : start + size, :].reshape(rows, width)
    inner = win_v.shape[2]
    step = 256 if inner % 256 == 0 else inner
    score = jnp.zeros((rows, 1), F32)
    total = None
    for r in range(shards):
        for copy in copies[r]:
            copy.wait()
        for f in range(inner // step):
            cols = slice(f * step, (f + 1) * step)
            out = slice(r * inner + f * step, r * inner + (f + 1) * step)
            hid, slope = gelu_pair(dot_nn(x, win_v[r, :, cols]))
            grad = dot_nn(g, wout_v[r, :, cols])
            hid = hid.astype(BF16)
            score = score + jnp.sum(grad * hid.astype(F32), axis=1, keepdims=True)
            hidden_ref[:, out] = hid
            pre_ref[:, out] = (grad * slope).astype(BF16)
        part = dot_nt(pre_ref[:, r * inner : (r + 1) * inner], win_v[r])
        total = part if total is None else total + part
    back = total.astype(BF16).reshape(sources, size, width)
    eye = iota((size, STRIDE), 1) == iota((size, STRIDE), 0) + start
    if last:
        back_ref[:, 0:size, :] = back
    else:
        back_ref[...] = back
    for s in range(sources):
        row = jnp.sum(jnp.where(eye, score[s * size : (s + 1) * size], 0.0), axis=0, keepdims=True)
        if last:
            if carry_ref is not None:
                row = row + carry_ref[s : s + 1, :]
            back_ref[s, size : size + PAYLOAD, 0 : 2 * STRIDE] = split_rows(row, PAYLOAD)
            back_ref[s, size : size + PAYLOAD, 2 * STRIDE :] = jnp.zeros((PAYLOAD, width - 2 * STRIDE), BF16)
        else:
            carry_out[s : s + 1, :] = row


def expert_out_body(shards, sources, sizes, *refs):
    hidden = refs[: len(sizes)]
    wout = refs[len(sizes) : len(sizes) + shards]
    out_ref = refs[-1]
    width, inner = wout[0].shape
    start = 0
    for ref, size in zip(hidden, sizes):
        total = None
        for r in range(shards):
            part = dot_nt(ref[:, r * inner : (r + 1) * inner], wout[r][...])
            total = part if total is None else total + part
        out_ref[:, start : start + size, :] = total.astype(BF16).reshape(sources, size, width)
        start += size


def expert_grad_body(shards, sources, sizes, *refs):
    count = len(sizes)
    x_refs, g_ref = refs[:count], refs[count]
    hidden, pre = refs[count + 1 : 2 * count + 1], refs[2 * count + 1 : 3 * count + 1]
    keep_ref, send_ref = refs[3 * count + 1], refs[3 * count + 2]
    xt, gt = refs[3 * count + 3 :]
    width = g_ref.shape[2]
    last = x_refs[-1]
    start, base = 0, 0
    for ref, size in zip(x_refs, sizes):
        rows = sources * size
        eye = iota((size, STRIDE), 1) == iota((size, STRIDE), 0) + start
        gate = []
        for s in range(sources):
            row = last[s, sizes[-1] : sizes[-1] + PAYLOAD, :].astype(F32)
            row = row[0:1, 0:STRIDE] + row[0:1, STRIDE : 2 * STRIDE]
            gate.append(jnp.sum(jnp.where(eye, row, 0.0), axis=1, keepdims=True))
        gate = jnp.concatenate(gate, axis=0)
        x = ref[:, 0:size, :].reshape(rows, width).astype(F32) * gate
        g = g_ref[:, start : start + size, :].reshape(rows, width).astype(F32) * gate
        xt[:, base : base + rows] = x.T.astype(BF16)
        gt[:, base : base + rows] = g.T.astype(BF16)
        start += size
        base += rows
    inner = hidden[0].shape[1] // shards
    for r in range(shards):
        cols = slice(r * inner, (r + 1) * inner)
        base = 0
        for index, size in enumerate(sizes):
            rows = sources * size
            one = dot_nn(xt[:, base : base + rows], pre[index][:, cols])
            two = dot_nn(gt[:, base : base + rows], hidden[index][:, cols])
            inward = one if index == 0 else inward + one
            outward = two if index == 0 else outward + two
            base += rows
        send_ref[r, 0] = inward.astype(BF16)
        send_ref[r, 1] = outward.astype(BF16)


def gather_body(rows_ref, codes_ref, col_ref, gates_ref, sum_ref):
    sources, size, width = rows_ref.shape
    codes = codes_ref[...]
    pick = jnp.where(col_ref[:, 0:1] == codes, gates_ref[:, 0:1], 0.0)
    pick = jnp.where(col_ref[:, 1:2] == codes, gates_ref[:, 1:2], pick).astype(BF16)
    sum_ref[...] = dot_nn(pick, rows_ref[...].reshape(sources * size, width))


def second_back_body(experts, size, has_sum, *refs):
    refs = list(refs)
    (rows_ref, codes_ref, col_ref, gates_ref, ids_ref, resid_ref, normed_ref, cot_ref, gain_ref, router_ref,
     w0, w1, w2, w3) = refs[:14]
    del refs[:14]
    sum_ref = refs.pop(0) if has_sum else None
    grad_ref, branch_ref, own_ref, send_ref, small_ref = refs
    sources, _, width = rows_ref.shape
    tokens = resid_ref.shape[0]
    codes = codes_ref[...]
    gates = [gates_ref[:, k : k + 1] for k in range(2)]
    slot = [col_ref[:, k : k + 1] for k in range(2)]
    pick = jnp.where(slot[0] == codes, gates[0], 0.0)
    pick = jnp.where(slot[1] == codes, gates[1], pick).astype(BF16)
    total = dot_nn(pick, rows_ref[:, 0:size, :].reshape(sources * size, width))
    if sum_ref is not None:
        total = total + sum_ref[...]
    scores = [jnp.zeros((tokens, 1), F32), jnp.zeros((tokens, 1), F32)]
    for e in range(experts):
        line = rows_ref[e, size : size + PAYLOAD, :].astype(F32)
        line = line[0:1, 0:STRIDE] + line[0:1, STRIDE : 2 * STRIDE]
        place = iota((tokens, STRIDE), 1) + e * STRIDE
        for k in range(2):
            scores[k] = scores[k] + jnp.sum(jnp.where(slot[k] == place, line, 0.0), axis=1, keepdims=True)
    inner = gates[0] * scores[0] + gates[1] * scores[1]
    lanes = iota((tokens, experts), 1)
    logit_grad = jnp.zeros((tokens, experts), F32)
    for k in range(2):
        logit_grad = jnp.where(ids_ref[:, k : k + 1] == lanes, gates[k] * (scores[k] - inner), logit_grad)
    logit_grad = logit_grad.astype(BF16)
    total = total + dot_nt(logit_grad, router_ref[...])
    normal, rate = norm_parts(resid_ref[...])
    grad = cot_ref[...].astype(F32) + norm_back(normal, rate, gain_ref[...], total)
    grad_ref[...] = grad
    branch = grad.astype(BF16)
    branch_ref[...] = branch
    own_ref[0] = dot_nt(branch, w0[...]).astype(BF16)
    own_ref[1] = dot_nt(branch, w2[...]).astype(BF16)
    send_ref[0] = dot_nt(branch, w1[...]).astype(BF16)
    send_ref[1] = dot_nt(branch, w3[...]).astype(BF16)
    small_ref[0:1, :] = jnp.sum(total * normal, axis=0, keepdims=True)
    small_ref[1:2, :] = jnp.sum(total, axis=0, keepdims=True)
    small_ref[2 : 2 + experts, :] = dot_tn(logit_grad, normed_ref[...])


def output_grad_body(branch_ref, m0, m1, m2, m3, out_ref):
    transposed = branch_ref[...].astype(F32).T.astype(BF16)
    for r, ref in enumerate((m0, m1, m2, m3)):
        out_ref[r] = dot_nn(transposed, ref[...]).astype(BF16)


def attend_back_body(half, has_sum, where_ref, *refs):
    refs = list(refs)
    q_ref, k_ref, v_ref, log_ref, gown_ref, gother_ref, own_ref, other_ref, wq_ref, wk_ref, wv_ref = refs[:11]
    del refs[:11]
    sums = (refs.pop(0), refs.pop(0)) if has_sum else None
    weight_ref, mine_ref, theirs_ref, rows, grads, keys, vals, dq, dk, dv, joined, pile = refs
    core = where_ref[0]
    mine = pl.multiple_of(core * half, half)
    theirs = pl.multiple_of((1 - core) * half, half)
    rows[pl.ds(mine, half), :] = own_ref[...]
    rows[pl.ds(theirs, half), :] = other_ref[...]
    grads[pl.ds(mine, half), :] = gown_ref[...]
    grads[pl.ds(theirs, half), :] = gother_ref[...]
    length, width = q_ref.shape
    heads = width // HD
    lane = iota((1, width), 1)
    triangle = iota((QUERY_ROWS, QUERY_ROWS), 0) >= iota((QUERY_ROWS, QUERY_ROWS), 1)
    qt = q_ref[...].astype(F32).T.astype(BF16)
    gt = grads[...].astype(F32).T.astype(BF16)
    dk[...] = jnp.zeros(dk.shape, F32)
    dv[...] = jnp.zeros(dv.shape, F32)
    for h in range(heads):
        keep = (lane >= h * HD) & (lane < (h + 1) * HD)
        keys[...] = jnp.where(keep, k_ref[...], 0)
        vals[...] = jnp.where(keep, v_ref[...], 0)
        head = slice(h * HD, (h + 1) * HD)
        for block in range(length // QUERY_ROWS):
            low = block * QUERY_ROWS
            here = slice(low, low + QUERY_ROWS)
            query, grad, log = q_ref[here, :], grads[here, :], log_ref[here, h : h + 1]
            spans = [slice(0, low)] if block else []
            spans.append(here)
            probs, outer = [], []
            inner = None
            for span in spans:
                score = dot_nt(query, keys[span, :])
                if span is here:
                    score = jnp.where(triangle, score, MASKED_SCORE)
                prob = jnp.exp(score - log)
                grad_prob = dot_nt(grad, vals[span, :])
                part = jnp.sum(prob * grad_prob, axis=1, keepdims=True)
                inner = part if inner is None else inner + part
                probs.append(prob)
                outer.append(grad_prob)
            query_grad = None
            for span, prob, grad_prob in zip(spans, probs, outer):
                score_grad = (prob * (grad_prob - inner)).astype(BF16)
                part = dot_nn(score_grad, keys[span, :])
                query_grad = part if query_grad is None else query_grad + part
                dv[head, span] = dv[head, span] + dot_nn(gt[head, here], prob.astype(BF16))
                dk[head, span] = dk[head, span] + dot_nn(qt[head, here], score_grad)
            if h:
                query_grad = query_grad + dq[here, :]
            dq[here, :] = query_grad
    joined[:, 0:width] = (dq[...].astype(BF16).astype(F32) * HD ** (-0.5)).astype(BF16)
    joined[:, width : 2 * width] = dk[...].T.astype(BF16)
    joined[:, 2 * width : 3 * width] = dv[...].T.astype(BF16)
    total = None
    for index, ref in enumerate((wq_ref, wk_ref, wv_ref)):
        part = dot_nt(joined[:, index * width : (index + 1) * width], ref[...])
        total = part if total is None else total + part
    pile[...] = total
    one, two = pile[pl.ds(mine, half), :], pile[pl.ds(theirs, half), :]
    if sums is not None:
        one, two = one + sums[0][...], two + sums[1][...]
    mine_ref[...] = one.astype(mine_ref.dtype)
    theirs_ref[...] = two.astype(theirs_ref.dtype)
    transposed = rows[...].astype(F32).T.astype(BF16)
    weight_ref[...] = dot_nn(transposed, joined[...]).astype(weight_ref.dtype)


def first_back_body(x_ref, gain_ref, mine_ref, other_ref, resid_ref, out_ref, small_ref):
    grad = mine_ref[...] + other_ref[...].astype(F32)
    normal, rate = norm_parts(x_ref[...].astype(F32))
    out_ref[...] = resid_ref[...] + norm_back(normal, rate, gain_ref[...], grad)
    small_ref[0:1, :] = jnp.sum(grad * normal, axis=0, keepdims=True)
    small_ref[1:2, :] = jnp.sum(grad, axis=0, keepdims=True)


def block_out_body(rows_ref, codes_ref, col_ref, gates_ref, resid_ref, out_ref):
    sources, size, width = rows_ref.shape
    codes = codes_ref[...]
    pick = jnp.where(col_ref[:, 0:1] == codes, gates_ref[:, 0:1], 0.0)
    pick = jnp.where(col_ref[:, 1:2] == codes, gates_ref[:, 1:2], pick).astype(BF16)
    moe = dot_nn(pick, rows_ref[...].reshape(sources * size, width))
    out_ref[...] = (resid_ref[...] + moe).astype(BF16)


def swap(value, axis, step):
    size = lax.axis_size(axis)
    return lax.ppermute(value, axis, [(i, i ^ step) for i in range(size)])


def exchange(value):
    return lax.all_to_all(value, "dp", split_axis=0, concat_axis=0, tiled=True)


def after(value, *others):
    return lax.optimization_barrier((value,) + others)[0]


def everywhere(value):
    for axis in ("head", "dp"):
        step = 1
        while step < lax.axis_size(axis):
            value = value + swap(value, axis, step)
            step *= 2
    return value


def codes_of(experts, start, size):
    table = np.arange(experts)[:, None] * STRIDE + start + np.arange(size)[None, :]
    return jnp.asarray(table.reshape(1, -1).astype(np.int32))


def per_device(activations, first_gain, first_shift, query_weight, key_weight, value_weight, output_weight,
               second_gain, second_shift, router_weight, expert_in, expert_out, expert_ids, capacity, new_mask,
               cotangent):
    tokens, width = activations.shape
    local = query_weight.shape[1]
    heads = local // HD
    experts = router_weight.shape[1]
    sources = lax.axis_size("dp")
    slots = 3 * tokens // experts
    sizes = (slots // 32 * 16, slots - slots // 32 * 16) if slots % 16 == 0 and slots >= 32 else (slots,)
    starts = tuple(sum(sizes[:i]) for i in range(len(sizes)))
    length = LENGTH
    half = tokens
    shards = lax.axis_size("head")
    me = lax.axis_index("head")
    where = jnp.stack([me % 2, lax.axis_index("dp")]).astype(jnp.int32)
    gain_one, shift_one = first_gain[None], first_shift[None]
    gain_two, shift_two = second_gain[None], second_shift[None]

    qkv = (query_weight, key_weight, value_weight)
    qkv_far = tuple(swap(w, "head", 2) for w in qkv)
    out_w = {0: output_weight}
    out_w[2] = swap(output_weight, "head", 2)
    out_w[1] = swap(output_weight, "head", 1)

    normed_first = call(first_norm_body, [sds((tokens, width), BF16)], "norm_first",
                        (activations, gain_one, shift_one), flops=tokens * width * 10)[0]
    normed_other = swap(normed_first, "head", 1)

    slot_col, slot_row, grad_send = call(
        functools.partial(route_body, experts, slots),
        [sds((tokens, 2), jnp.int32), sds((2, tokens), jnp.int32), sds((experts, slots, width), BF16)],
        "route", (expert_ids, expert_ids.T, capacity[None], capacity[:, None], cotangent),
        flops=2 * experts * slots * tokens * width)
    grad_rows = exchange(grad_send)

    def attend(weights):
        return call(
            functools.partial(attend_body, half),
            [sds((length, local), BF16)] * 3 + [sds((length, heads), F32)] + [sds((half, local), BF16)] * 2,
            "attend", (where, normed_first, normed_other) + tuple(weights),
            flops=6 * length * width * local + 4 * heads * length * length * local, smem=(0,),
            scratch=[pltpu.VMEM((length, width), BF16), pltpu.VMEM((length, local), F32),
                     pltpu.VMEM((length, local), BF16), pltpu.VMEM((length, local), BF16)])

    near = attend(qkv)
    mixed = {0: near[4], 1: swap(near[5], "head", 1)}
    qkv_far = tuple(after(w, near[4]) for w in qkv_far)
    far = attend(qkv_far)
    mixed[2], mixed[3] = far[4], swap(far[5], "head", 1)

    out_w[3] = swap(out_w[2], "head", 1)
    win, wout = {0: expert_in[0]}, {0: expert_out[0]}
    first_in, first_out, _ = lax.optimization_barrier((win[0], wout[0], qkv_far[2]))
    win[2], wout[2] = swap(first_in, "head", 2), swap(first_out, "head", 2)
    win[1], wout[1] = swap(first_in, "head", 1), swap(first_out, "head", 1)
    win[3], wout[3] = swap(win[2], "head", 1), swap(wout[2], "head", 1)

    chunk_shapes = [sds((experts, size, width), BF16) for size in sizes[:-1]]
    chunk_shapes.append(sds((experts, sizes[-1] + PAYLOAD, width), BF16))
    posted = call(
        functools.partial(post_body, experts, sizes),
        [sds((tokens, width), F32), sds((tokens, width), BF16), sds((tokens, 2), F32)] + chunk_shapes,
        "post_attend",
        (activations, mixed[0], mixed[1], mixed[2], mixed[3], out_w[0], out_w[1], out_w[2], out_w[3],
         gain_two, shift_two, router_weight, expert_ids, slot_col, slot_row),
        flops=2 * tokens * width * (width + experts * slots))
    residual, normed_second, gates = posted[:3]
    rows_in = [exchange(part) for part in posted[3:]]

    inner = win[0].shape[1]
    hidden, pre, back = [], [], []
    carry = None
    for index, size in enumerate(sizes):
        last = index == len(sizes) - 1
        rows = sources * size
        outs = [sds((rows, shards * inner), BF16), sds((rows, shards * inner), BF16),
                sds((sources, size + (PAYLOAD if last else 0), width), BF16)]
        ins = (rows_in[index], grad_rows) + tuple(win[r] for r in range(shards)) + tuple(wout[r] for r in range(shards))
        if last:
            ins = ins + ((carry,) if index else ())
        else:
            outs.append(sds((sources, STRIDE), F32))
        result = call(
            functools.partial(expert_body, shards, sources, starts[index], size, last), outs, "expert", ins,
            flops=6 * rows * width * shards * inner, vmem=56, hbm=tuple(range(2, 2 + 2 * shards)),
            scratch=[pltpu.VMEM((shards, width, inner), BF16), pltpu.VMEM((shards, width, inner), BF16),
                     pltpu.SemaphoreType.DMA((2 * shards,))])
        hidden.append(result[0])
        pre.append(result[1])
        back.append(result[2])
        if not last:
            carry = result[3]
    returned = [exchange(part) for part in back]

    expert_rows = call(
        functools.partial(expert_out_body, shards, sources, sizes), [sds((sources, slots, width), BF16)],
        "expert_rows", tuple(hidden) + tuple(wout[r] for r in range(shards)),
        flops=2 * sources * slots * width * shards * inner, vmem=48)[0]

    keep = jnp.sum(jnp.where(jnp.arange(experts) == lax.axis_index("dp"), new_mask, 0)).astype(F32)
    all_rows = sources * slots
    expert_grads = call(
        functools.partial(expert_grad_body, shards, sources, sizes), [sds((shards, 2, width, inner), BF16)],
        "expert_grads", tuple(rows_in) + (grad_rows,) + tuple(hidden) + tuple(pre) + (slot_row,),
        flops=4 * all_rows * width * shards * inner, vmem=60,
        scratch=[pltpu.VMEM((width, all_rows), BF16), pltpu.VMEM((width, all_rows), BF16)])[0]

    partial_sums = ()
    for index in range(len(sizes) - 1):
        done = call(gather_body, [sds((tokens, width), F32)], "gather_back",
                    (returned[index], codes_of(experts, starts[index], sizes[index]), slot_col, gates),
                    flops=2 * tokens * width * experts * sizes[index])[0]
        partial_sums = (done,)
    small_rows = 16 * ((2 + experts + 15) // 16)
    grad_residual, grad_branch, mixed_grad, mixed_send, small_two = call(
        functools.partial(second_back_body, experts, sizes[-1], bool(partial_sums)),
        [sds((tokens, width), F32), sds((tokens, width), BF16), sds((2, tokens, local), BF16),
         sds((2, tokens, local), BF16), sds((2 + experts, width), F32)],
        "second_back",
        (returned[-1], codes_of(experts, starts[-1], sizes[-1]), slot_col, gates, expert_ids, residual,
         normed_second, cotangent, gain_two, router_weight, out_w[0], out_w[1], out_w[2], out_w[3]) + partial_sums,
        flops=2 * tokens * width * (width + experts * sizes[-1]))
    mixed_got = swap(mixed_send, "head", 1)

    def attend_back(group, parts, weights, sums, weight_type, types):
        return call(
            functools.partial(attend_back_body, half, bool(sums)),
            [sds((width, 3 * local), weight_type), sds((half, width), types[0]), sds((half, width), types[1])],
            "attend_back",
            (where, parts[0], parts[1], parts[2], parts[3], mixed_grad[group], mixed_got[group], normed_first,
             normed_other) + tuple(weights) + tuple(sums),
            flops=12 * length * width * local + 10 * heads * length * length * local, smem=(0,), vmem=48,
            scratch=[pltpu.VMEM((length, width), BF16), pltpu.VMEM((length, local), BF16),
                     pltpu.VMEM((length, local), BF16), pltpu.VMEM((length, local), BF16),
                     pltpu.VMEM((length, local), F32), pltpu.VMEM((local, length), F32),
                     pltpu.VMEM((local, length), F32), pltpu.VMEM((length, 3 * local), BF16),
                     pltpu.VMEM((length, width), F32)])

    far_grad, far_mine, far_theirs = attend_back(1, far, qkv_far, (), BF16, (F32, F32))
    far_got = swap(far_grad, "head", 2)
    near_grad, near_mine, near_theirs = attend_back(0, near, qkv, (far_mine, far_theirs), F32, (F32, BF16))
    first_got = swap(near_theirs, "head", 1)
    grad_input, small_one = call(
        first_back_body, [sds((tokens, width), F32), sds((2, width), F32)], "first_back",
        (activations, gain_one, near_mine, first_got, grad_residual), flops=tokens * width * 20)

    rows_back = exchange(after(expert_rows, returned[-1]))
    block_out = call(
        block_out_body, [sds((tokens, width), BF16)], "block_out",
        (rows_back, codes_of(experts, 0, slots), slot_col, gates, residual),
        flops=2 * tokens * width * experts * slots)[0]

    grads_got = swap(jnp.stack([expert_grads[1], expert_grads[3]]), "head", 1)
    far_sum = (expert_grads[2].astype(F32) + grads_got[1].astype(F32)).astype(BF16)
    far_sum = swap(far_sum, "head", 2)
    grad_expert = (expert_grads[0].astype(F32) + grads_got[0].astype(F32) + far_sum.astype(F32)) * keep

    out_grads = call(
        output_grad_body, [sds((4, width, local), BF16)], "output_grad",
        (grad_branch, mixed[0], mixed[1], mixed[2], mixed[3]), flops=2 * tokens * width * width)[0]
    out_got = swap(jnp.stack([out_grads[1], out_grads[3]]), "head", 1)
    out_far = swap((out_grads[2].astype(F32) + out_got[1].astype(F32)).astype(BF16), "head", 2)
    out_sum = out_grads[0].astype(F32) + out_got[0].astype(F32) + out_far.astype(F32)

    joined = jnp.concatenate([near_grad + far_got.astype(F32), out_sum], axis=1).astype(BF16)
    scattered = exchange(joined.reshape(sources, width // sources, 4 * local))
    reduced = jnp.sum(scattered.astype(F32), axis=0).astype(BF16)
    gathered = exchange(jnp.broadcast_to(reduced[None], (sources,) + reduced.shape))
    gathered = gathered.reshape(width, 4 * local).astype(F32)

    small = jnp.concatenate([small_one, small_two], axis=0)
    pad = (-small.shape[0]) % 8
    small = everywhere(jnp.pad(small, ((0, pad), (0, 0))))
    mask = new_mask.astype(F32)[None, :]
    return (
        block_out,
        grad_input,
        small[0],
        small[1],
        gathered[:, :local],
        gathered[:, local : 2 * local],
        gathered[:, 2 * local : 3 * local],
        gathered[:, 3 * local :].T,
        small[2],
        small[3],
        small[4 : 4 + experts].T * mask,
        grad_expert[0][None],
        grad_expert[1][None],
    )


def solution(mesh):
    placed = (
        P(("dp", "head"), None),
        P(),
        P(),
        P(None, "head"),
        P(None, "head"),
        P(None, "head"),
        P("head", None),
        P(),
        P(),
        P(),
        P("dp", None, "head"),
        P("dp", None, "head"),
        P(("dp", "head"), None),
        P(),
        P(),
        P(("dp", "head"), None),
    )
    return jax.shard_map(
        per_device,
        mesh=mesh,
        in_specs=placed,
        out_specs=(
            P(("dp", "head"), None),
            P(("dp", "head"), None),
            P(),
            P(),
            P(None, "head"),
            P(None, "head"),
            P(None, "head"),
            P("head", None),
            P(),
            P(),
            P(),
            P("dp", None, "head"),
            P("dp", None, "head"),
        ),
        check_vma=False,
    )
```

```python
import functools

import jax
import jax.numpy as jnp
import numpy as np
from jax import lax
from jax.experimental import pallas as pl
from jax.experimental.pallas import tpu as pltpu
from jax.sharding import PartitionSpec as P

HD = 64
LENGTH = 1024
NORM_EPSILON = 1e-05
MASKED_SCORE = -1e30
QUERY_ROWS = 256
STRIDE = 256
PAYLOAD = 16
MIB = 1 << 20
F32 = jnp.float32
BF16 = jnp.bfloat16
GELU_A = 0.7978845608028654
GELU_B = 0.044715


def dot_nn(left, right):
    return lax.dot_general(left, right, (((1,), (0,)), ((), ())), preferred_element_type=F32)


def dot_nt(left, right):
    return lax.dot_general(left, right, (((1,), (1,)), ((), ())), preferred_element_type=F32)


def dot_tn(left, right):
    return lax.dot_general(left, right, (((0,), (0,)), ((), ())), preferred_element_type=F32)


def iota(shape, axis):
    return lax.broadcasted_iota(jnp.int32, shape, axis)


def call(body, outs, name, ins, vmem=24, scratch=(), smem=(), hbm=(), free=(), near=(), out_hbm=()):
    specs, given = [], []
    for index, value in enumerate(ins):
        if index in smem:
            specs.append(pl.BlockSpec(memory_space=pltpu.SMEM))
        elif index in hbm:
            specs.append(pl.BlockSpec(memory_space=pltpu.HBM))
        else:
            specs.append(pl.BlockSpec())
        if index not in smem and index not in near and value.size * value.dtype.itemsize >= 1 << 16:
            value = pltpu.with_memory_space_constraint(value, pltpu.HBM)
        given.append(value)
    return pl.pallas_call(
        body,
        out_shape=[o if i in free else pltpu.HBM(o.shape, o.dtype) for i, o in enumerate(outs)],
        in_specs=specs,
        out_specs=[pl.BlockSpec(memory_space=pltpu.HBM) if i in out_hbm else pl.BlockSpec() for i in range(len(outs))],
        scratch_shapes=list(scratch),
        compiler_params=pltpu.CompilerParams(vmem_limit_bytes=vmem * MIB),
        cost_estimate=pl.CostEstimate(flops=1, bytes_accessed=1, transcendentals=0),
        name=name,
    )(*given)


def sds(shape, dtype):
    return jax.ShapeDtypeStruct(shape, dtype)


def norm_parts(values):
    center = jnp.mean(values, axis=1, keepdims=True)
    centered = values - center
    rate = lax.rsqrt(jnp.mean(centered * centered, axis=1, keepdims=True) + NORM_EPSILON)
    return centered * rate, rate


def norm_back(normal, rate, gain, grad):
    scaled = grad * gain
    first = jnp.mean(scaled, axis=1, keepdims=True)
    second = jnp.mean(scaled * normal, axis=1, keepdims=True)
    return rate * (scaled - first - normal * second)


def first_norm_body(x_ref, gain_ref, shift_ref, out_ref):
    normal, _ = norm_parts(x_ref[...].astype(F32))
    out_ref[...] = (normal * gain_ref[...] + shift_ref[...]).astype(BF16)


def slot_hits(slot_row, experts, start, count):
    tokens = slot_row.shape[1]
    parts = []
    for e in range(experts):
        codes = iota((count, tokens), 0) + (e * STRIDE + start)
        hit = (slot_row[0:1] == codes) | (slot_row[1:2] == codes)
        parts.append(jnp.where(hit, 1.0, 0.0))
    return jnp.concatenate(parts, axis=0).astype(BF16)


def slots_of(ids, cap_col):
    tokens = ids.shape[1]
    experts = cap_col.shape[0]
    upper = jnp.where(iota((tokens, tokens), 0) < iota((tokens, tokens), 1), 1.0, 0.0).astype(BF16)
    rows_e = iota((experts, tokens), 0)
    hot = [jnp.where(ids[k : k + 1] == rows_e, 1.0, 0.0) for k in range(2)]
    earlier = dot_nn((hot[0] + hot[1]).astype(BF16), upper)
    limit = cap_col.astype(F32)
    rows = []
    for k in range(2):
        place = jnp.sum(hot[k] * earlier, axis=0, keepdims=True)
        top = jnp.sum(hot[k] * limit, axis=0, keepdims=True)
        rows.append(jnp.where(place < top, ids[k : k + 1] * STRIDE + place.astype(jnp.int32), -1))
    return jnp.concatenate(rows, axis=0)


def block_hits(slot_row, block, count):
    codes = iota((count, slot_row.shape[1]), 0) + block * STRIDE
    return jnp.where((slot_row[0:1] == codes) | (slot_row[1:2] == codes), 1.0, 0.0).astype(BF16)


def sort_rows(slots, here, slot_row, rows, send_refs):
    hits = [block_hits(slot_row, here ^ j, slots) for j in range(len(send_refs))]
    sent = dot_nn(jnp.concatenate(hits, axis=0), rows).astype(BF16)
    for j, ref in enumerate(send_refs):
        ref[...] = sent[j * slots : (j + 1) * slots]


def route_body(slots, where_ref, ids_row_ref, cap_col_ref, grad_ref, ids_ref, col_ref, row_ref, *send_refs):
    ids = ids_row_ref[...]
    slot_row = slots_of(ids, cap_col_ref[...])
    row_ref[...] = slot_row
    col_ref[...] = slot_row.astype(F32).T.astype(jnp.int32)
    ids_ref[...] = ids.astype(F32).T.astype(jnp.int32)
    sort_rows(slots, where_ref[1], slot_row, grad_ref[...], send_refs)


def mirror_body(slots, where_ref, cap_col_ref, grad_ref, *send_refs):
    tokens = grad_ref.shape[0] - PAYLOAD
    ids = grad_ref[tokens:, 0:tokens].astype(F32)[0:2].astype(jnp.int32)
    sort_rows(slots, where_ref[1], slots_of(ids, cap_col_ref[...]), grad_ref[0:tokens, :], send_refs)


def attend_body(half, where_ref, own_ref, other_ref, w_ref,
                q_ref, k_ref, v_ref, log_ref, mine_ref, theirs_ref, rows, mixed, keys, vals):
    core = where_ref[0]
    mine = pl.multiple_of(core * half, half)
    theirs = pl.multiple_of((1 - core) * half, half)
    rows[pl.ds(mine, half), :] = own_ref[...]
    rows[pl.ds(theirs, half), :] = other_ref[...]
    length, width = q_ref.shape
    for part in range(2):
        block = slice(part * half, (part + 1) * half)
        source = rows[block, :]
        q_ref[block, :] = (dot_nt(source, w_ref[0:width, :]) * HD ** (-0.5)).astype(BF16)
        k_ref[block, :] = dot_nt(source, w_ref[width : 2 * width, :]).astype(BF16)
        v_ref[block, :] = dot_nt(source, w_ref[2 * width :, :]).astype(BF16)
    heads = width // HD
    lane = iota((1, width), 1)
    triangle = iota((QUERY_ROWS, QUERY_ROWS), 0) >= iota((QUERY_ROWS, QUERY_ROWS), 1)
    for h in range(heads):
        keep = (lane >= h * HD) & (lane < (h + 1) * HD)
        keys[...] = jnp.where(keep, k_ref[...], 0)
        vals[...] = jnp.where(keep, v_ref[...], 0)
        for block in range(length // QUERY_ROWS):
            low = block * QUERY_ROWS
            here = slice(low, low + QUERY_ROWS)
            query = q_ref[here, :]
            diag = jnp.where(triangle, dot_nt(query, keys[here, :]), MASKED_SCORE)
            top = jnp.max(diag, axis=1, keepdims=True)
            if block:
                wide = dot_nt(query, keys[0:low, :])
                top = jnp.maximum(top, jnp.max(wide, axis=1, keepdims=True))
            diag = jnp.exp(diag - top)
            total = jnp.sum(diag, axis=1, keepdims=True)
            result = dot_nn(diag.astype(BF16), vals[here, :])
            if block:
                wide = jnp.exp(wide - top)
                total = total + jnp.sum(wide, axis=1, keepdims=True)
                result = result + dot_nn(wide.astype(BF16), vals[0:low, :])
            result = result / total
            log_ref[here, h : h + 1] = top + jnp.log(total)
            if h:
                result = result + mixed[here, :]
            mixed[here, :] = result
    mine_ref[...] = mixed[pl.ds(mine, half), :].astype(BF16)
    theirs_ref[...] = mixed[pl.ds(theirs, half), :].astype(BF16)


def gates_of(logits, ids_ref, lanes):
    hot = [ids_ref[:, k : k + 1] == lanes for k in range(2)]
    pair = [jnp.sum(jnp.where(hot[k], logits, 0.0), axis=1, keepdims=True) for k in range(2)]
    top = jnp.maximum(pair[0], pair[1])
    raised = [jnp.exp(p - top) for p in pair]
    total = raised[0] + raised[1]
    return [r / total for r in raised]


def split_rows(row, lines):
    high = row.astype(BF16).astype(F32)
    low = row - high
    both = jnp.concatenate([high, low], axis=1)
    return jnp.where(iota((lines, both.shape[1]), 0) == 0, both, 0.0).astype(BF16)


def post_body(experts, chunk_sizes, x_ref, m0, m1, m2, m3, w0, w1, w2, w3, gain_ref, shift_ref, router_ref,
              ids_ref, col_ref, row_ref, resid_ref, normed_ref, gates_ref, *send_refs):
    branch = dot_nn(m0[...], w0[...]) + dot_nn(m1[...], w1[...])
    branch = branch + (dot_nn(m2[...], w2[...]) + dot_nn(m3[...], w3[...]))
    residual = x_ref[...].astype(F32) + branch
    resid_ref[...] = residual
    normal, _ = norm_parts(residual)
    normed = (normal * gain_ref[...] + shift_ref[...]).astype(BF16)
    normed_ref[...] = normed
    tokens, width = normed.shape
    slot_row = row_ref[...]
    start = 0
    for size, ref in zip(chunk_sizes[:-1], send_refs[:-1]):
        hits = slot_hits(slot_row, experts, start, size)
        ref[...] = dot_nn(hits, normed).astype(BF16).reshape(ref.shape)
        start += size
    logits = dot_nt(normed, router_ref[...])
    gates = gates_of(logits, ids_ref, iota((tokens, experts), 1))
    gates_ref[:, 0:1] = gates[0]
    gates_ref[:, 1:2] = gates[1]
    size, ref = chunk_sizes[-1], send_refs[-1]
    hits = slot_hits(slot_row, experts, start, size)
    ref[:, 0:size, :] = dot_nn(hits, normed).astype(BF16).reshape(experts, size, width)
    for e in range(experts):
        codes = iota((tokens, STRIDE), 1) + e * STRIDE
        picked = [jnp.where(col_ref[:, k : k + 1] == codes, gates[k], 0.0) for k in range(2)]
        row = jnp.sum(picked[0] + picked[1], axis=0, keepdims=True)
        ref[e, size : size + PAYLOAD, 0 : 2 * STRIDE] = split_rows(row, PAYLOAD)
        ref[e, size : size + PAYLOAD, 2 * STRIDE :] = jnp.zeros((PAYLOAD, width - 2 * STRIDE), BF16)


def gelu_pair(values):
    square = values * values
    inner = values * (GELU_A + (GELU_A * GELU_B) * square)
    tanh = jnp.tanh(inner)
    half = 0.5 * tanh + 0.5
    slope = half + 0.5 * values * (1.0 - tanh * tanh) * (GELU_A + (3.0 * GELU_A * GELU_B) * square)
    return values * half, slope


def expert_body(shards, sources, start, size, last, where_ref, x_ref, *refs):
    refs = list(refs)
    side = sources // 2

    def take(count):
        taken = refs[:count]
        del refs[:count]
        return taken

    g_own, g_mirror, weights = take(side), take(side), take(shards)
    carry_ref, prior_ref = take(2) if last and start else (None, None)
    hidden_ref, pre_ref, g_ref, back_ref, rows_ref = take(5)
    carry_out = None if last else take(1)[0]
    win_v, wout_v, hid_v, pre_v, in_sems, out_sems = refs
    copies = []
    for r in range(shards):
        pair = (pltpu.make_async_copy(weights[r].at[0], win_v.at[r], in_sems.at[2 * r]),
                pltpu.make_async_copy(weights[r].at[1], wout_v.at[r], in_sems.at[2 * r + 1]))
        for copy in pair:
            copy.start()
        copies.append(pair)
    width = x_ref.shape[2]
    rows = sources * size
    x = x_ref[:, 0:size, :].reshape(rows, width)
    here = where_ref[1]
    for j in range(side):
        g_ref[here ^ j] = g_own[j][start : start + size, :]
        g_ref[(here ^ j) ^ side] = g_mirror[j][start : start + size, :]
    g = g_ref[...].reshape(rows, width)
    inner = win_v.shape[2]
    step = 256 if inner % 256 == 0 else inner
    score = jnp.zeros((rows, 1), F32)
    total, result = None, None
    outgoing = []
    for r in range(shards):
        for copy in copies[r]:
            copy.wait()
        for f in range(inner // step):
            cols = slice(f * step, (f + 1) * step)
            hid, slope = gelu_pair(dot_nn(x, win_v[r, :, cols]))
            grad = dot_nn(g, wout_v[r, :, cols])
            hid = hid.astype(BF16)
            score = score + jnp.sum(grad * hid.astype(F32), axis=1, keepdims=True)
            hid_v[r, :, cols] = hid
            pre_v[r, :, cols] = (grad * slope).astype(BF16)
        for source, target in ((hid_v, hidden_ref), (pre_v, pre_ref)):
            copy = pltpu.make_async_copy(source.at[r], target.at[r], out_sems.at[len(outgoing)])
            copy.start()
            outgoing.append(copy)
        part, out = dot_nt(pre_v[r], win_v[r]), dot_nt(hid_v[r], wout_v[r])
        total = part if total is None else total + part
        result = out if result is None else result + out
    back = total.astype(BF16).reshape(sources, size, width)
    result = result.astype(BF16).reshape(sources, size, width)
    eye = iota((size, STRIDE), 1) == iota((size, STRIDE), 0) + start
    if last:
        back_ref[:, 0:size, :] = back
        rows_ref[:, start:, :] = result
        if prior_ref is not None:
            rows_ref[:, 0:start, :] = prior_ref[...]
    else:
        back_ref[...] = back
        rows_ref[...] = result
    for s in range(sources):
        row = jnp.sum(jnp.where(eye, score[s * size : (s + 1) * size], 0.0), axis=0, keepdims=True)
        if last:
            if carry_ref is not None:
                row = row + carry_ref[s : s + 1, :]
            back_ref[s, size : size + PAYLOAD, 0 : 2 * STRIDE] = split_rows(row, PAYLOAD)
            back_ref[s, size : size + PAYLOAD, 2 * STRIDE :] = jnp.zeros((PAYLOAD, width - 2 * STRIDE), BF16)
        else:
            carry_out[s : s + 1, :] = row
    for copy in outgoing:
        copy.wait()


def expert_grad_body(shards, sources, sizes, *refs):
    count = len(sizes)
    x_refs, g_refs = refs[:count], refs[count : 2 * count]
    hidden, pre = refs[2 * count : 3 * count], refs[3 * count : 4 * count]
    home_ref, far_ref, send_ref, xt, gt, hid_v, pre_v, out_v, in_sems, out_sems = refs[4 * count :]
    copies = []
    for r in range(shards):
        base = 0
        group = []
        for index, size in enumerate(sizes):
            rows = sources * size
            for place, (source, target) in enumerate(((pre[index], pre_v), (hidden[index], hid_v))):
                copy = pltpu.make_async_copy(source.at[r], target.at[r, pl.ds(base, rows)],
                                             in_sems.at[(r * count + index) * 2 + place])
                copy.start()
                group.append(copy)
            base += rows
        copies.append(group)
    width = x_refs[0].shape[2]
    last = x_refs[-1]
    start, base = 0, 0
    for ref, g_ref, size in zip(x_refs, g_refs, sizes):
        rows = sources * size
        eye = iota((size, STRIDE), 1) == iota((size, STRIDE), 0) + start
        gate = []
        for s in range(sources):
            row = last[s, sizes[-1] : sizes[-1] + PAYLOAD, :].astype(F32)
            row = row[0:1, 0:STRIDE] + row[0:1, STRIDE : 2 * STRIDE]
            gate.append(jnp.sum(jnp.where(eye, row, 0.0), axis=1, keepdims=True))
        gate = jnp.concatenate(gate, axis=0)
        x = ref[:, 0:size, :].reshape(rows, width).astype(F32) * gate
        g = g_ref[...].reshape(rows, width).astype(F32) * gate
        xt[:, base : base + rows] = x.T.astype(BF16)
        gt[:, base : base + rows] = g.T.astype(BF16)
        start += size
        base += rows
    outgoing = []
    for r in range(shards):
        for copy in copies[r]:
            copy.wait()
        out_v[r, 0] = dot_nn(xt[...], pre_v[r]).astype(BF16)
        out_v[r, 1] = dot_nn(gt[...], hid_v[r]).astype(BF16)
        target = send_ref.at[r // 2] if r % 2 else (far_ref if r else home_ref)
        copy = pltpu.make_async_copy(out_v.at[r], target, out_sems.at[r])
        copy.start()
        outgoing.append(copy)
    for copy in outgoing:
        copy.wait()


def gather_body(rows_ref, codes_ref, col_ref, gates_ref, sum_ref):
    sources, size, width = rows_ref.shape
    codes = codes_ref[...]
    pick = jnp.where(col_ref[:, 0:1] == codes, gates_ref[:, 0:1], 0.0)
    pick = jnp.where(col_ref[:, 1:2] == codes, gates_ref[:, 1:2], pick).astype(BF16)
    sum_ref[...] = dot_nn(pick, rows_ref[...].reshape(sources * size, width))


def second_back_body(experts, size, has_sum, *refs):
    refs = list(refs)
    (rows_ref, codes_ref, col_ref, gates_ref, ids_ref, resid_ref, normed_ref, cot_ref, gain_ref, router_ref,
     w0, w1, w2, w3) = refs[:14]
    del refs[:14]
    sum_ref = refs.pop(0) if has_sum else None
    grad_ref, branch_ref, own_ref, send_ref, small_ref = refs
    sources, _, width = rows_ref.shape
    tokens = resid_ref.shape[0]
    codes = codes_ref[...]
    gates = [gates_ref[:, k : k + 1] for k in range(2)]
    slot = [col_ref[:, k : k + 1] for k in range(2)]
    pick = jnp.where(slot[0] == codes, gates[0], 0.0)
    pick = jnp.where(slot[1] == codes, gates[1], pick).astype(BF16)
    total = dot_nn(pick, rows_ref[:, 0:size, :].reshape(sources * size, width))
    if sum_ref is not None:
        total = total + sum_ref[...]
    scores = [jnp.zeros((tokens, 1), F32), jnp.zeros((tokens, 1), F32)]
    for e in range(experts):
        line = rows_ref[e, size : size + PAYLOAD, :].astype(F32)
        line = line[0:1, 0:STRIDE] + line[0:1, STRIDE : 2 * STRIDE]
        place = iota((tokens, STRIDE), 1) + e * STRIDE
        for k in range(2):
            scores[k] = scores[k] + jnp.sum(jnp.where(slot[k] == place, line, 0.0), axis=1, keepdims=True)
    inner = gates[0] * scores[0] + gates[1] * scores[1]
    lanes = iota((tokens, experts), 1)
    logit_grad = jnp.zeros((tokens, experts), F32)
    for k in range(2):
        logit_grad = jnp.where(ids_ref[:, k : k + 1] == lanes, gates[k] * (scores[k] - inner), logit_grad)
    logit_grad = logit_grad.astype(BF16)
    total = total + dot_nn(logit_grad, router_ref[...])
    normal, rate = norm_parts(resid_ref[...])
    grad = cot_ref[...].astype(F32) + norm_back(normal, rate, gain_ref[...], total)
    grad_ref[...] = grad
    branch = grad.astype(BF16)
    branch_ref[...] = branch
    own_ref[0] = dot_nt(branch, w0[...]).astype(BF16)
    own_ref[1] = dot_nt(branch, w2[...]).astype(BF16)
    send_ref[0] = dot_nt(branch, w1[...]).astype(BF16)
    send_ref[1] = dot_nt(branch, w3[...]).astype(BF16)
    small_ref[0:1, :] = jnp.sum(total * normal, axis=0, keepdims=True)
    small_ref[1:2, :] = jnp.sum(total, axis=0, keepdims=True)
    small_ref[2 : 2 + experts, :] = dot_tn(logit_grad, normed_ref[...])


def output_grad_body(branch_ref, m0, m1, m2, m3, home_ref, send_ref):
    for ref, out in ((m0, home_ref.at[0]), (m2, home_ref.at[1]), (m1, send_ref.at[0]), (m3, send_ref.at[1])):
        out[...] = dot_nn(ref[...].astype(F32).T.astype(BF16), branch_ref[...]).astype(BF16)


def attend_back_body(half, has_sum, where_ref, *refs):
    refs = list(refs)
    q_ref, k_ref, v_ref, log_ref, gown_ref, gother_ref, own_ref, other_ref, w_ref = refs[:9]
    del refs[:9]
    sums = (refs.pop(0), refs.pop(0)) if has_sum else None
    weight_ref, mine_ref, theirs_ref, rows, grads, keys, vals, dq, dk, dv, joined, pile = refs
    core = where_ref[0]
    mine = pl.multiple_of(core * half, half)
    theirs = pl.multiple_of((1 - core) * half, half)
    rows[pl.ds(mine, half), :] = own_ref[...]
    rows[pl.ds(theirs, half), :] = other_ref[...]
    grads[pl.ds(mine, half), :] = gown_ref[...]
    grads[pl.ds(theirs, half), :] = gother_ref[...]
    length, width = q_ref.shape
    heads = width // HD
    lane = iota((1, width), 1)
    triangle = iota((QUERY_ROWS, QUERY_ROWS), 0) >= iota((QUERY_ROWS, QUERY_ROWS), 1)
    qt = q_ref[...].astype(F32).T.astype(BF16)
    gt = grads[...].astype(F32).T.astype(BF16)
    dk[...] = jnp.zeros(dk.shape, F32)
    dv[...] = jnp.zeros(dv.shape, F32)
    for h in range(heads):
        keep = (lane >= h * HD) & (lane < (h + 1) * HD)
        keys[...] = jnp.where(keep, k_ref[...], 0)
        vals[...] = jnp.where(keep, v_ref[...], 0)
        head = slice(h * HD, (h + 1) * HD)
        for block in range(length // QUERY_ROWS):
            low = block * QUERY_ROWS
            here = slice(low, low + QUERY_ROWS)
            query, grad, log = q_ref[here, :], grads[here, :], log_ref[here, h : h + 1]
            spans = [slice(0, low)] if block else []
            spans.append(here)
            probs, outer = [], []
            inner = None
            for span in spans:
                score = dot_nt(query, keys[span, :])
                if span is here:
                    score = jnp.where(triangle, score, MASKED_SCORE)
                prob = jnp.exp(score - log)
                grad_prob = dot_nt(grad, vals[span, :])
                part = jnp.sum(prob * grad_prob, axis=1, keepdims=True)
                inner = part if inner is None else inner + part
                probs.append(prob)
                outer.append(grad_prob)
            query_grad = None
            for span, prob, grad_prob in zip(spans, probs, outer):
                score_grad = (prob * (grad_prob - inner)).astype(BF16)
                part = dot_nn(score_grad, keys[span, :])
                query_grad = part if query_grad is None else query_grad + part
                dv[head, span] = dv[head, span] + dot_nn(gt[head, here], prob.astype(BF16))
                dk[head, span] = dk[head, span] + dot_nn(qt[head, here], score_grad)
            if h:
                query_grad = query_grad + dq[here, :]
            dq[here, :] = query_grad
    query_grads = dq[...].astype(BF16).astype(F32) * HD ** (-0.5)
    joined[0:width, :] = query_grads.T.astype(BF16)
    joined[width : 2 * width, :] = dk[...].astype(BF16)
    joined[2 * width : 3 * width, :] = dv[...].astype(BF16)
    total = dot_nn(query_grads.astype(BF16), w_ref[0:width, :])
    total = total + dot_nn(dk[...].T.astype(BF16), w_ref[width : 2 * width, :])
    total = total + dot_nn(dv[...].T.astype(BF16), w_ref[2 * width :, :])
    pile[...] = total
    one, two = pile[pl.ds(mine, half), :], pile[pl.ds(theirs, half), :]
    if sums is not None:
        one, two = one + sums[0][...], two + sums[1][...]
    mine_ref[...] = one.astype(mine_ref.dtype)
    theirs_ref[...] = two.astype(theirs_ref.dtype)
    weight_ref[...] = dot_nn(joined[...], rows[...]).astype(weight_ref.dtype)


def first_back_body(x_ref, gain_ref, mine_ref, other_ref, resid_ref, out_ref, small_ref):
    grad = mine_ref[...] + other_ref[...].astype(F32)
    normal, rate = norm_parts(x_ref[...].astype(F32))
    out_ref[...] = resid_ref[...] + norm_back(normal, rate, gain_ref[...], grad)
    small_ref[0:1, :] = jnp.sum(grad * normal, axis=0, keepdims=True)
    small_ref[1:2, :] = jnp.sum(grad, axis=0, keepdims=True)


def block_out_body(rows_ref, codes_ref, col_ref, gates_ref, resid_ref, out_ref):
    sources, size, width = rows_ref.shape
    codes = codes_ref[...]
    pick = jnp.where(col_ref[:, 0:1] == codes, gates_ref[:, 0:1], 0.0)
    pick = jnp.where(col_ref[:, 1:2] == codes, gates_ref[:, 1:2], pick).astype(BF16)
    moe = dot_nn(pick, rows_ref[...].reshape(sources * size, width))
    out_ref[...] = (resid_ref[...] + moe).astype(BF16)


def final_body(all_ref, *out_refs):
    rows = out_refs[0].shape[0]
    for index, ref in enumerate(out_refs):
        ref[...] = all_ref[index * rows : (index + 1) * rows, :].astype(F32)


def swap(value, axis, step):
    size = lax.axis_size(axis)
    return lax.ppermute(value, axis, [(i, i ^ step) for i in range(size)])


def exchange(value):
    return lax.all_to_all(value, "dp", split_axis=0, concat_axis=0, tiled=True)


def after(value, *others):
    return lax.optimization_barrier((value,) + others)[0]


def codes_of(experts, start, size):
    table = np.arange(experts)[:, None] * STRIDE + start + np.arange(size)[None, :]
    return jnp.asarray(table.reshape(1, -1).astype(np.int32))


def per_device(activations, first_gain, first_shift, query_weight, key_weight, value_weight, output_weight,
               second_gain, second_shift, router_weight, expert_in, expert_out, expert_ids, capacity, new_mask,
               cotangent):
    tokens, width = activations.shape
    local = query_weight.shape[1]
    heads = local // HD
    experts = router_weight.shape[1]
    sources = lax.axis_size("dp")
    slots = 3 * tokens // experts
    sizes = (slots // 32 * 16, slots - slots // 32 * 16) if slots % 16 == 0 and slots >= 32 else (slots,)
    starts = tuple(sum(sizes[:i]) for i in range(len(sizes)))
    length = LENGTH
    half = tokens
    shards = lax.axis_size("head")
    me = lax.axis_index("head")
    where = jnp.stack([me % 2, lax.axis_index("dp")]).astype(jnp.int32)
    gain_one, shift_one = first_gain[None], first_shift[None]
    gain_two, shift_two = second_gain[None], second_shift[None]

    qkv = jnp.concatenate([query_weight.T, key_weight.T, value_weight.T], axis=0)
    far = swap(jnp.concatenate([qkv, output_weight], axis=0), "head", 2)
    router = router_weight.T

    normed_first = call(first_norm_body, [sds((tokens, width), BF16)], "norm_first",
                        (activations, gain_one, shift_one), vmem=16)[0]
    normed_other = swap(normed_first, "head", 1)

    side = sources // 2
    ids_row, cap_col = expert_ids.T, capacity[:, None]
    extra = jnp.pad(ids_row.astype(BF16), ((0, PAYLOAD - 2), (0, width - tokens)))
    mirror_grad = swap(jnp.concatenate([cotangent, extra], axis=0), "dp", side)
    routed = call(
        functools.partial(route_body, slots),
        [sds((tokens, 2), jnp.int32), sds((tokens, 2), jnp.int32), sds((2, tokens), jnp.int32)]
        + [sds((slots, width), BF16)] * side,
        "route", (where, ids_row, cap_col, cotangent), smem=(0,))
    ids_col, slot_col, slot_row = routed[:3]
    grad_own = [routed[3]] + [swap(routed[3 + j], "dp", j) for j in range(1, side)]
    out_w = {0: output_weight, 1: swap(output_weight, "head", 1)}
    weights = {0: jnp.stack([expert_in[0], expert_out[0]])}
    weights[1] = swap(weights[0], "head", 1)

    def attend(weights):
        return call(
            functools.partial(attend_body, half),
            [sds((length, local), BF16)] * 3 + [sds((length, heads), F32)] + [sds((half, local), BF16)] * 2,
            "attend", (where, normed_first, normed_other, weights), smem=(0,),
            scratch=[pltpu.VMEM((length, width), BF16), pltpu.VMEM((length, local), F32),
                     pltpu.VMEM((length, local), BF16), pltpu.VMEM((length, local), BF16)])

    near = attend(qkv)
    mixed = {0: near[4], 1: swap(near[5], "head", 1)}
    far = after(far, near[4], out_w[1], weights[1])
    qkv_far, out_far = far[: 3 * local], far[3 * local :]
    away = attend(qkv_far)
    mixed[2], mixed[3] = away[4], swap(away[5], "head", 1)

    out_w[2], out_w[3] = out_far, swap(out_far, "head", 1)
    weights[2] = swap(after(weights[0], far), "head", 2)
    weights[3] = swap(weights[2], "head", 1)
    mirror_send = call(
        functools.partial(mirror_body, slots), [sds((slots, width), BF16)] * side, "mirror",
        (where, cap_col, mirror_grad), smem=(0,), free=tuple(range(1, side)))
    grad_mirror = [mirror_send[0]] + [swap(mirror_send[j], "dp", j) for j in range(1, side)]

    chunk_shapes = [sds((experts, size, width), BF16) for size in sizes[:-1]]
    chunk_shapes.append(sds((experts, sizes[-1] + PAYLOAD, width), BF16))
    posted = call(
        functools.partial(post_body, experts, sizes),
        [sds((tokens, width), F32), sds((tokens, width), BF16), sds((tokens, 2), F32)] + chunk_shapes,
        "post_attend",
        (activations, mixed[0], mixed[1], mixed[2], mixed[3], out_w[0], out_w[1], out_w[2], out_w[3],
         gain_two, shift_two, router, ids_col, slot_col, slot_row), free=(3, 4, 5))
    residual, normed_second, gates = posted[:3]
    rows_in, done = [], grad_own[0]
    for index, part in enumerate(posted[3:]):
        ready = (mirror_send[0],) + tuple(grad_own[1:]) if index == 0 else (weights[2],) + tuple(grad_mirror[1:])
        done = exchange(after(part, done, *ready))
        rows_in.append(done)

    inner = weights[0].shape[2]
    hidden, pre, grads, back = [], [], [], []
    carry = ()
    for index, size in enumerate(sizes):
        last = index == len(sizes) - 1
        rows = sources * size
        kept = slots if last else size
        outs = [sds((shards, rows, inner), BF16), sds((shards, rows, inner), BF16), sds((sources, size, width), BF16),
                sds((sources, size + (PAYLOAD if last else 0), width), BF16), sds((sources, kept, width), BF16)]
        ins = (where, rows_in[index]) + tuple(grad_own) + tuple(grad_mirror)
        first = len(ins)
        ins = ins + tuple(weights[r] for r in range(shards)) + carry
        if not last:
            outs.append(sds((sources, STRIDE), F32))
        result = call(
            functools.partial(expert_body, shards, sources, starts[index], size, last), outs, "expert", ins,
            vmem=48 if rows <= 768 else 62, smem=(0,), hbm=tuple(range(first, first + shards)), free=(3,),
            out_hbm=(0, 1),
            scratch=[pltpu.VMEM((shards, width, inner), BF16), pltpu.VMEM((shards, width, inner), BF16),
                     pltpu.VMEM((shards, rows, inner), BF16), pltpu.VMEM((shards, rows, inner), BF16),
                     pltpu.SemaphoreType.DMA((2 * shards,)), pltpu.SemaphoreType.DMA((2 * shards,))])
        hidden.append(result[0])
        pre.append(result[1])
        grads.append(result[2])
        back.append(result[3])
        expert_rows = result[4]
        if not last:
            carry = (result[5], result[4])
    returned = []
    for part in back:
        done = exchange(after(part, done))
        returned.append(done)

    keep = jnp.sum(jnp.where(jnp.arange(experts) == lax.axis_index("dp"), new_mask, 0)).astype(F32)
    all_rows = sources * slots
    expert_grads = call(
        functools.partial(expert_grad_body, shards, sources, sizes),
        [sds((2, width, inner), BF16), sds((2, width, inner), BF16), sds((2, 2, width, inner), BF16)],
        "expert_grads", tuple(rows_in) + tuple(grads) + tuple(hidden) + tuple(pre), vmem=56,
        hbm=tuple(range(2 * len(sizes), 4 * len(sizes))), out_hbm=(0, 1, 2),
        scratch=[pltpu.VMEM((width, all_rows), BF16), pltpu.VMEM((width, all_rows), BF16),
                 pltpu.VMEM((shards, all_rows, inner), BF16), pltpu.VMEM((shards, all_rows, inner), BF16),
                 pltpu.VMEM((shards, 2, width, inner), BF16),
                 pltpu.SemaphoreType.DMA((4 * shards,)), pltpu.SemaphoreType.DMA((shards,))])

    partial_sums = ()
    for index in range(len(sizes) - 1):
        done = call(gather_body, [sds((tokens, width), F32)], "gather_back",
                    (returned[index], codes_of(experts, starts[index], sizes[index]), slot_col, gates), free=(0,))[0]
        partial_sums = (done,)
    small_rows = 16 * ((2 + experts + 15) // 16)
    grad_residual, grad_branch, mixed_grad, mixed_send, small_two = call(
        functools.partial(second_back_body, experts, sizes[-1], bool(partial_sums)),
        [sds((tokens, width), F32), sds((tokens, width), BF16), sds((2, tokens, local), BF16),
         sds((2, tokens, local), BF16), sds((2 + experts, width), F32)],
        "second_back",
        (returned[-1], codes_of(experts, starts[-1], sizes[-1]), slot_col, gates, ids_col, residual,
         normed_second, cotangent, gain_two, router, out_w[0], out_w[1], out_w[2], out_w[3]) + partial_sums, free=(2, 3, 4), near=(14,))
    mixed_got = swap(mixed_send, "head", 1)

    def attend_back(group, parts, weights, sums, weight_type, types):
        return call(
            functools.partial(attend_back_body, half, bool(sums)),
            [sds((3 * local, width), weight_type), sds((half, width), types[0]), sds((half, width), types[1])],
            "attend_back",
            (where, parts[0], parts[1], parts[2], parts[3], mixed_grad[group], mixed_got[group], normed_first,
             normed_other, weights) + tuple(sums), smem=(0,), vmem=24, free=(0, 1, 2), near=(5, 6, 10, 11),
            scratch=[pltpu.VMEM((length, width), BF16), pltpu.VMEM((length, local), BF16),
                     pltpu.VMEM((length, local), BF16), pltpu.VMEM((length, local), BF16),
                     pltpu.VMEM((length, local), F32), pltpu.VMEM((local, length), F32),
                     pltpu.VMEM((local, length), F32), pltpu.VMEM((3 * local, length), BF16),
                     pltpu.VMEM((length, width), F32)])

    far_grad, far_mine, far_theirs = attend_back(1, away, qkv_far, (), BF16, (F32, F32))
    out_grads = call(
        output_grad_body, [sds((2, local, width), BF16)] * 2, "output_grad",
        (after(grad_branch, mixed_got), mixed[0], mixed[1], mixed[2], mixed[3]))
    out_got = swap(out_grads[1], "head", 1)
    out_part = [out_grads[0][i].astype(F32) + out_got[i].astype(F32) for i in range(2)]
    far_got, out_far = swap(far_grad, "head", 2), swap(out_part[1].astype(BF16), "head", 2)

    grads_got = swap(expert_grads[2], "head", 1)
    far_sum = (expert_grads[1].astype(F32) + grads_got[1].astype(F32)).astype(BF16)
    far_sum = swap(after(far_sum, far_got), "head", 2)
    grad_expert = (expert_grads[0].astype(F32) + grads_got[0].astype(F32) + far_sum.astype(F32)) * keep
    near_grad, near_mine, near_theirs = attend_back(0, near, qkv, (far_mine, far_theirs), F32, (F32, BF16))
    first_got = swap(near_theirs, "head", 1)
    grad_input, small_one = call(
        first_back_body, [sds((tokens, width), F32), sds((2, width), F32)], "first_back",
        (activations, gain_one, near_mine, first_got, grad_residual))

    rows_back = exchange(after(expert_rows, returned[-1], expert_grads[0]))
    block_out = call(
        block_out_body, [sds((tokens, width), BF16)], "block_out",
        (rows_back, codes_of(experts, 0, slots), slot_col, gates, residual))[0]

    joined = jnp.concatenate([near_grad + far_got.astype(F32), (out_part[0] + out_far.astype(F32))], axis=0)
    joined = joined.astype(BF16)
    joined = after(joined, rows_back)
    scattered = exchange(joined.reshape(sources, 4 * local // sources, width))
    reduced = jnp.sum(scattered.astype(F32), axis=0).astype(BF16)
    small = jnp.concatenate([small_one, small_two], axis=0)
    small = jnp.pad(small, ((0, -small.shape[0] % 8), (0, 0)))
    small = small + swap(small, "head", 1)
    small = small + swap(small, "dp", 1)
    reduced = after(reduced, small, block_out)
    gathered = exchange(jnp.broadcast_to(reduced[None], (sources,) + reduced.shape))
    gathered = gathered.reshape(4 * local, width)

    step = 2
    while step < sources:
        small = small + swap(small, "dp", step)
        step *= 2
    small = small + swap(small, "head", 2)
    mask = new_mask.astype(F32)[None, :]
    gathered, grad_expert = lax.optimization_barrier((gathered, grad_expert))
    final = call(final_body, [sds((local, width), F32)] * 4, "final", (gathered,))
    return (
        block_out,
        grad_input,
        small[0],
        small[1],
        final[0].T,
        final[1].T,
        final[2].T,
        final[3],
        small[2],
        small[3],
        small[4 : 4 + experts].T * mask,
        grad_expert[0][None],
        grad_expert[1][None],
    )


def solution(mesh):
    placed = (
        P(("dp", "head"), None),
        P(),
        P(),
        P(None, "head"),
        P(None, "head"),
        P(None, "head"),
        P("head", None),
        P(),
        P(),
        P(),
        P("dp", None, "head"),
        P("dp", None, "head"),
        P(("dp", "head"), None),
        P(),
        P(),
        P(("dp", "head"), None),
    )
    return jax.shard_map(
        per_device,
        mesh=mesh,
        in_specs=placed,
        out_specs=(
            P(("dp", "head"), None),
            P(("dp", "head"), None),
            P(),
            P(),
            P(None, "head"),
            P(None, "head"),
            P(None, "head"),
            P("head", None),
            P(),
            P(),
            P(),
            P("dp", None, "head"),
            P("dp", None, "head"),
        ),
        check_vma=False,
    )
```

```python
import functools

import jax
import jax.numpy as jnp
import numpy as np
from jax import lax
from jax.experimental import pallas as pl
from jax.experimental.pallas import tpu as pltpu
from jax.sharding import PartitionSpec as P

HD = 64
LENGTH = 1024
NORM_EPSILON = 1e-05
MASKED_SCORE = -1e30
QUERY_ROWS = 256
STRIDE = 256
PAYLOAD = 16
MIB = 1 << 20
F32 = jnp.float32
BF16 = jnp.bfloat16
GELU_A = 0.7978845608028654
GELU_B = 0.044715


def dot_nn(left, right):
    return lax.dot_general(left, right, (((1,), (0,)), ((), ())), preferred_element_type=F32)


def dot_nt(left, right):
    return lax.dot_general(left, right, (((1,), (1,)), ((), ())), preferred_element_type=F32)


def dot_tn(left, right):
    return lax.dot_general(left, right, (((0,), (0,)), ((), ())), preferred_element_type=F32)


def iota(shape, axis):
    return lax.broadcasted_iota(jnp.int32, shape, axis)


def call(body, outs, name, ins, vmem=24, scratch=(), smem=(), hbm=(), free=(), out_hbm=(), pins=None, blocks=None):
    specs, given = [], []
    blocks = blocks or {}
    for index, value in enumerate(ins):
        if index in smem:
            specs.append(pl.BlockSpec(memory_space=pltpu.SMEM))
        elif index in hbm:
            specs.append(pl.BlockSpec(memory_space=pltpu.HBM))
        elif index in blocks:
            specs.append(blocks[index])
        else:
            specs.append(pl.BlockSpec())
        if index not in smem and any(value is p for p in pins):
            value = pltpu.with_memory_space_constraint(value, pltpu.HBM)
        given.append(value)
    results = pl.pallas_call(
        body,
        grid=(1,) if blocks else (),
        out_shape=[o if i in free else pltpu.HBM(o.shape, o.dtype) for i, o in enumerate(outs)],
        in_specs=specs,
        out_specs=[pl.BlockSpec(memory_space=pltpu.HBM) if i in out_hbm else pl.BlockSpec() for i in range(len(outs))],
        scratch_shapes=list(scratch),
        compiler_params=pltpu.CompilerParams(vmem_limit_bytes=vmem * MIB),
        cost_estimate=pl.CostEstimate(flops=1, bytes_accessed=1, transcendentals=0),
        name=name,
    )(*given)
    pins.extend(r for i, r in enumerate(results) if i not in free)
    return results


def sds(shape, dtype):
    return jax.ShapeDtypeStruct(shape, dtype)


def norm_parts(values):
    center = jnp.mean(values, axis=1, keepdims=True)
    centered = values - center
    rate = lax.rsqrt(jnp.mean(centered * centered, axis=1, keepdims=True) + NORM_EPSILON)
    return centered * rate, rate


def norm_back(normal, rate, gain, grad):
    scaled = grad * gain
    first = jnp.mean(scaled, axis=1, keepdims=True)
    second = jnp.mean(scaled * normal, axis=1, keepdims=True)
    return rate * (scaled - first - normal * second)


def first_norm_body(x_ref, norms_ref, out_ref):
    normal, _ = norm_parts(x_ref[...].astype(F32))
    out_ref[...] = (normal * norms_ref[0:1, :] + norms_ref[1:2, :]).astype(BF16)


def slot_hits(slot_row, experts, start, count):
    tokens = slot_row.shape[1]
    parts = []
    for e in range(experts):
        codes = iota((count, tokens), 0) + (e * STRIDE + start)
        hit = (slot_row[0:1] == codes) | (slot_row[1:2] == codes)
        parts.append(jnp.where(hit, 1.0, 0.0))
    return jnp.concatenate(parts, axis=0).astype(BF16)


def slots_of(ids, cap_ref):
    tokens = ids.shape[1]
    experts = cap_ref.shape[0]
    upper = jnp.where(iota((tokens, tokens), 0) < iota((tokens, tokens), 1), 1.0, 0.0).astype(BF16)
    rows_e = iota((experts, tokens), 0)
    hot = [jnp.where(ids[k : k + 1] == rows_e, 1.0, 0.0) for k in range(2)]
    earlier = dot_nn((hot[0] + hot[1]).astype(BF16), upper)
    column = iota((experts, 1), 0)
    limit = jnp.zeros((experts, 1), jnp.int32)
    for e in range(experts):
        limit = jnp.where(column == e, cap_ref[e], limit)
    limit = limit.astype(F32)
    rows = []
    for k in range(2):
        place = jnp.sum(hot[k] * earlier, axis=0, keepdims=True)
        top = jnp.sum(hot[k] * limit, axis=0, keepdims=True)
        rows.append(jnp.where(place < top, ids[k : k + 1] * STRIDE + place.astype(jnp.int32), -1))
    return jnp.concatenate(rows, axis=0)


def block_hits(slot_row, block, count):
    codes = iota((count, slot_row.shape[1]), 0) + block * STRIDE
    return jnp.where((slot_row[0:1] == codes) | (slot_row[1:2] == codes), 1.0, 0.0).astype(BF16)


def sort_rows(slots, here, slot_row, rows, send_refs):
    hits = [block_hits(slot_row, here ^ j, slots) for j in range(len(send_refs))]
    sent = dot_nn(jnp.concatenate(hits, axis=0), rows).astype(BF16)
    for j, ref in enumerate(send_refs):
        ref[...] = sent[j * slots : (j + 1) * slots]


def route_body(slots, where_ref, ids_row_ref, cap_ref, grad_ref, ids_ref, col_ref, row_ref, *send_refs):
    ids = ids_row_ref[...]
    slot_row = slots_of(ids, cap_ref)
    row_ref[...] = slot_row
    col_ref[...] = slot_row.astype(F32).T.astype(jnp.int32)
    ids_ref[...] = ids.astype(F32).T.astype(jnp.int32)
    sort_rows(slots, where_ref[1], slot_row, grad_ref[...], send_refs)


def mirror_body(slots, where_ref, cap_ref, grad_ref, *send_refs):
    tokens = grad_ref.shape[0] - PAYLOAD
    ids = grad_ref[tokens:, 0:tokens].astype(F32)[0:2].astype(jnp.int32)
    sort_rows(slots, where_ref[1], slots_of(ids, cap_ref), grad_ref[0:tokens, :], send_refs)


def attend_body(half, where_ref, own_ref, other_ref, w_ref,
                q_ref, k_ref, v_ref, log_ref, mine_ref, theirs_ref, rows, mixed, keys, vals):
    core = where_ref[0]
    mine = pl.multiple_of(core * half, half)
    theirs = pl.multiple_of((1 - core) * half, half)
    rows[pl.ds(mine, half), :] = own_ref[...]
    rows[pl.ds(theirs, half), :] = other_ref[...]
    length, width = q_ref.shape
    for part in range(2):
        block = slice(part * half, (part + 1) * half)
        source = rows[block, :]
        q_ref[block, :] = (dot_nt(source, w_ref[0:width, :]) * HD ** (-0.5)).astype(BF16)
        k_ref[block, :] = dot_nt(source, w_ref[width : 2 * width, :]).astype(BF16)
        v_ref[block, :] = dot_nt(source, w_ref[2 * width : 3 * width, :]).astype(BF16)
    heads = width // HD
    lane = iota((1, width), 1)
    triangle = iota((QUERY_ROWS, QUERY_ROWS), 0) >= iota((QUERY_ROWS, QUERY_ROWS), 1)
    for h in range(heads):
        keep = (lane >= h * HD) & (lane < (h + 1) * HD)
        keys[...] = jnp.where(keep, k_ref[...], 0)
        vals[...] = jnp.where(keep, v_ref[...], 0)
        for block in range(length // QUERY_ROWS):
            low = block * QUERY_ROWS
            here = slice(low, low + QUERY_ROWS)
            query = q_ref[here, :]
            diag = jnp.where(triangle, dot_nt(query, keys[here, :]), MASKED_SCORE)
            top = jnp.max(diag, axis=1, keepdims=True)
            if block:
                wide = dot_nt(query, keys[0:low, :])
                top = jnp.maximum(top, jnp.max(wide, axis=1, keepdims=True))
            diag = jnp.exp(diag - top)
            total = jnp.sum(diag, axis=1, keepdims=True)
            result = dot_nn(diag.astype(BF16), vals[here, :])
            if block:
                wide = jnp.exp(wide - top)
                total = total + jnp.sum(wide, axis=1, keepdims=True)
                result = result + dot_nn(wide.astype(BF16), vals[0:low, :])
            result = result / total
            log_ref[here, h : h + 1] = top + jnp.log(total)
            if h:
                result = result + mixed[here, :]
            mixed[here, :] = result
    mine_ref[...] = mixed[pl.ds(mine, half), :].astype(BF16)
    theirs_ref[...] = mixed[pl.ds(theirs, half), :].astype(BF16)


def gates_of(logits, ids_ref, lanes):
    hot = [ids_ref[:, k : k + 1] == lanes for k in range(2)]
    pair = [jnp.sum(jnp.where(hot[k], logits, 0.0), axis=1, keepdims=True) for k in range(2)]
    top = jnp.maximum(pair[0], pair[1])
    raised = [jnp.exp(p - top) for p in pair]
    total = raised[0] + raised[1]
    return [r / total for r in raised]


def split_rows(row, lines):
    high = row.astype(BF16).astype(F32)
    low = row - high
    both = jnp.concatenate([high, low], axis=1)
    return jnp.where(iota((lines, both.shape[1]), 0) == 0, both, 0.0).astype(BF16)


def post_body(experts, size, x_ref, m0, m1, m2, m3, near_ref, w1, far_ref, w3, norms_ref, row_ref,
              resid_ref, normed_ref, send_ref):
    branch = dot_nn(m0[...], near_ref[...]) + dot_nn(m1[...], w1[...])
    branch = branch + (dot_nn(m2[...], far_ref[...]) + dot_nn(m3[...], w3[...]))
    residual = x_ref[...].astype(F32) + branch
    resid_ref[...] = residual
    normal, _ = norm_parts(residual)
    normed = (normal * norms_ref[2:3, :] + norms_ref[3:4, :]).astype(BF16)
    normed_ref[...] = normed
    if size:
        hits = slot_hits(row_ref[...], experts, 0, size)
        send_ref[...] = dot_nn(hits, normed).astype(BF16).reshape(send_ref.shape)


def gate_body(experts, start, size, normed_ref, router_ref, ids_ref, col_ref, row_ref, gates_ref, send_ref):
    normed = normed_ref[...]
    tokens, width = normed.shape
    logits = dot_nt(normed, router_ref[...])
    gates = gates_of(logits, ids_ref, iota((tokens, experts), 1))
    gates_ref[:, 0:1] = gates[0]
    gates_ref[:, 1:2] = gates[1]
    hits = slot_hits(row_ref[...], experts, start, size)
    send_ref[:, 0:size, :] = dot_nn(hits, normed).astype(BF16).reshape(experts, size, width)
    for e in range(experts):
        codes = iota((tokens, STRIDE), 1) + e * STRIDE
        picked = [jnp.where(col_ref[:, k : k + 1] == codes, gates[k], 0.0) for k in range(2)]
        row = jnp.sum(picked[0] + picked[1], axis=0, keepdims=True)
        send_ref[e, size : size + PAYLOAD, 0 : 2 * STRIDE] = split_rows(row, PAYLOAD)
        send_ref[e, size : size + PAYLOAD, 2 * STRIDE :] = jnp.zeros((PAYLOAD, width - 2 * STRIDE), BF16)


def gelu_pair(values):
    square = values * values
    inner = values * (GELU_A + (GELU_A * GELU_B) * square)
    tanh = jnp.tanh(inner)
    half = 0.5 * tanh + 0.5
    slope = half + 0.5 * values * (1.0 - tanh * tanh) * (GELU_A + (3.0 * GELU_A * GELU_B) * square)
    return values * half, slope


def fetch_grads(here, own, mirror, start, size, target, sems):
    side = len(own)
    copies = []
    for j in range(side):
        for place, ref in ((here ^ j, own[j]), ((here ^ j) ^ side, mirror[j])):
            copies.append(pltpu.make_async_copy(ref.at[pl.ds(start, size)], target.at[place], sems.at[len(copies)]))
    for copy in copies:
        copy.start()
    return copies


def expert_body(shards, sources, start, size, last, where_ref, x_ref, *refs):
    refs = list(refs)
    side = sources // 2

    def take(count):
        taken = refs[:count]
        del refs[:count]
        return taken

    g_own, g_mirror, weights = take(side), take(side), take(shards)
    carry_ref, prior_ref = take(2) if last and start else (None, None)
    hidden_ref, pre_ref, back_ref, rows_ref = take(4)
    carry_out = None if last else take(1)[0]
    win_v, wout_v, hid_v, pre_v, g_v, in_sems, out_sems, g_sems = refs
    arriving = fetch_grads(where_ref[1], g_own, g_mirror, start, size, g_v, g_sems)
    copies = []
    for r in range(shards):
        pair = (pltpu.make_async_copy(weights[r].at[0], win_v.at[r], in_sems.at[2 * r]),
                pltpu.make_async_copy(weights[r].at[1], wout_v.at[r], in_sems.at[2 * r + 1]))
        for copy in pair:
            copy.start()
        copies.append(pair)
    width = x_ref.shape[2]
    rows = sources * size
    x = x_ref[:, 0:size, :].reshape(rows, width)
    for copy in arriving:
        copy.wait()
    g = g_v[...].reshape(rows, width)
    inner = win_v.shape[2]
    step = 256 if inner % 256 == 0 else inner
    score = jnp.zeros((rows, 1), F32)
    total, result = None, None
    outgoing = []
    for r in range(shards):
        for copy in copies[r]:
            copy.wait()
        for f in range(inner // step):
            cols = slice(f * step, (f + 1) * step)
            hid, slope = gelu_pair(dot_nn(x, win_v[r, :, cols]))
            grad = dot_nn(g, wout_v[r, :, cols])
            hid = hid.astype(BF16)
            score = score + jnp.sum(grad * hid.astype(F32), axis=1, keepdims=True)
            hid_v[r, :, cols] = hid
            pre_v[r, :, cols] = (grad * slope).astype(BF16)
        for source, target in ((hid_v, hidden_ref), (pre_v, pre_ref)):
            copy = pltpu.make_async_copy(source.at[r], target.at[r], out_sems.at[len(outgoing)])
            copy.start()
            outgoing.append(copy)
        part, out = dot_nt(pre_v[r], win_v[r]), dot_nt(hid_v[r], wout_v[r])
        total = part if total is None else total + part
        result = out if result is None else result + out
    back = total.astype(BF16).reshape(sources, size, width)
    result = result.astype(BF16).reshape(sources, size, width)
    eye = iota((size, STRIDE), 1) == iota((size, STRIDE), 0) + start
    if last:
        back_ref[:, 0:size, :] = back
        rows_ref[:, start:, :] = result
        if prior_ref is not None:
            rows_ref[:, 0:start, :] = prior_ref[...]
    else:
        back_ref[...] = back
        rows_ref[...] = result
    for s in range(sources):
        row = jnp.sum(jnp.where(eye, score[s * size : (s + 1) * size], 0.0), axis=0, keepdims=True)
        if last:
            if carry_ref is not None:
                row = row + carry_ref[s : s + 1, :]
            back_ref[s, size : size + PAYLOAD, 0 : 2 * STRIDE] = split_rows(row, PAYLOAD)
            back_ref[s, size : size + PAYLOAD, 2 * STRIDE :] = jnp.zeros((PAYLOAD, width - 2 * STRIDE), BF16)
        else:
            carry_out[s : s + 1, :] = row
    for copy in outgoing:
        copy.wait()


def expert_grad_body(picks, shards, sources, sizes, where_ref, *refs):
    refs = list(refs)
    count = len(sizes)

    def take(number):
        taken = refs[:number]
        del refs[:number]
        return taken

    x_refs, g_own, g_mirror, hidden, pre = take(count), take(sources // 2), take(sources // 2), take(count), take(count)
    home_ref, send_ref = take(2)
    xt, gt, hid_v, pre_v, out_v, g_v, in_sems, out_sems, g_sems = refs
    arriving = fetch_grads(where_ref[1], g_own, g_mirror, 0, sum(sizes), g_v, g_sems)
    copies = []
    for place, r in enumerate(picks):
        base = 0
        group = []
        for index, size in enumerate(sizes):
            rows = sources * size
            for which, (source, target) in enumerate(((pre[index], pre_v), (hidden[index], hid_v))):
                copy = pltpu.make_async_copy(source.at[r], target.at[place, pl.ds(base, rows)],
                                             in_sems.at[(place * count + index) * 2 + which])
                copy.start()
                group.append(copy)
            base += rows
        copies.append(group)
    width = x_refs[0].shape[2]
    last = x_refs[-1]
    for copy in arriving:
        copy.wait()
    start, base = 0, 0
    for ref, size in zip(x_refs, sizes):
        rows = sources * size
        eye = iota((size, STRIDE), 1) == iota((size, STRIDE), 0) + start
        gate = []
        for s in range(sources):
            row = last[s, sizes[-1] : sizes[-1] + PAYLOAD, :].astype(F32)
            row = row[0:1, 0:STRIDE] + row[0:1, STRIDE : 2 * STRIDE]
            gate.append(jnp.sum(jnp.where(eye, row, 0.0), axis=1, keepdims=True))
        gate = jnp.concatenate(gate, axis=0)
        x = ref[:, 0:size, :].reshape(rows, width).astype(F32) * gate
        g = g_v[:, start : start + size, :].reshape(rows, width).astype(F32) * gate
        xt[:, base : base + rows] = x.T.astype(BF16)
        gt[:, base : base + rows] = g.T.astype(BF16)
        start += size
        base += rows
    outgoing = []
    for place, r in enumerate(picks):
        for copy in copies[place]:
            copy.wait()
        for which, (left, right) in enumerate(((xt, pre_v), (gt, hid_v))):
            out_v[place, which] = dot_nn(left[...], right[place]).astype(BF16)
            target = (send_ref if r % 2 else home_ref).at[r // 2, which]
            copy = pltpu.make_async_copy(out_v.at[place, which], target, out_sems.at[2 * place + which])
            copy.start()
            outgoing.append(copy)
    for copy in outgoing:
        copy.wait()


def grad_sum_body(keep_ref, home_ref, got_ref, passed_ref, *out_refs):
    for index, ref in enumerate(out_refs):
        total = home_ref[0, index].astype(F32) + got_ref[0, index].astype(F32)
        ref[...] = (total + passed_ref[index].astype(F32)) * keep_ref[0, 0]


def gather_body(rows_ref, codes_ref, col_ref, gates_ref, sum_ref):
    sources, size, width = rows_ref.shape
    codes = codes_ref[...]
    pick = jnp.where(col_ref[:, 0:1] == codes, gates_ref[:, 0:1], 0.0)
    pick = jnp.where(col_ref[:, 1:2] == codes, gates_ref[:, 1:2], pick).astype(BF16)
    sum_ref[...] = dot_nn(pick, rows_ref[...].reshape(sources * size, width))


def second_back_body(experts, size, has_sum, *refs):
    refs = list(refs)
    (rows_ref, codes_ref, col_ref, gates_ref, ids_ref, resid_ref, normed_ref, cot_ref, norms_ref, router_ref) = refs[:10]
    del refs[:10]
    sum_ref = refs.pop(0) if has_sum else None
    grad_ref, branch_ref, small_ref = refs
    sources, _, width = rows_ref.shape
    tokens = resid_ref.shape[0]
    codes = codes_ref[...]
    gates = [gates_ref[:, k : k + 1] for k in range(2)]
    slot = [col_ref[:, k : k + 1] for k in range(2)]
    pick = jnp.where(slot[0] == codes, gates[0], 0.0)
    pick = jnp.where(slot[1] == codes, gates[1], pick).astype(BF16)
    total = dot_nn(pick, rows_ref[:, 0:size, :].reshape(sources * size, width))
    if sum_ref is not None:
        total = total + sum_ref[...]
    scores = [jnp.zeros((tokens, 1), F32), jnp.zeros((tokens, 1), F32)]
    for e in range(experts):
        line = rows_ref[e, size : size + PAYLOAD, :].astype(F32)
        line = line[0:1, 0:STRIDE] + line[0:1, STRIDE : 2 * STRIDE]
        place = iota((tokens, STRIDE), 1) + e * STRIDE
        for k in range(2):
            scores[k] = scores[k] + jnp.sum(jnp.where(slot[k] == place, line, 0.0), axis=1, keepdims=True)
    inner = gates[0] * scores[0] + gates[1] * scores[1]
    lanes = iota((tokens, experts), 1)
    logit_grad = jnp.zeros((tokens, experts), F32)
    for k in range(2):
        logit_grad = jnp.where(ids_ref[:, k : k + 1] == lanes, gates[k] * (scores[k] - inner), logit_grad)
    logit_grad = logit_grad.astype(BF16)
    total = total + dot_nn(logit_grad, router_ref[...])
    normal, rate = norm_parts(resid_ref[...])
    grad = cot_ref[...].astype(F32) + norm_back(normal, rate, norms_ref[2:3, :], total)
    grad_ref[...] = grad
    branch_ref[...] = grad.astype(BF16)
    small_ref[0:1, :] = jnp.sum(total * normal, axis=0, keepdims=True)
    small_ref[1:2, :] = jnp.sum(total, axis=0, keepdims=True)
    small_ref[2 : 2 + experts, :] = dot_tn(logit_grad, normed_ref[...])


def attend_back_body(half, has_sum, where_ref, *refs):
    refs = list(refs)
    (q_ref, k_ref, v_ref, log_ref, mixed_own, mixed_other, branch_own, branch_other, own_ref, other_ref,
     w_ref) = refs[:11]
    del refs[:11]
    sums = (refs.pop(0), refs.pop(0)) if has_sum else None
    weight_ref, mine_ref, theirs_ref, rows, branch, grads, mixed, keys, vals, dq, dk, dv, joined, pile = refs
    core = where_ref[0]
    mine = pl.multiple_of(core * half, half)
    theirs = pl.multiple_of((1 - core) * half, half)
    rows[pl.ds(mine, half), :] = own_ref[...]
    rows[pl.ds(theirs, half), :] = other_ref[...]
    branch[pl.ds(mine, half), :] = branch_own[...]
    branch[pl.ds(theirs, half), :] = branch_other[...]
    mixed[pl.ds(mine, half), :] = mixed_own[...]
    mixed[pl.ds(theirs, half), :] = mixed_other[...]
    length, width = q_ref.shape
    grads[...] = dot_nt(branch[...], w_ref[3 * width :, :]).astype(BF16)
    heads = width // HD
    lane = iota((1, width), 1)
    triangle = iota((QUERY_ROWS, QUERY_ROWS), 0) >= iota((QUERY_ROWS, QUERY_ROWS), 1)
    qt = q_ref[...].astype(F32).T.astype(BF16)
    gt = grads[...].astype(F32).T.astype(BF16)
    dk[...] = jnp.zeros(dk.shape, F32)
    dv[...] = jnp.zeros(dv.shape, F32)
    for h in range(heads):
        keep = (lane >= h * HD) & (lane < (h + 1) * HD)
        keys[...] = jnp.where(keep, k_ref[...], 0)
        vals[...] = jnp.where(keep, v_ref[...], 0)
        head = slice(h * HD, (h + 1) * HD)
        for block in range(length // QUERY_ROWS):
            low = block * QUERY_ROWS
            here = slice(low, low + QUERY_ROWS)
            query, grad, log = q_ref[here, :], grads[here, :], log_ref[here, h : h + 1]
            spans = [slice(0, low)] if block else []
            spans.append(here)
            probs, outer = [], []
            inner = None
            for span in spans:
                score = dot_nt(query, keys[span, :])
                if span is here:
                    score = jnp.where(triangle, score, MASKED_SCORE)
                prob = jnp.exp(score - log)
                grad_prob = dot_nt(grad, vals[span, :])
                part = jnp.sum(prob * grad_prob, axis=1, keepdims=True)
                inner = part if inner is None else inner + part
                probs.append(prob)
                outer.append(grad_prob)
            query_grad = None
            for span, prob, grad_prob in zip(spans, probs, outer):
                score_grad = (prob * (grad_prob - inner)).astype(BF16)
                part = dot_nn(score_grad, keys[span, :])
                query_grad = part if query_grad is None else query_grad + part
                dv[head, span] = dv[head, span] + dot_nn(gt[head, here], prob.astype(BF16))
                dk[head, span] = dk[head, span] + dot_nn(qt[head, here], score_grad)
            if h:
                query_grad = query_grad + dq[here, :]
            dq[here, :] = query_grad
    query_grads = dq[...].astype(BF16).astype(F32) * HD ** (-0.5)
    joined[0:width, :] = query_grads.T.astype(BF16)
    joined[width : 2 * width, :] = dk[...].astype(BF16)
    joined[2 * width : 3 * width, :] = dv[...].astype(BF16)
    total = dot_nn(query_grads.astype(BF16), w_ref[0:width, :])
    total = total + dot_nn(dk[...].T.astype(BF16), w_ref[width : 2 * width, :])
    total = total + dot_nn(dv[...].T.astype(BF16), w_ref[2 * width : 3 * width, :])
    pile[...] = total
    one, two = pile[pl.ds(mine, half), :], pile[pl.ds(theirs, half), :]
    if sums is not None:
        one, two = one + sums[0][...], two + sums[1][...]
    mine_ref[...] = one.astype(mine_ref.dtype)
    theirs_ref[...] = two.astype(theirs_ref.dtype)
    weight_ref[0 : 3 * width, :] = dot_nn(joined[...], rows[...]).astype(weight_ref.dtype)
    turned = mixed[...].astype(F32).T.astype(BF16)
    weight_ref[3 * width :, :] = dot_nn(turned, branch[...]).astype(weight_ref.dtype)


def first_back_body(x_ref, norms_ref, mine_ref, other_ref, resid_ref, out_ref, small_ref):
    grad = mine_ref[...] + other_ref[...].astype(F32)
    normal, rate = norm_parts(x_ref[...].astype(F32))
    out_ref[...] = resid_ref[...] + norm_back(normal, rate, norms_ref[0:1, :], grad)
    small_ref[0:1, :] = jnp.sum(grad * normal, axis=0, keepdims=True)
    small_ref[1:2, :] = jnp.sum(grad, axis=0, keepdims=True)


def block_out_body(rows_ref, codes_ref, col_ref, gates_ref, resid_ref, out_ref):
    sources, size, width = rows_ref.shape
    codes = codes_ref[...]
    pick = jnp.where(col_ref[:, 0:1] == codes, gates_ref[:, 0:1], 0.0)
    pick = jnp.where(col_ref[:, 1:2] == codes, gates_ref[:, 1:2], pick).astype(BF16)
    moe = dot_nn(pick, rows_ref[...].reshape(sources * size, width))
    out_ref[...] = (resid_ref[...] + moe).astype(BF16)


def final_body(all_ref, *out_refs):
    rows = out_refs[0].shape[0]
    for index, ref in enumerate(out_refs):
        ref[...] = all_ref[index * rows : (index + 1) * rows, :].astype(F32)


def swap(value, axis, step):
    size = lax.axis_size(axis)
    return lax.ppermute(value, axis, [(i, i ^ step) for i in range(size)])


def exchange(value):
    return lax.all_to_all(value, "dp", split_axis=0, concat_axis=0, tiled=True)


def after(value, *others):
    return lax.optimization_barrier((value,) + others)[0]


def codes_of(experts, start, size):
    table = np.arange(experts)[:, None] * STRIDE + start + np.arange(size)[None, :]
    return jnp.asarray(table.reshape(1, -1).astype(np.int32))


def per_device(activations, first_gain, first_shift, query_weight, key_weight, value_weight, output_weight,
               second_gain, second_shift, router_weight, expert_in, expert_out, expert_ids, capacity, new_mask,
               cotangent):
    kernel = functools.partial(call, pins=[activations, output_weight, cotangent])
    tokens, width = activations.shape
    local = query_weight.shape[1]
    heads = local // HD
    experts = router_weight.shape[1]
    sources = lax.axis_size("dp")
    shards = lax.axis_size("head")
    slots = 3 * tokens // experts
    sizes = (slots // 32 * 16, slots - slots // 32 * 16) if slots % 16 == 0 and slots >= 32 else (slots,)
    starts = tuple(sum(sizes[:i]) for i in range(len(sizes)))
    length, half, side = LENGTH, tokens, sources // 2
    where = jnp.stack([lax.axis_index("head") % 2, lax.axis_index("dp")]).astype(jnp.int32)
    last_rows = pl.BlockSpec((local, width), lambda i: (3, 0))

    attn_w = jnp.concatenate([query_weight.T, key_weight.T, value_weight.T, output_weight], axis=0)
    far_w = swap(attn_w, "head", 2)
    norms = jnp.stack([first_gain, first_shift, second_gain, second_shift])
    router = router_weight.T

    normed_first = kernel(first_norm_body, [sds((tokens, width), BF16)], "norm_first", (activations, norms), vmem=16)[0]
    normed_other = swap(normed_first, "head", 1)

    ids_row = expert_ids.T
    extra = jnp.pad(ids_row.astype(BF16), ((0, PAYLOAD - 2), (0, width - tokens)))
    mirror_grad = swap(jnp.concatenate([cotangent, extra], axis=0), "dp", side)
    routed = kernel(
        functools.partial(route_body, slots),
        [sds((tokens, 2), jnp.int32), sds((tokens, 2), jnp.int32), sds((2, tokens), jnp.int32)]
        + [sds((slots, width), BF16)] * side,
        "route", (where, ids_row, capacity, cotangent), smem=(0, 2))
    ids_col, slot_col, slot_row = routed[:3]
    grad_own = [routed[3]] + [swap(routed[3 + j], "dp", j) for j in range(1, side)]

    def attend(weight):
        return kernel(
            functools.partial(attend_body, half),
            [sds((length, local), BF16)] * 3 + [sds((length, heads), F32)] + [sds((half, local), BF16)] * 2,
            "attend", (where, normed_first, normed_other, weight), smem=(0,),
            scratch=[pltpu.VMEM((length, width), BF16), pltpu.VMEM((length, local), F32),
                     pltpu.VMEM((length, local), BF16), pltpu.VMEM((length, local), BF16)])

    near = attend(attn_w)
    mixed = {0: near[4], 1: swap(near[5], "head", 1)}
    far_w = after(far_w, near[4], slot_row)
    away = attend(far_w)
    mixed[2], mixed[3] = away[4], swap(away[5], "head", 1)
    out_w = {1: swap(output_weight, "head", 1), 3: swap(far_w[3 * local :], "head", 1)}

    weights = {0: jnp.stack([expert_in[0], expert_out[0]])}
    weights[1] = swap(weights[0], "head", 1)
    weights[2] = swap(after(weights[0], far_w), "head", 2)
    weights[3] = swap(weights[2], "head", 1)
    inner = weights[0].shape[2]

    mirror_send = kernel(
        functools.partial(mirror_body, slots), [sds((slots, width), BF16)] * side, "mirror",
        (where, capacity, mirror_grad), smem=(0, 1))
    grad_mirror = [mirror_send[0]] + [swap(mirror_send[j], "dp", j) for j in range(1, side)]
    first_size = sizes[0] if len(sizes) > 1 else 0
    residual, normed_second, sent = kernel(
        functools.partial(post_body, experts, first_size),
        [sds((tokens, width), F32), sds((tokens, width), BF16), sds((experts, max(first_size, 16), width), BF16)],
        "post_attend",
        (activations, mixed[0], mixed[1], mixed[2], mixed[3], output_weight, out_w[1], far_w, out_w[3], norms,
         after(slot_row, mirror_send[0], *grad_own[1:])), free=(2,), blocks={7: last_rows}, vmem=32)
    gates, sent_last = kernel(
        functools.partial(gate_body, experts, starts[-1], sizes[-1]),
        [sds((tokens, 2), F32), sds((experts, sizes[-1] + PAYLOAD, width), BF16)],
        "gates", (normed_second, router, ids_col, slot_col, slot_row))
    rows_in = []
    if first_size:
        rows_in.append(exchange(sent))
    sent_last = after(sent_last, weights[2], *(rows_in + grad_mirror[1:]))
    rows_in.append(exchange(sent_last))

    hidden, pre, back = [], [], []
    carry = ()
    for index, size in enumerate(sizes):
        last = index == len(sizes) - 1
        rows = sources * size
        kept = slots if last else size
        outs = [sds((shards, rows, inner), BF16), sds((shards, rows, inner), BF16),
                sds((sources, size + (PAYLOAD if last else 0), width), BF16), sds((sources, kept, width), BF16)]
        ins = (where, rows_in[index]) + tuple(grad_own) + tuple(grad_mirror)
        first = len(ins)
        ins = ins + tuple(weights[r] for r in range(shards)) + carry
        if not last:
            outs.append(sds((sources, STRIDE), F32))
        result = kernel(
            functools.partial(expert_body, shards, sources, starts[index], size, last), outs, "expert", ins,
            vmem=60 if rows <= 768 else 62, smem=(0,), hbm=tuple(range(2, first + shards)), free=(2,),
            out_hbm=(0, 1),
            scratch=[pltpu.VMEM((shards, width, inner), BF16), pltpu.VMEM((shards, width, inner), BF16),
                     pltpu.VMEM((shards, rows, inner), BF16), pltpu.VMEM((shards, rows, inner), BF16),
                     pltpu.VMEM((sources, size, width), BF16), pltpu.SemaphoreType.DMA((2 * shards,)),
                     pltpu.SemaphoreType.DMA((2 * shards,)), pltpu.SemaphoreType.DMA((sources,))])
        hidden.append(result[0])
        pre.append(result[1])
        back.append(result[2])
        expert_rows = result[3]
        if not last:
            carry = (result[4], result[3])
    returned, done = [], rows_in[-1]
    for part in back:
        done = exchange(after(part, done))
        returned.append(done)

    keep = jnp.sum(jnp.where(jnp.arange(experts) == lax.axis_index("dp"), new_mask, 0)).astype(F32).reshape(1, 1)
    all_rows = sources * slots
    picks = tuple(range(1, shards, 2)) + tuple(range(0, shards, 2))
    skip = 1 + len(sizes)
    grads_home, grads_send = kernel(
        functools.partial(expert_grad_body, picks, shards, sources, sizes),
        [sds((shards // 2, 2, width, inner), BF16)] * 2, "expert_grads",
        (where,) + tuple(rows_in) + tuple(grad_own) + tuple(grad_mirror) + tuple(hidden) + tuple(pre), vmem=60,
        smem=(0,), hbm=tuple(range(skip, skip + sources + 2 * len(sizes))), out_hbm=(0, 1),
        scratch=[pltpu.VMEM((width, all_rows), BF16), pltpu.VMEM((width, all_rows), BF16),
                 pltpu.VMEM((shards, all_rows, inner), BF16), pltpu.VMEM((shards, all_rows, inner), BF16),
                 pltpu.VMEM((shards, 2, width, inner), BF16), pltpu.VMEM((sources, slots, width), BF16),
                 pltpu.SemaphoreType.DMA((4 * shards,)), pltpu.SemaphoreType.DMA((2 * shards,)),
                 pltpu.SemaphoreType.DMA((sources,))])
    grads_got = swap(grads_send, "head", 1)

    partial_sums = ()
    if first_size:
        partial_sums = tuple(kernel(
            gather_body, [sds((tokens, width), F32)], "gather_back",
            (returned[0], codes_of(experts, 0, first_size), slot_col, gates), free=(0,)))
    grad_residual, grad_branch, small_two = kernel(
        functools.partial(second_back_body, experts, sizes[-1], bool(partial_sums)),
        [sds((tokens, width), F32), sds((tokens, width), BF16), sds((2 + experts, width), F32)], "second_back",
        (returned[-1], codes_of(experts, starts[-1], sizes[-1]), slot_col, gates, ids_col, residual,
         normed_second, cotangent, norms, router) + partial_sums, free=(1, 2))
    branch_other = swap(grad_branch, "head", 1)

    def attend_back(parts, mixed_other, weight, sums, weight_type, types):
        return kernel(
            functools.partial(attend_back_body, half, bool(sums)),
            [sds((4 * local, width), weight_type), sds((half, width), types[0]), sds((half, width), types[1])],
            "attend_back",
            (where,) + tuple(parts[:4]) + (parts[4], parts[5], grad_branch, branch_other, normed_first, normed_other,
                                           weight) + tuple(sums),
            smem=(0,), vmem=32, free=(0, 1, 2),
            scratch=[pltpu.VMEM((length, width), BF16), pltpu.VMEM((length, width), BF16),
                     pltpu.VMEM((length, local), BF16), pltpu.VMEM((length, local), BF16),
                     pltpu.VMEM((length, local), BF16), pltpu.VMEM((length, local), BF16),
                     pltpu.VMEM((length, local), F32), pltpu.VMEM((local, length), F32),
                     pltpu.VMEM((local, length), F32), pltpu.VMEM((3 * local, length), BF16),
                     pltpu.VMEM((length, width), F32)])

    far_grad, far_mine, far_theirs = attend_back(away, mixed[3], far_w, (), BF16, (F32, F32))
    far_got = swap(far_grad, "head", 2)
    near_grad, near_mine, near_theirs = attend_back(near, mixed[1], attn_w, (far_mine, far_theirs), F32, (F32, BF16))
    first_got = swap(near_theirs, "head", 1)
    grad_input, small_one = kernel(
        first_back_body, [sds((tokens, width), F32), sds((2, width), F32)], "first_back",
        (activations, norms, near_mine, first_got, grad_residual))

    rows_back = exchange(after(expert_rows, returned[-1], grads_home, *partial_sums))
    block_out = kernel(
        block_out_body, [sds((tokens, width), BF16)], "block_out",
        (rows_back, codes_of(experts, 0, slots), slot_col, gates, residual))[0]

    passed = (grads_home[1].astype(F32) + grads_got[1].astype(F32)).astype(BF16)
    joined = after((near_grad + far_got.astype(F32)).astype(BF16), rows_back, passed)
    passed = swap(after(passed, far_got), "head", 2)
    scattered = exchange(joined.reshape(sources, 4 * local // sources, width))
    reduced = jnp.sum(scattered.astype(F32), axis=0).astype(BF16)
    small = jnp.concatenate([small_one, small_two], axis=0)
    small = jnp.pad(small, ((0, -small.shape[0] % 8), (0, 0)))
    small = small + swap(small, "head", 1)
    step = 1
    while step < sources:
        small = small + swap(small if step == 1 else after(small, block_out), "dp", step)
        step *= 2
    reduced = after(reduced, small)
    gathered = exchange(jnp.broadcast_to(reduced[None], (sources,) + reduced.shape))

    part = pl.BlockSpec((1, 2, width, inner), lambda i: (0, 0, 0, 0))
    grad_in, grad_out = kernel(
        grad_sum_body, [sds((width, inner), F32), sds((width, inner), F32)], "grad_sum",
        (keep, grads_home, grads_got, passed), smem=(0,), vmem=40, blocks={1: part, 2: part})

    small = small + swap(small, "head", 2)
    gathered = after(gathered.reshape(4 * local, width), grad_in)
    final = kernel(final_body, [sds((local, width), F32)] * 4, "final", (gathered,))
    mask = new_mask.astype(F32)[None, :]
    return (
        block_out,
        grad_input,
        small[0],
        small[1],
        final[0].T,
        final[1].T,
        final[2].T,
        final[3],
        small[2],
        small[3],
        small[4 : 4 + experts].T * mask,
        grad_in[None],
        grad_out[None],
    )


def solution(mesh):
    placed = (
        P(("dp", "head"), None),
        P(),
        P(),
        P(None, "head"),
        P(None, "head"),
        P(None, "head"),
        P("head", None),
        P(),
        P(),
        P(),
        P("dp", None, "head"),
        P("dp", None, "head"),
        P(("dp", "head"), None),
        P(),
        P(),
        P(("dp", "head"), None),
    )
    return jax.shard_map(
        per_device,
        mesh=mesh,
        in_specs=placed,
        out_specs=(
            P(("dp", "head"), None),
            P(("dp", "head"), None),
            P(),
            P(),
            P(None, "head"),
            P(None, "head"),
            P(None, "head"),
            P("head", None),
            P(),
            P(),
            P(),
            P("dp", None, "head"),
            P("dp", None, "head"),
        ),
        check_vma=False,
    )
```

```python
import functools

import jax
import jax.numpy as jnp
import numpy as np
from jax import lax
from jax.experimental import pallas as pl
from jax.experimental.pallas import tpu as pltpu
from jax.sharding import PartitionSpec as P

HD = 64
LENGTH = 1024
NORM_EPSILON = 1e-05
MASKED_SCORE = -1e30
QUERY_ROWS = 256
STRIDE = 256
PAYLOAD = 8
MIB = 1 << 20
F32 = jnp.float32
BF16 = jnp.bfloat16
GELU_A = 0.7978845608028654
GELU_B = 0.044715


def dot_nn(left, right):
    return lax.dot_general(left, right, (((1,), (0,)), ((), ())), preferred_element_type=F32)


def dot_nt(left, right):
    return lax.dot_general(left, right, (((1,), (1,)), ((), ())), preferred_element_type=F32)


def dot_tn(left, right):
    return lax.dot_general(left, right, (((0,), (0,)), ((), ())), preferred_element_type=F32)


def iota(shape, axis):
    return lax.broadcasted_iota(jnp.int32, shape, axis)


def call(body, outs, name, ins, vmem=24, scratch=(), smem=(), hbm=(), free=(), out_hbm=(), pins=None, blocks=None):
    specs, given = [], []
    blocks = blocks or {}
    for index, value in enumerate(ins):
        if index in smem:
            specs.append(pl.BlockSpec(memory_space=pltpu.SMEM))
        elif index in hbm:
            specs.append(pl.BlockSpec(memory_space=pltpu.HBM))
        elif index in blocks:
            specs.append(blocks[index])
        else:
            specs.append(pl.BlockSpec())
        if index not in smem and any(value is p for p in pins):
            value = pltpu.with_memory_space_constraint(value, pltpu.HBM)
        given.append(value)
    results = pl.pallas_call(
        body,
        grid=(1,) if blocks else (),
        out_shape=[o if i in free else pltpu.HBM(o.shape, o.dtype) for i, o in enumerate(outs)],
        in_specs=specs,
        out_specs=[pl.BlockSpec(memory_space=pltpu.HBM) if i in out_hbm else pl.BlockSpec() for i in range(len(outs))],
        scratch_shapes=list(scratch),
        compiler_params=pltpu.CompilerParams(vmem_limit_bytes=vmem * MIB),
        cost_estimate=pl.CostEstimate(flops=1, bytes_accessed=1, transcendentals=0),
        name=name,
    )(*given)
    pins.extend(r for i, r in enumerate(results) if i not in free)
    return results


def sds(shape, dtype):
    return jax.ShapeDtypeStruct(shape, dtype)


def norm_parts(values):
    center = jnp.mean(values, axis=1, keepdims=True)
    centered = values - center
    rate = lax.rsqrt(jnp.mean(centered * centered, axis=1, keepdims=True) + NORM_EPSILON)
    return centered * rate, rate


def norm_back(normal, rate, gain, grad):
    scaled = grad * gain
    first = jnp.mean(scaled, axis=1, keepdims=True)
    second = jnp.mean(scaled * normal, axis=1, keepdims=True)
    return rate * (scaled - first - normal * second)


def first_norm_body(x_ref, norms_ref, out_ref):
    normal, _ = norm_parts(x_ref[...].astype(F32))
    out_ref[...] = (normal * norms_ref[0:1, :] + norms_ref[1:2, :]).astype(BF16)


def slot_hits(slot_row, experts, start, count):
    tokens = slot_row.shape[1]
    parts = []
    for e in range(experts):
        codes = iota((count, tokens), 0) + (e * STRIDE + start)
        hit = (slot_row[0:1] == codes) | (slot_row[1:2] == codes)
        parts.append(jnp.where(hit, 1.0, 0.0))
    return jnp.concatenate(parts, axis=0).astype(BF16)


def slots_of(ids, cap_ref):
    tokens = ids.shape[1]
    experts = cap_ref.shape[0]
    upper = jnp.where(iota((tokens, tokens), 0) < iota((tokens, tokens), 1), 1.0, 0.0).astype(BF16)
    rows_e = iota((experts, tokens), 0)
    hot = [jnp.where(ids[k : k + 1] == rows_e, 1.0, 0.0) for k in range(2)]
    earlier = dot_nn((hot[0] + hot[1]).astype(BF16), upper)
    column = iota((experts, 1), 0)
    limit = jnp.zeros((experts, 1), jnp.int32)
    for e in range(experts):
        limit = jnp.where(column == e, cap_ref[e], limit)
    limit = limit.astype(F32)
    rows = []
    for k in range(2):
        place = jnp.sum(hot[k] * earlier, axis=0, keepdims=True)
        top = jnp.sum(hot[k] * limit, axis=0, keepdims=True)
        rows.append(jnp.where(place < top, ids[k : k + 1] * STRIDE + place.astype(jnp.int32), -1))
    return jnp.concatenate(rows, axis=0)


def block_hits(slot_row, block, count):
    codes = iota((count, slot_row.shape[1]), 0) + block * STRIDE
    return jnp.where((slot_row[0:1] == codes) | (slot_row[1:2] == codes), 1.0, 0.0).astype(BF16)


def sort_rows(slots, here, slot_row, rows, send_refs):
    hits = [block_hits(slot_row, here ^ j, slots) for j in range(len(send_refs))]
    sent = dot_nn(jnp.concatenate(hits, axis=0), rows).astype(BF16)
    for j, refs in enumerate(send_refs):
        start = j * slots
        for ref in refs:
            ref[...] = sent[start : start + ref.shape[0]]
            start += ref.shape[0]


def route_body(slots, where_ref, ids_row_ref, cap_ref, grad_ref, ids_ref, col_ref, row_ref, *send_refs):
    ids = ids_row_ref[...]
    slot_row = slots_of(ids, cap_ref)
    row_ref[...] = slot_row
    col_ref[...] = slot_row.astype(F32).T.astype(jnp.int32)
    ids_ref[...] = ids.astype(F32).T.astype(jnp.int32)
    sort_rows(slots, where_ref[1], slot_row, grad_ref[...], [[ref] for ref in send_refs])


def mirror_body(slots, parts, where_ref, cap_ref, grad_ref, *send_refs):
    tokens = grad_ref.shape[0] - PAYLOAD
    ids = grad_ref[tokens:, 0:tokens].astype(F32)[0:2].astype(jnp.int32)
    side = len(send_refs) // parts
    groups = [send_refs[j::side] for j in range(side)]
    sort_rows(slots, where_ref[1], slots_of(ids, cap_ref), grad_ref[0:tokens, :], groups)


def attend_body(half, where_ref, own_ref, other_ref, w_ref,
                q_ref, k_ref, v_ref, log_ref, mine_ref, theirs_ref, rows, mixed, keys, vals):
    core = where_ref[0]
    mine = pl.multiple_of(core * half, half)
    theirs = pl.multiple_of((1 - core) * half, half)
    rows[pl.ds(mine, half), :] = own_ref[...]
    rows[pl.ds(theirs, half), :] = other_ref[...]
    length, width = q_ref.shape
    for part in range(2):
        block = slice(part * half, (part + 1) * half)
        source = rows[block, :]
        q_ref[block, :] = (dot_nt(source, w_ref[0:width, :]) * HD ** (-0.5)).astype(BF16)
        k_ref[block, :] = dot_nt(source, w_ref[width : 2 * width, :]).astype(BF16)
        v_ref[block, :] = dot_nt(source, w_ref[2 * width : 3 * width, :]).astype(BF16)
    heads = width // HD
    lane = iota((1, width), 1)
    triangle = iota((QUERY_ROWS, QUERY_ROWS), 0) >= iota((QUERY_ROWS, QUERY_ROWS), 1)
    for h in range(heads):
        keep = (lane >= h * HD) & (lane < (h + 1) * HD)
        keys[...] = jnp.where(keep, k_ref[...], 0)
        vals[...] = jnp.where(keep, v_ref[...], 0)
        for block in range(length // QUERY_ROWS):
            low = block * QUERY_ROWS
            here = slice(low, low + QUERY_ROWS)
            query = q_ref[here, :]
            diag = jnp.where(triangle, dot_nt(query, keys[here, :]), MASKED_SCORE)
            top = jnp.max(diag, axis=1, keepdims=True)
            if block:
                wide = dot_nt(query, keys[0:low, :])
                top = jnp.maximum(top, jnp.max(wide, axis=1, keepdims=True))
            diag = jnp.exp(diag - top)
            total = jnp.sum(diag, axis=1, keepdims=True)
            result = dot_nn(diag.astype(BF16), vals[here, :])
            if block:
                wide = jnp.exp(wide - top)
                total = total + jnp.sum(wide, axis=1, keepdims=True)
                result = result + dot_nn(wide.astype(BF16), vals[0:low, :])
            result = result / total
            log_ref[here, h : h + 1] = top + jnp.log(total)
            if h:
                result = result + mixed[here, :]
            mixed[here, :] = result
    mine_ref[...] = mixed[pl.ds(mine, half), :].astype(BF16)
    theirs_ref[...] = mixed[pl.ds(theirs, half), :].astype(BF16)


def gates_of(logits, ids_ref, lanes):
    hot = [ids_ref[:, k : k + 1] == lanes for k in range(2)]
    pair = [jnp.sum(jnp.where(hot[k], logits, 0.0), axis=1, keepdims=True) for k in range(2)]
    top = jnp.maximum(pair[0], pair[1])
    raised = [jnp.exp(p - top) for p in pair]
    total = raised[0] + raised[1]
    return [r / total for r in raised]


def split_rows(row, lines):
    high = row.astype(BF16).astype(F32)
    low = row - high
    both = jnp.concatenate([high, low], axis=1)
    return jnp.where(iota((lines, both.shape[1]), 0) == 0, both, 0.0).astype(BF16)


def post_body(experts, size, x_ref, m0, m1, m2, m3, near_ref, w1, far_ref, w3, norms_ref, row_ref,
              resid_ref, normed_ref, send_ref):
    branch = dot_nn(m0[...], near_ref[...]) + dot_nn(m1[...], w1[...])
    branch = branch + (dot_nn(m2[...], far_ref[...]) + dot_nn(m3[...], w3[...]))
    residual = x_ref[...].astype(F32) + branch
    resid_ref[...] = residual
    normal, _ = norm_parts(residual)
    normed = (normal * norms_ref[2:3, :] + norms_ref[3:4, :]).astype(BF16)
    normed_ref[...] = normed
    if size:
        hits = slot_hits(row_ref[...], experts, 0, size)
        send_ref[...] = dot_nn(hits, normed).astype(BF16).reshape(send_ref.shape)


def gate_body(experts, start, size, normed_ref, router_ref, ids_ref, col_ref, row_ref, gates_ref, send_ref):
    normed = normed_ref[...]
    tokens, width = normed.shape
    logits = dot_nt(normed, router_ref[...])
    gates = gates_of(logits, ids_ref, iota((tokens, experts), 1))
    gates_ref[:, 0:1] = gates[0]
    gates_ref[:, 1:2] = gates[1]
    hits = slot_hits(row_ref[...], experts, start, size)
    send_ref[:, 0:size, :] = dot_nn(hits, normed).astype(BF16).reshape(experts, size, width)
    for e in range(experts):
        codes = iota((tokens, STRIDE), 1) + e * STRIDE
        picked = [jnp.where(col_ref[:, k : k + 1] == codes, gates[k], 0.0) for k in range(2)]
        row = jnp.sum(picked[0] + picked[1], axis=0, keepdims=True)
        send_ref[e, size : size + PAYLOAD, 0 : 2 * STRIDE] = split_rows(row, PAYLOAD)
        send_ref[e, size : size + PAYLOAD, 2 * STRIDE :] = jnp.zeros((PAYLOAD, width - 2 * STRIDE), BF16)


def gelu_pair(values):
    square = values * values
    inner = values * (GELU_A + (GELU_A * GELU_B) * square)
    tanh = jnp.tanh(inner)
    half = 0.5 * tanh + 0.5
    slope = half + 0.5 * values * (1.0 - tanh * tanh) * (GELU_A + (3.0 * GELU_A * GELU_B) * square)
    return values * half, slope


def fetch_grads(here, own, mirror, start, size, target, first, sems):
    side = len(own)
    copies = []
    for j in range(side):
        own_part = own[j].at[pl.ds(start, size)]
        for place, ref in ((here ^ j, own_part), ((here ^ j) ^ side, mirror[j])):
            copies.append(pltpu.make_async_copy(ref, target.at[place, pl.ds(first, size)], sems.at[len(copies)]))
    for copy in copies:
        copy.start()
    return copies


def expert_body(shards, sources, start, size, last, where_ref, x_ref, *refs):
    refs = list(refs)
    side = sources // 2

    def take(count):
        taken = refs[:count]
        del refs[:count]
        return taken

    g_own, g_mirror, weights = take(side), take(side), take(shards)
    carry_ref, prior_ref = take(2) if last and start else (None, None)
    hidden_ref, pre_ref, back_ref, rows_ref = take(4)
    carry_out = None if last else take(1)[0]
    win_v, wout_v, hid_v, pre_v, g_v, in_sems, out_sems, g_sems = refs
    arriving = fetch_grads(where_ref[1], g_own, g_mirror, start, size, g_v, 0, g_sems)
    copies = []
    for r in range(shards):
        pair = (pltpu.make_async_copy(weights[r].at[0], win_v.at[r], in_sems.at[2 * r]),
                pltpu.make_async_copy(weights[r].at[1], wout_v.at[r], in_sems.at[2 * r + 1]))
        for copy in pair:
            copy.start()
        copies.append(pair)
    width = x_ref.shape[2]
    rows = sources * size
    x = x_ref[:, 0:size, :].reshape(rows, width)
    for copy in arriving:
        copy.wait()
    g = g_v[...].reshape(rows, width)
    inner = win_v.shape[2]
    step = 256 if inner % 256 == 0 else inner
    score = jnp.zeros((rows, 1), F32)
    total, result = None, None
    outgoing = []
    for r in range(shards):
        for copy in copies[r]:
            copy.wait()
        for f in range(inner // step):
            cols = slice(f * step, (f + 1) * step)
            hid, slope = gelu_pair(dot_nn(x, win_v[r, :, cols]))
            grad = dot_nn(g, wout_v[r, :, cols])
            hid = hid.astype(BF16)
            score = score + jnp.sum(grad * hid.astype(F32), axis=1, keepdims=True)
            hid_v[r, :, cols] = hid
            pre_v[r, :, cols] = (grad * slope).astype(BF16)
        for source, target in ((hid_v, hidden_ref), (pre_v, pre_ref)):
            copy = pltpu.make_async_copy(source.at[r], target.at[r], out_sems.at[len(outgoing)])
            copy.start()
            outgoing.append(copy)
        part, out = dot_nt(pre_v[r], win_v[r]), dot_nt(hid_v[r], wout_v[r])
        total = part if total is None else total + part
        result = out if result is None else result + out
    back = total.astype(BF16).reshape(sources, size, width)
    result = result.astype(BF16).reshape(sources, size, width)
    eye = iota((size, STRIDE), 1) == iota((size, STRIDE), 0) + start
    if last:
        back_ref[:, 0:size, :] = back
        rows_ref[:, start:, :] = result
        if prior_ref is not None:
            rows_ref[:, 0:start, :] = prior_ref[...]
    else:
        back_ref[...] = back
        rows_ref[...] = result
    for s in range(sources):
        row = jnp.sum(jnp.where(eye, score[s * size : (s + 1) * size], 0.0), axis=0, keepdims=True)
        if last:
            if carry_ref is not None:
                row = row + carry_ref[s : s + 1, :]
            back_ref[s, size : size + PAYLOAD, 0 : 2 * STRIDE] = split_rows(row, PAYLOAD)
            back_ref[s, size : size + PAYLOAD, 2 * STRIDE :] = jnp.zeros((PAYLOAD, width - 2 * STRIDE), BF16)
        else:
            carry_out[s : s + 1, :] = row
    for copy in outgoing:
        copy.wait()


def expert_grad_body(picks, shards, sources, sizes, where_ref, *refs):
    refs = list(refs)
    count = len(sizes)

    def take(number):
        taken = refs[:number]
        del refs[:number]
        return taken

    side = sources // 2
    x_refs, g_own, g_mirror = take(count), take(side), [take(side) for _ in range(count)]
    hidden, pre = take(count), take(count)
    home_ref, send_ref = take(2)
    xt, gt, hid_v, pre_v, out_v, g_v, in_sems, out_sems, g_sems = refs
    arriving = []
    for index, size in enumerate(sizes):
        first = sum(sizes[:index])
        arriving += fetch_grads(where_ref[1], g_own, g_mirror[index], first, size, g_v, first, g_sems.at[index])
    copies = []
    for place, r in enumerate(picks):
        base = 0
        group = []
        for index, size in enumerate(sizes):
            rows = sources * size
            for which, (source, target) in enumerate(((pre[index], pre_v), (hidden[index], hid_v))):
                copy = pltpu.make_async_copy(source.at[r], target.at[place, pl.ds(base, rows)],
                                             in_sems.at[(place * count + index) * 2 + which])
                group.append(copy)
            base += rows
        copies.append(group)
    for copy in copies[0]:
        copy.start()
    width = x_refs[0].shape[2]
    last = x_refs[-1]
    for copy in arriving:
        copy.wait()
    start, base = 0, 0
    for ref, size in zip(x_refs, sizes):
        rows = sources * size
        eye = iota((size, STRIDE), 1) == iota((size, STRIDE), 0) + start
        gate = []
        for s in range(sources):
            row = last[s, sizes[-1] : sizes[-1] + PAYLOAD, :].astype(F32)
            row = row[0:1, 0:STRIDE] + row[0:1, STRIDE : 2 * STRIDE]
            gate.append(jnp.sum(jnp.where(eye, row, 0.0), axis=1, keepdims=True))
        gate = jnp.concatenate(gate, axis=0)
        x = ref[:, 0:size, :].reshape(rows, width).astype(F32) * gate
        g = g_v[:, start : start + size, :].reshape(rows, width).astype(F32) * gate
        xt[:, base : base + rows] = x.T.astype(BF16)
        gt[:, base : base + rows] = g.T.astype(BF16)
        start += size
        base += rows
    outgoing = []
    for place, r in enumerate(picks):
        for copy in copies[place]:
            copy.wait()
        for copy in copies[place + 1] if place + 1 < len(picks) else ():
            copy.start()
        for which, (left, right) in enumerate(((xt, pre_v), (gt, hid_v))):
            out_v[place, which] = dot_nn(left[...], right[place]).astype(BF16)
            target = (send_ref if r % 2 else home_ref).at[r // 2, which]
            copy = pltpu.make_async_copy(out_v.at[place, which], target, out_sems.at[2 * place + which])
            copy.start()
            outgoing.append(copy)
    for copy in outgoing:
        copy.wait()


def grad_sum_body(keep_ref, home_ref, got_ref, passed_ref, *out_refs):
    for index, ref in enumerate(out_refs):
        total = home_ref[0, index].astype(F32) + got_ref[0, index].astype(F32)
        ref[...] = (total + passed_ref[index].astype(F32)) * keep_ref[0, 0]


def gather_body(rows_ref, codes_ref, col_ref, gates_ref, sum_ref):
    sources, size, width = rows_ref.shape
    codes = codes_ref[...]
    pick = jnp.where(col_ref[:, 0:1] == codes, gates_ref[:, 0:1], 0.0)
    pick = jnp.where(col_ref[:, 1:2] == codes, gates_ref[:, 1:2], pick).astype(BF16)
    sum_ref[...] = dot_nn(pick, rows_ref[...].reshape(sources * size, width))


def second_back_body(experts, size, has_sum, *refs):
    refs = list(refs)
    (rows_ref, codes_ref, col_ref, gates_ref, ids_ref, resid_ref, normed_ref, cot_ref, norms_ref, router_ref) = refs[:10]
    del refs[:10]
    sum_ref = refs.pop(0) if has_sum else None
    grad_ref, branch_ref, small_ref = refs
    sources, _, width = rows_ref.shape
    tokens = resid_ref.shape[0]
    codes = codes_ref[...]
    gates = [gates_ref[:, k : k + 1] for k in range(2)]
    slot = [col_ref[:, k : k + 1] for k in range(2)]
    pick = jnp.where(slot[0] == codes, gates[0], 0.0)
    pick = jnp.where(slot[1] == codes, gates[1], pick).astype(BF16)
    total = dot_nn(pick, rows_ref[:, 0:size, :].reshape(sources * size, width))
    if sum_ref is not None:
        total = total + sum_ref[...]
    scores = [jnp.zeros((tokens, 1), F32), jnp.zeros((tokens, 1), F32)]
    for e in range(experts):
        line = rows_ref[e, size : size + PAYLOAD, :].astype(F32)
        line = line[0:1, 0:STRIDE] + line[0:1, STRIDE : 2 * STRIDE]
        place = iota((tokens, STRIDE), 1) + e * STRIDE
        for k in range(2):
            scores[k] = scores[k] + jnp.sum(jnp.where(slot[k] == place, line, 0.0), axis=1, keepdims=True)
    inner = gates[0] * scores[0] + gates[1] * scores[1]
    lanes = iota((tokens, experts), 1)
    logit_grad = jnp.zeros((tokens, experts), F32)
    for k in range(2):
        logit_grad = jnp.where(ids_ref[:, k : k + 1] == lanes, gates[k] * (scores[k] - inner), logit_grad)
    logit_grad = logit_grad.astype(BF16)
    total = total + dot_nn(logit_grad, router_ref[...])
    normal, rate = norm_parts(resid_ref[...])
    grad = cot_ref[...].astype(F32) + norm_back(normal, rate, norms_ref[2:3, :], total)
    grad_ref[...] = grad
    branch_ref[...] = grad.astype(BF16)
    small_ref[0:1, :] = jnp.sum(total * normal, axis=0, keepdims=True)
    small_ref[1:2, :] = jnp.sum(total, axis=0, keepdims=True)
    small_ref[2 : 2 + experts, :] = dot_tn(logit_grad, normed_ref[...])


def attend_back_body(half, has_sum, where_ref, *refs):
    refs = list(refs)
    (q_ref, k_ref, v_ref, log_ref, mixed_own, mixed_other, branch_own, branch_other, own_ref, other_ref,
     w_ref) = refs[:11]
    del refs[:11]
    sums = (refs.pop(0), refs.pop(0)) if has_sum else None
    weight_ref, mine_ref, theirs_ref, rows, branch, grads, mixed, keys, vals, dq, dk, dv, joined, pile = refs
    core = where_ref[0]
    mine = pl.multiple_of(core * half, half)
    theirs = pl.multiple_of((1 - core) * half, half)
    rows[pl.ds(mine, half), :] = own_ref[...]
    rows[pl.ds(theirs, half), :] = other_ref[...]
    branch[pl.ds(mine, half), :] = branch_own[...]
    branch[pl.ds(theirs, half), :] = branch_other[...]
    mixed[pl.ds(mine, half), :] = mixed_own[...]
    mixed[pl.ds(theirs, half), :] = mixed_other[...]
    length, width = q_ref.shape
    grads[...] = dot_nt(branch[...], w_ref[3 * width :, :]).astype(BF16)
    heads = width // HD
    lane = iota((1, width), 1)
    triangle = iota((QUERY_ROWS, QUERY_ROWS), 0) >= iota((QUERY_ROWS, QUERY_ROWS), 1)
    qt = q_ref[...].astype(F32).T.astype(BF16)
    gt = grads[...].astype(F32).T.astype(BF16)
    dk[...] = jnp.zeros(dk.shape, F32)
    dv[...] = jnp.zeros(dv.shape, F32)
    for h in range(heads):
        keep = (lane >= h * HD) & (lane < (h + 1) * HD)
        keys[...] = jnp.where(keep, k_ref[...], 0)
        vals[...] = jnp.where(keep, v_ref[...], 0)
        head = slice(h * HD, (h + 1) * HD)
        for block in range(length // QUERY_ROWS):
            low = block * QUERY_ROWS
            here = slice(low, low + QUERY_ROWS)
            query, grad, log = q_ref[here, :], grads[here, :], log_ref[here, h : h + 1]
            spans = [slice(0, low)] if block else []
            spans.append(here)
            probs, outer = [], []
            inner = None
            for span in spans:
                score = dot_nt(query, keys[span, :])
                if span is here:
                    score = jnp.where(triangle, score, MASKED_SCORE)
                prob = jnp.exp(score - log)
                grad_prob = dot_nt(grad, vals[span, :])
                part = jnp.sum(prob * grad_prob, axis=1, keepdims=True)
                inner = part if inner is None else inner + part
                probs.append(prob)
                outer.append(grad_prob)
            query_grad = None
            for span, prob, grad_prob in zip(spans, probs, outer):
                score_grad = (prob * (grad_prob - inner)).astype(BF16)
                part = dot_nn(score_grad, keys[span, :])
                query_grad = part if query_grad is None else query_grad + part
                dv[head, span] = dv[head, span] + dot_nn(gt[head, here], prob.astype(BF16))
                dk[head, span] = dk[head, span] + dot_nn(qt[head, here], score_grad)
            if h:
                query_grad = query_grad + dq[here, :]
            dq[here, :] = query_grad
    query_grads = dq[...].astype(BF16).astype(F32) * HD ** (-0.5)
    joined[0:width, :] = query_grads.T.astype(BF16)
    joined[width : 2 * width, :] = dk[...].astype(BF16)
    joined[2 * width : 3 * width, :] = dv[...].astype(BF16)
    total = dot_nn(query_grads.astype(BF16), w_ref[0:width, :])
    total = total + dot_nn(dk[...].T.astype(BF16), w_ref[width : 2 * width, :])
    total = total + dot_nn(dv[...].T.astype(BF16), w_ref[2 * width : 3 * width, :])
    pile[...] = total
    one, two = pile[pl.ds(mine, half), :], pile[pl.ds(theirs, half), :]
    if sums is not None:
        one, two = one + sums[0][...], two + sums[1][...]
    mine_ref[...] = one.astype(mine_ref.dtype)
    theirs_ref[...] = two.astype(theirs_ref.dtype)
    weight_ref[0 : 3 * width, :] = dot_nn(joined[...], rows[...]).astype(weight_ref.dtype)
    turned = mixed[...].astype(F32).T.astype(BF16)
    weight_ref[3 * width :, :] = dot_nn(turned, branch[...]).astype(weight_ref.dtype)


def first_back_body(x_ref, norms_ref, mine_ref, other_ref, resid_ref, out_ref, small_ref):
    grad = mine_ref[...] + other_ref[...].astype(F32)
    normal, rate = norm_parts(x_ref[...].astype(F32))
    out_ref[...] = resid_ref[...] + norm_back(normal, rate, norms_ref[0:1, :], grad)
    small_ref[0:1, :] = jnp.sum(grad * normal, axis=0, keepdims=True)
    small_ref[1:2, :] = jnp.sum(grad, axis=0, keepdims=True)


def block_out_body(rows_ref, codes_ref, col_ref, gates_ref, resid_ref, out_ref):
    sources, size, width = rows_ref.shape
    codes = codes_ref[...]
    pick = jnp.where(col_ref[:, 0:1] == codes, gates_ref[:, 0:1], 0.0)
    pick = jnp.where(col_ref[:, 1:2] == codes, gates_ref[:, 1:2], pick).astype(BF16)
    moe = dot_nn(pick, rows_ref[...].reshape(sources * size, width))
    out_ref[...] = (resid_ref[...] + moe).astype(BF16)


def final_body(all_ref, *out_refs):
    rows = out_refs[0].shape[0]
    for index, ref in enumerate(out_refs):
        ref[...] = all_ref[index * rows : (index + 1) * rows, :].astype(F32)


def swap(value, axis, step):
    size = lax.axis_size(axis)
    return lax.ppermute(value, axis, [(i, i ^ step) for i in range(size)])


def exchange(value):
    return lax.all_to_all(value, "dp", split_axis=0, concat_axis=0, tiled=True)


def after(value, *others):
    return lax.optimization_barrier((value,) + others)[0]


def codes_of(experts, start, size):
    table = np.arange(experts)[:, None] * STRIDE + start + np.arange(size)[None, :]
    return jnp.asarray(table.reshape(1, -1).astype(np.int32))


def per_device(activations, first_gain, first_shift, query_weight, key_weight, value_weight, output_weight,
               second_gain, second_shift, router_weight, expert_in, expert_out, expert_ids, capacity, new_mask,
               cotangent):
    kernel = functools.partial(call, pins=[activations, output_weight, cotangent])
    tokens, width = activations.shape
    local = query_weight.shape[1]
    heads = local // HD
    experts = router_weight.shape[1]
    sources = lax.axis_size("dp")
    shards = lax.axis_size("head")
    slots = 3 * tokens // experts
    sizes = (slots // 32 * 16, slots - slots // 32 * 16) if slots % 16 == 0 and slots >= 32 else (slots,)
    starts = tuple(sum(sizes[:i]) for i in range(len(sizes)))
    length, half, side = LENGTH, tokens, sources // 2
    where = jnp.stack([lax.axis_index("head") % 2, lax.axis_index("dp")]).astype(jnp.int32)
    last_rows = pl.BlockSpec((local, width), lambda i: (3, 0))

    attn_w = jnp.concatenate([query_weight.T, key_weight.T, value_weight.T, output_weight], axis=0)
    far_w = swap(attn_w, "head", 2)
    norms = jnp.stack([first_gain, first_shift, second_gain, second_shift])
    router = router_weight.T

    normed_first = kernel(first_norm_body, [sds((tokens, width), BF16)], "norm_first", (activations, norms), vmem=16)[0]
    normed_other = swap(normed_first, "head", 1)

    ids_row = expert_ids.T
    extra = jnp.pad(ids_row.astype(BF16), ((0, PAYLOAD - 2), (0, width - tokens)))
    mirror_grad = swap(jnp.concatenate([cotangent, extra], axis=0), "dp", side)
    routed = kernel(
        functools.partial(route_body, slots),
        [sds((tokens, 2), jnp.int32), sds((tokens, 2), jnp.int32), sds((2, tokens), jnp.int32)]
        + [sds((slots, width), BF16)] * side,
        "route", (where, ids_row, capacity, cotangent), smem=(0, 2))
    ids_col, slot_col, slot_row = routed[:3]
    grad_own = [routed[3]] + [swap(routed[3 + j], "dp", j) for j in range(1, side)]

    def attend(weight):
        return kernel(
            functools.partial(attend_body, half),
            [sds((length, local), BF16)] * 3 + [sds((length, heads), F32)] + [sds((half, local), BF16)] * 2,
            "attend", (where, normed_first, normed_other, weight), smem=(0,),
            scratch=[pltpu.VMEM((length, width), BF16), pltpu.VMEM((length, local), F32),
                     pltpu.VMEM((length, local), BF16), pltpu.VMEM((length, local), BF16)])

    near = attend(attn_w)
    mixed = {0: near[4], 1: swap(near[5], "head", 1)}
    far_w = after(far_w, near[4], slot_row)
    away = attend(far_w)
    mixed[2], mixed[3] = away[4], swap(away[5], "head", 1)
    out_w = {1: swap(output_weight, "head", 1), 3: swap(far_w[3 * local :], "head", 1)}

    weights = {0: jnp.stack([expert_in[0], expert_out[0]])}
    weights[1] = swap(weights[0], "head", 1)
    weights[2] = swap(after(weights[0], far_w), "head", 2)
    weights[3] = swap(weights[2], "head", 1)
    inner = weights[0].shape[2]

    mirror_send = kernel(
        functools.partial(mirror_body, slots, len(sizes)),
        [sds((size, width), BF16) for size in sizes for _ in range(side)], "mirror",
        (where, capacity, mirror_grad), smem=(0, 1))
    grad_mirror = []
    for index in range(len(sizes)):
        group = mirror_send[index * side : (index + 1) * side]
        grad_mirror.append([group[0]] + [swap(group[j], "dp", j) for j in range(1, side)])

    first_size = sizes[0] if len(sizes) > 1 else 0
    residual, normed_second, sent = kernel(
        functools.partial(post_body, experts, first_size),
        [sds((tokens, width), F32), sds((tokens, width), BF16), sds((experts, max(first_size, 16), width), BF16)],
        "post_attend",
        (activations, mixed[0], mixed[1], mixed[2], mixed[3], output_weight, out_w[1], far_w, out_w[3], norms,
         after(slot_row, mirror_send[0], *grad_own[1:])), blocks={7: last_rows}, vmem=32)
    gates, sent_last = kernel(
        functools.partial(gate_body, experts, starts[-1], sizes[-1]),
        [sds((tokens, 2), F32), sds((experts, sizes[-1] + PAYLOAD, width), BF16)],
        "gates", (normed_second, router, ids_col, slot_col, slot_row))
    rows_in = []
    if first_size:
        rows_in.append(exchange(sent))
    sent_last = after(sent_last, weights[2], *(rows_in + grad_mirror[0][1:]))
    rows_in.append(exchange(sent_last))

    hidden, pre, back = [], [], []
    carry = ()
    for index, size in enumerate(sizes):
        last = index == len(sizes) - 1
        rows = sources * size
        kept = slots if last else size
        outs = [sds((shards, rows, inner), BF16), sds((shards, rows, inner), BF16),
                sds((sources, size + (PAYLOAD if last else 0), width), BF16), sds((sources, kept, width), BF16)]
        ins = (where, rows_in[index]) + tuple(grad_own) + tuple(grad_mirror[index])
        first = len(ins)
        ins = ins + tuple(weights[r] for r in range(shards)) + carry
        if not last:
            outs.append(sds((sources, STRIDE), F32))
        result = kernel(
            functools.partial(expert_body, shards, sources, starts[index], size, last), outs, "expert", ins,
            vmem=60 if rows <= 768 else 62, smem=(0,), hbm=tuple(range(2, first + shards)), free=(2,),
            out_hbm=(0, 1),
            scratch=[pltpu.VMEM((shards, width, inner), BF16), pltpu.VMEM((shards, width, inner), BF16),
                     pltpu.VMEM((shards, rows, inner), BF16), pltpu.VMEM((shards, rows, inner), BF16),
                     pltpu.VMEM((sources, size, width), BF16), pltpu.SemaphoreType.DMA((2 * shards,)),
                     pltpu.SemaphoreType.DMA((2 * shards,)), pltpu.SemaphoreType.DMA((sources,))])
        hidden.append(result[0])
        pre.append(result[1])
        back.append(result[2])
        expert_rows = result[3]
        if not last:
            carry = (result[4], result[3])
    returned, done = [], rows_in[-1]
    for index, part in enumerate(back):
        done = exchange(after(part, done, *(grad_mirror[-1][1:] if index == 0 else ())))
        returned.append(done)

    keep = jnp.sum(jnp.where(jnp.arange(experts) == lax.axis_index("dp"), new_mask, 0)).astype(F32).reshape(1, 1)
    all_rows = sources * slots
    picks = tuple(range(1, shards, 2)) + tuple(range(0, shards, 2))
    skip = 1 + len(sizes)
    grads_home, grads_send = kernel(
        functools.partial(expert_grad_body, picks, shards, sources, sizes),
        [sds((shards // 2, 2, width, inner), BF16)] * 2, "expert_grads",
        (where,) + tuple(rows_in) + tuple(grad_own) + sum(map(tuple, grad_mirror), ()) + tuple(hidden) + tuple(pre), vmem=60,
        smem=(0,), hbm=tuple(range(skip, skip + side * (1 + len(sizes)) + 2 * len(sizes))), out_hbm=(0, 1),
        scratch=[pltpu.VMEM((width, all_rows), BF16), pltpu.VMEM((width, all_rows), BF16),
                 pltpu.VMEM((shards, all_rows, inner), BF16), pltpu.VMEM((shards, all_rows, inner), BF16),
                 pltpu.VMEM((shards, 2, width, inner), BF16), pltpu.VMEM((sources, slots, width), BF16),
                 pltpu.SemaphoreType.DMA((4 * shards,)), pltpu.SemaphoreType.DMA((2 * shards,)),
                 pltpu.SemaphoreType.DMA((len(sizes), sources))])
    grads_got = swap(grads_send, "head", 1)

    partial_sums = ()
    if first_size:
        partial_sums = tuple(kernel(
            gather_body, [sds((tokens, width), F32)], "gather_back",
            (returned[0], codes_of(experts, 0, first_size), slot_col, gates)))
    grad_residual, grad_branch, small_two = kernel(
        functools.partial(second_back_body, experts, sizes[-1], bool(partial_sums)),
        [sds((tokens, width), F32), sds((tokens, width), BF16), sds((2 + experts, width), F32)], "second_back",
        (returned[-1], codes_of(experts, starts[-1], sizes[-1]), slot_col, gates, ids_col, residual,
         normed_second, cotangent, norms, router) + partial_sums, free=(1, 2))
    branch_other = swap(grad_branch, "head", 1)

    def attend_back(parts, mixed_other, weight, sums, weight_type, types):
        return kernel(
            functools.partial(attend_back_body, half, bool(sums)),
            [sds((4 * local, width), weight_type), sds((half, width), types[0]), sds((half, width), types[1])],
            "attend_back",
            (where,) + tuple(parts[:4]) + (parts[4], parts[5], grad_branch, branch_other, normed_first, normed_other,
                                           weight) + tuple(sums),
            smem=(0,), vmem=32, free=(0, 1, 2),
            scratch=[pltpu.VMEM((length, width), BF16), pltpu.VMEM((length, width), BF16),
                     pltpu.VMEM((length, local), BF16), pltpu.VMEM((length, local), BF16),
                     pltpu.VMEM((length, local), BF16), pltpu.VMEM((length, local), BF16),
                     pltpu.VMEM((length, local), F32), pltpu.VMEM((local, length), F32),
                     pltpu.VMEM((local, length), F32), pltpu.VMEM((3 * local, length), BF16),
                     pltpu.VMEM((length, width), F32)])

    far_grad, far_mine, far_theirs = attend_back(away, mixed[3], far_w, (), BF16, (F32, F32))
    far_got = swap(far_grad, "head", 2)
    near_grad, near_mine, near_theirs = attend_back(near, mixed[1], attn_w, (far_mine, far_theirs), F32, (F32, BF16))
    first_got = swap(near_theirs, "head", 1)
    grad_input, small_one = kernel(
        first_back_body, [sds((tokens, width), F32), sds((2, width), F32)], "first_back",
        (activations, norms, near_mine, first_got, grad_residual))

    rows_back = exchange(after(expert_rows, returned[-1], grads_home, *partial_sums))
    block_out = kernel(
        block_out_body, [sds((tokens, width), BF16)], "block_out",
        (rows_back, codes_of(experts, 0, slots), slot_col, gates, residual))[0]

    passed = (grads_home[1].astype(F32) + grads_got[1].astype(F32)).astype(BF16)
    joined = after((near_grad + far_got.astype(F32)).astype(BF16), rows_back, passed)
    passed = swap(after(passed, far_got), "head", 2)
    scattered = exchange(joined.reshape(sources, 4 * local // sources, width))
    reduced = jnp.sum(scattered.astype(F32), axis=0).astype(BF16)
    small = jnp.concatenate([small_one, small_two], axis=0)
    small = jnp.pad(small, ((0, -small.shape[0] % 8), (0, 0)))
    small = small + swap(small, "head", 1)
    step = 1
    while step < sources:
        small = small + swap(small if step == 1 else after(small, block_out), "dp", step)
        step *= 2
    reduced = after(reduced, small)
    gathered = exchange(jnp.broadcast_to(reduced[None], (sources,) + reduced.shape))

    part = pl.BlockSpec((1, 2, width, inner), lambda i: (0, 0, 0, 0))
    grad_in, grad_out = kernel(
        grad_sum_body, [sds((width, inner), F32), sds((width, inner), F32)], "grad_sum",
        (keep, grads_home, grads_got, passed), smem=(0,), vmem=40, blocks={1: part, 2: part})

    small = small + swap(small, "head", 2)
    gathered = after(gathered.reshape(4 * local, width), grad_in)
    final = kernel(final_body, [sds((local, width), F32)] * 4, "final", (gathered,))
    mask = new_mask.astype(F32)[None, :]
    return (
        block_out,
        grad_input,
        small[0],
        small[1],
        final[0].T,
        final[1].T,
        final[2].T,
        final[3],
        small[2],
        small[3],
        small[4 : 4 + experts].T * mask,
        grad_in[None],
        grad_out[None],
    )


def solution(mesh):
    placed = (
        P(("dp", "head"), None),
        P(),
        P(),
        P(None, "head"),
        P(None, "head"),
        P(None, "head"),
        P("head", None),
        P(),
        P(),
        P(),
        P("dp", None, "head"),
        P("dp", None, "head"),
        P(("dp", "head"), None),
        P(),
        P(),
        P(("dp", "head"), None),
    )
    return jax.shard_map(
        per_device,
        mesh=mesh,
        in_specs=placed,
        out_specs=(
            P(("dp", "head"), None),
            P(("dp", "head"), None),
            P(),
            P(),
            P(None, "head"),
            P(None, "head"),
            P(None, "head"),
            P("head", None),
            P(),
            P(),
            P(),
            P("dp", None, "head"),
            P("dp", None, "head"),
        ),
        check_vma=False,
    )
```

```python
import functools

import jax
import jax.numpy as jnp
import numpy as np
from jax import lax
from jax.experimental import pallas as pl
from jax.experimental.pallas import tpu as pltpu
from jax.sharding import PartitionSpec as P

HD = 64
LENGTH = 1024
NORM_EPSILON = 1e-05
MASKED_SCORE = -1e30
QUERY_ROWS = 256
STRIDE = 256
PAYLOAD = 8
MIB = 1 << 20
F32 = jnp.float32
BF16 = jnp.bfloat16
GELU_A = 0.7978845608028654
GELU_B = 0.044715


def dot_nn(left, right):
    return lax.dot_general(left, right, (((1,), (0,)), ((), ())), preferred_element_type=F32)


def dot_nt(left, right):
    return lax.dot_general(left, right, (((1,), (1,)), ((), ())), preferred_element_type=F32)


def dot_tn(left, right):
    return lax.dot_general(left, right, (((0,), (0,)), ((), ())), preferred_element_type=F32)


def iota(shape, axis):
    return lax.broadcasted_iota(jnp.int32, shape, axis)


def call(body, outs, name, ins, vmem=24, scratch=(), smem=(), hbm=(), free=(), out_hbm=(), pins=None, blocks=None):
    specs, given = [], []
    blocks = blocks or {}
    for index, value in enumerate(ins):
        if index in smem:
            specs.append(pl.BlockSpec(memory_space=pltpu.SMEM))
        elif index in hbm:
            specs.append(pl.BlockSpec(memory_space=pltpu.HBM))
        elif index in blocks:
            specs.append(blocks[index])
        else:
            specs.append(pl.BlockSpec())
        if index not in smem and any(value is p for p in pins):
            value = pltpu.with_memory_space_constraint(value, pltpu.HBM)
        given.append(value)
    results = pl.pallas_call(
        body,
        grid=(1,) if blocks else (),
        out_shape=[o if i in free else pltpu.HBM(o.shape, o.dtype) for i, o in enumerate(outs)],
        in_specs=specs,
        out_specs=[pl.BlockSpec(memory_space=pltpu.HBM) if i in out_hbm else pl.BlockSpec() for i in range(len(outs))],
        scratch_shapes=list(scratch),
        compiler_params=pltpu.CompilerParams(vmem_limit_bytes=vmem * MIB),
        cost_estimate=pl.CostEstimate(flops=1, bytes_accessed=1, transcendentals=0),
        name=name,
    )(*given)
    pins.extend(r for i, r in enumerate(results) if i not in free)
    return results


def sds(shape, dtype):
    return jax.ShapeDtypeStruct(shape, dtype)


def norm_parts(values):
    center = jnp.mean(values, axis=1, keepdims=True)
    centered = values - center
    rate = lax.rsqrt(jnp.mean(centered * centered, axis=1, keepdims=True) + NORM_EPSILON)
    return centered * rate, rate


def norm_back(normal, rate, gain, grad):
    scaled = grad * gain
    first = jnp.mean(scaled, axis=1, keepdims=True)
    second = jnp.mean(scaled * normal, axis=1, keepdims=True)
    return rate * (scaled - first - normal * second)


def first_norm_body(x_ref, norms_ref, out_ref):
    normal, _ = norm_parts(x_ref[...].astype(F32))
    out_ref[...] = (normal * norms_ref[0:1, :] + norms_ref[1:2, :]).astype(BF16)


def slot_hits(slot_row, experts, start, count):
    tokens = slot_row.shape[1]
    parts = []
    for e in range(experts):
        codes = iota((count, tokens), 0) + (e * STRIDE + start)
        hit = (slot_row[0:1] == codes) | (slot_row[1:2] == codes)
        parts.append(jnp.where(hit, 1.0, 0.0))
    return jnp.concatenate(parts, axis=0).astype(BF16)


def slots_of(ids, cap_ref):
    tokens = ids.shape[1]
    experts = cap_ref.shape[0]
    upper = jnp.where(iota((tokens, tokens), 0) < iota((tokens, tokens), 1), 1.0, 0.0).astype(BF16)
    rows_e = iota((experts, tokens), 0)
    hot = [jnp.where(ids[k : k + 1] == rows_e, 1.0, 0.0) for k in range(2)]
    earlier = dot_nn((hot[0] + hot[1]).astype(BF16), upper)
    column = iota((experts, 1), 0)
    limit = jnp.zeros((experts, 1), jnp.int32)
    for e in range(experts):
        limit = jnp.where(column == e, cap_ref[e], limit)
    limit = limit.astype(F32)
    rows = []
    for k in range(2):
        place = jnp.sum(hot[k] * earlier, axis=0, keepdims=True)
        top = jnp.sum(hot[k] * limit, axis=0, keepdims=True)
        rows.append(jnp.where(place < top, ids[k : k + 1] * STRIDE + place.astype(jnp.int32), -1))
    return jnp.concatenate(rows, axis=0)


def block_hits(slot_row, block, count):
    codes = iota((count, slot_row.shape[1]), 0) + block * STRIDE
    return jnp.where((slot_row[0:1] == codes) | (slot_row[1:2] == codes), 1.0, 0.0).astype(BF16)


def sort_rows(slots, here, slot_row, rows, send_refs):
    hits = [block_hits(slot_row, here ^ j, slots) for j in range(len(send_refs))]
    sent = dot_nn(jnp.concatenate(hits, axis=0), rows).astype(BF16)
    for j, refs in enumerate(send_refs):
        start = j * slots
        for ref in refs:
            ref[...] = sent[start : start + ref.shape[0]]
            start += ref.shape[0]


def route_body(slots, where_ref, ids_row_ref, cap_ref, grad_ref, ids_ref, col_ref, row_ref, *send_refs):
    ids = ids_row_ref[...]
    slot_row = slots_of(ids, cap_ref)
    row_ref[...] = slot_row
    col_ref[...] = slot_row.astype(F32).T.astype(jnp.int32)
    ids_ref[...] = ids.astype(F32).T.astype(jnp.int32)
    sort_rows(slots, where_ref[1], slot_row, grad_ref[...], [[ref] for ref in send_refs])


def mirror_body(slots, parts, where_ref, cap_ref, grad_ref, *send_refs):
    tokens = grad_ref.shape[0] - PAYLOAD
    ids = grad_ref[tokens:, 0:tokens].astype(F32)[0:2].astype(jnp.int32)
    side = len(send_refs) // parts
    groups = [send_refs[j::side] for j in range(side)]
    sort_rows(slots, where_ref[1], slots_of(ids, cap_ref), grad_ref[0:tokens, :], groups)


def attend_body(half, where_ref, own_ref, other_ref, w_ref,
                q_ref, k_ref, v_ref, log_ref, mine_ref, theirs_ref, rows, mixed, keys, vals):
    core = where_ref[0]
    mine = pl.multiple_of(core * half, half)
    theirs = pl.multiple_of((1 - core) * half, half)
    rows[pl.ds(mine, half), :] = own_ref[...]
    rows[pl.ds(theirs, half), :] = other_ref[...]
    length, width = q_ref.shape
    for part in range(2):
        block = slice(part * half, (part + 1) * half)
        source = rows[block, :]
        q_ref[block, :] = (dot_nt(source, w_ref[0:width, :]) * HD ** (-0.5)).astype(BF16)
        k_ref[block, :] = dot_nt(source, w_ref[width : 2 * width, :]).astype(BF16)
        v_ref[block, :] = dot_nt(source, w_ref[2 * width : 3 * width, :]).astype(BF16)
    heads = width // HD
    lane = iota((1, width), 1)
    triangle = iota((QUERY_ROWS, QUERY_ROWS), 0) >= iota((QUERY_ROWS, QUERY_ROWS), 1)
    for h in range(heads):
        keep = (lane >= h * HD) & (lane < (h + 1) * HD)
        keys[...] = jnp.where(keep, k_ref[...], 0)
        vals[...] = jnp.where(keep, v_ref[...], 0)
        for block in range(length // QUERY_ROWS):
            low = block * QUERY_ROWS
            here = slice(low, low + QUERY_ROWS)
            query = q_ref[here, :]
            diag = jnp.where(triangle, dot_nt(query, keys[here, :]), MASKED_SCORE)
            top = jnp.max(diag, axis=1, keepdims=True)
            if block:
                wide = dot_nt(query, keys[0:low, :])
                top = jnp.maximum(top, jnp.max(wide, axis=1, keepdims=True))
            diag = jnp.exp(diag - top)
            total = jnp.sum(diag, axis=1, keepdims=True)
            result = dot_nn(diag.astype(BF16), vals[here, :])
            if block:
                wide = jnp.exp(wide - top)
                total = total + jnp.sum(wide, axis=1, keepdims=True)
                result = result + dot_nn(wide.astype(BF16), vals[0:low, :])
            result = result / total
            log_ref[here, h : h + 1] = top + jnp.log(total)
            if h:
                result = result + mixed[here, :]
            mixed[here, :] = result
    mine_ref[...] = mixed[pl.ds(mine, half), :].astype(BF16)
    theirs_ref[...] = mixed[pl.ds(theirs, half), :].astype(BF16)


def gates_of(logits, ids_ref, lanes):
    hot = [ids_ref[:, k : k + 1] == lanes for k in range(2)]
    pair = [jnp.sum(jnp.where(hot[k], logits, 0.0), axis=1, keepdims=True) for k in range(2)]
    top = jnp.maximum(pair[0], pair[1])
    raised = [jnp.exp(p - top) for p in pair]
    total = raised[0] + raised[1]
    return [r / total for r in raised]


def split_rows(row, lines):
    high = row.astype(BF16).astype(F32)
    low = row - high
    both = jnp.concatenate([high, low], axis=1)
    return jnp.where(iota((lines, both.shape[1]), 0) == 0, both, 0.0).astype(BF16)


def post_body(experts, size, x_ref, m0, m1, m2, m3, near_ref, w1, far_ref, w3, norms_ref, row_ref,
              resid_ref, normed_ref, send_ref):
    branch = dot_nn(m0[...], near_ref[...]) + dot_nn(m1[...], w1[...])
    branch = branch + (dot_nn(m2[...], far_ref[...]) + dot_nn(m3[...], w3[...]))
    residual = x_ref[...].astype(F32) + branch
    resid_ref[...] = residual
    normal, _ = norm_parts(residual)
    normed = (normal * norms_ref[2:3, :] + norms_ref[3:4, :]).astype(BF16)
    normed_ref[...] = normed
    if size:
        hits = slot_hits(row_ref[...], experts, 0, size)
        send_ref[...] = dot_nn(hits, normed).astype(BF16).reshape(send_ref.shape)


def gate_body(experts, start, size, normed_ref, router_ref, ids_ref, col_ref, row_ref, gates_ref, send_ref):
    normed = normed_ref[...]
    tokens, width = normed.shape
    logits = dot_nt(normed, router_ref[...])
    gates = gates_of(logits, ids_ref, iota((tokens, experts), 1))
    gates_ref[:, 0:1] = gates[0]
    gates_ref[:, 1:2] = gates[1]
    hits = slot_hits(row_ref[...], experts, start, size)
    send_ref[:, 0:size, :] = dot_nn(hits, normed).astype(BF16).reshape(experts, size, width)
    for e in range(experts):
        codes = iota((tokens, STRIDE), 1) + e * STRIDE
        picked = [jnp.where(col_ref[:, k : k + 1] == codes, gates[k], 0.0) for k in range(2)]
        row = jnp.sum(picked[0] + picked[1], axis=0, keepdims=True)
        send_ref[e, size : size + PAYLOAD, 0 : 2 * STRIDE] = split_rows(row, PAYLOAD)
        send_ref[e, size : size + PAYLOAD, 2 * STRIDE :] = jnp.zeros((PAYLOAD, width - 2 * STRIDE), BF16)


def gelu_pair(values):
    square = values * values
    inner = values * (GELU_A + (GELU_A * GELU_B) * square)
    tanh = jnp.tanh(inner)
    half = 0.5 * tanh + 0.5
    slope = half + 0.5 * values * (1.0 - tanh * tanh) * (GELU_A + (3.0 * GELU_A * GELU_B) * square)
    return values * half, slope


def fetch_grads(here, own, mirror, start, size, target, first, sems):
    side = len(own)
    copies = []
    for j in range(side):
        own_part = own[j].at[pl.ds(start, size)]
        for place, ref in ((here ^ j, own_part), ((here ^ j) ^ side, mirror[j])):
            copies.append(pltpu.make_async_copy(ref, target.at[place, pl.ds(first, size)], sems.at[len(copies)]))
    for copy in copies:
        copy.start()
    return copies


def expert_body(shards, sources, start, size, last, where_ref, x_ref, *refs):
    refs = list(refs)
    side = sources // 2

    def take(count):
        taken = refs[:count]
        del refs[:count]
        return taken

    g_own, g_mirror, weights = take(side), take(side), take(shards)
    carry_ref, prior_ref = take(2) if last and start else (None, None)
    hidden_ref, pre_ref, back_ref, rows_ref = take(4)
    carry_out = None if last else take(1)[0]
    win_v, wout_v, hid_v, pre_v, g_v, in_sems, out_sems, g_sems = refs
    arriving = fetch_grads(where_ref[1], g_own, g_mirror, start, size, g_v, 0, g_sems)
    copies = []
    for r in range(shards):
        pair = (pltpu.make_async_copy(weights[r].at[0], win_v.at[r], in_sems.at[2 * r]),
                pltpu.make_async_copy(weights[r].at[1], wout_v.at[r], in_sems.at[2 * r + 1]))
        for copy in pair:
            copy.start()
        copies.append(pair)
    width = x_ref.shape[2]
    rows = sources * size
    x = x_ref[:, 0:size, :].reshape(rows, width)
    for copy in arriving:
        copy.wait()
    g = g_v[...].reshape(rows, width)
    inner = win_v.shape[2]
    step = 256 if inner % 256 == 0 else inner
    score = jnp.zeros((rows, 1), F32)
    total, result = None, None
    outgoing = []
    for r in range(shards):
        for copy in copies[r]:
            copy.wait()
        for f in range(inner // step):
            cols = slice(f * step, (f + 1) * step)
            hid, slope = gelu_pair(dot_nn(x, win_v[r, :, cols]))
            grad = dot_nn(g, wout_v[r, :, cols])
            hid = hid.astype(BF16)
            score = score + jnp.sum(grad * hid.astype(F32), axis=1, keepdims=True)
            hid_v[r, :, cols] = hid
            pre_v[r, :, cols] = (grad * slope).astype(BF16)
        for source, target in ((hid_v, hidden_ref), (pre_v, pre_ref)):
            copy = pltpu.make_async_copy(source.at[r], target.at[r], out_sems.at[len(outgoing)])
            copy.start()
            outgoing.append(copy)
        part, out = dot_nt(pre_v[r], win_v[r]), dot_nt(hid_v[r], wout_v[r])
        total = part if total is None else total + part
        result = out if result is None else result + out
    back = total.astype(BF16).reshape(sources, size, width)
    result = result.astype(BF16).reshape(sources, size, width)
    eye = iota((size, STRIDE), 1) == iota((size, STRIDE), 0) + start
    if last:
        back_ref[:, 0:size, :] = back
        rows_ref[:, start:, :] = result
        if prior_ref is not None:
            rows_ref[:, 0:start, :] = prior_ref[...]
    else:
        back_ref[...] = back
        rows_ref[...] = result
    for s in range(sources):
        row = jnp.sum(jnp.where(eye, score[s * size : (s + 1) * size], 0.0), axis=0, keepdims=True)
        if last:
            if carry_ref is not None:
                row = row + carry_ref[s : s + 1, :]
            back_ref[s, size : size + PAYLOAD, 0 : 2 * STRIDE] = split_rows(row, PAYLOAD)
            back_ref[s, size : size + PAYLOAD, 2 * STRIDE :] = jnp.zeros((PAYLOAD, width - 2 * STRIDE), BF16)
        else:
            carry_out[s : s + 1, :] = row
    for copy in outgoing:
        copy.wait()


def expert_grad_body(picks, shards, sources, sizes, where_ref, *refs):
    refs = list(refs)
    count = len(sizes)

    def take(number):
        taken = refs[:number]
        del refs[:number]
        return taken

    side = sources // 2
    x_refs, g_own, g_mirror = take(count), take(side), [take(side) for _ in range(count)]
    hidden, pre = take(count), take(count)
    home_ref, send_ref = take(2)
    xt, gt, hid_v, pre_v, out_v, g_v, in_sems, out_sems, g_sems = refs
    arriving = []
    for index, size in enumerate(sizes):
        first = sum(sizes[:index])
        arriving += fetch_grads(where_ref[1], g_own, g_mirror[index], first, size, g_v, first, g_sems.at[index])
    copies = []
    for place, r in enumerate(picks):
        base = 0
        group = []
        for index, size in enumerate(sizes):
            rows = sources * size
            for which, (source, target) in enumerate(((pre[index], pre_v), (hidden[index], hid_v))):
                copy = pltpu.make_async_copy(source.at[r], target.at[place, pl.ds(base, rows)],
                                             in_sems.at[(place * count + index) * 2 + which])
                group.append(copy)
            base += rows
        copies.append(group)
    for copy in copies[0]:
        copy.start()
    width = x_refs[0].shape[2]
    last = x_refs[-1]
    for copy in arriving:
        copy.wait()
    start, base = 0, 0
    for ref, size in zip(x_refs, sizes):
        rows = sources * size
        eye = iota((size, STRIDE), 1) == iota((size, STRIDE), 0) + start
        gate = []
        for s in range(sources):
            row = last[s, sizes[-1] : sizes[-1] + PAYLOAD, :].astype(F32)
            row = row[0:1, 0:STRIDE] + row[0:1, STRIDE : 2 * STRIDE]
            gate.append(jnp.sum(jnp.where(eye, row, 0.0), axis=1, keepdims=True))
        gate = jnp.concatenate(gate, axis=0)
        x = ref[:, 0:size, :].reshape(rows, width).astype(F32) * gate
        g = g_v[:, start : start + size, :].reshape(rows, width).astype(F32) * gate
        xt[:, base : base + rows] = x.T.astype(BF16)
        gt[:, base : base + rows] = g.T.astype(BF16)
        start += size
        base += rows
    outgoing = []
    for place, r in enumerate(picks):
        for copy in copies[place]:
            copy.wait()
        for copy in copies[place + 1] if place + 1 < len(picks) else ():
            copy.start()
        for which, (left, right) in enumerate(((xt, pre_v), (gt, hid_v))):
            out_v[place, which] = dot_nn(left[...], right[place]).astype(BF16)
            target = (send_ref if r % 2 else home_ref).at[r // 2, which]
            copy = pltpu.make_async_copy(out_v.at[place, which], target, out_sems.at[2 * place + which])
            copy.start()
            outgoing.append(copy)
    for copy in outgoing:
        copy.wait()


def grad_sum_body(keep_ref, home_ref, got_ref, passed_ref, *out_refs):
    for index, ref in enumerate(out_refs):
        total = home_ref[0, index].astype(F32) + got_ref[0, index].astype(F32)
        ref[...] = (total + passed_ref[index].astype(F32)) * keep_ref[0, 0]


def gather_body(rows_ref, codes_ref, col_ref, gates_ref, sum_ref):
    sources, size, width = rows_ref.shape
    codes = codes_ref[...]
    pick = jnp.where(col_ref[:, 0:1] == codes, gates_ref[:, 0:1], 0.0)
    pick = jnp.where(col_ref[:, 1:2] == codes, gates_ref[:, 1:2], pick).astype(BF16)
    sum_ref[...] = dot_nn(pick, rows_ref[...].reshape(sources * size, width))


def second_back_body(experts, size, has_sum, *refs):
    refs = list(refs)
    (rows_ref, codes_ref, col_ref, gates_ref, ids_ref, resid_ref, normed_ref, cot_ref, norms_ref, router_ref) = refs[:10]
    del refs[:10]
    sum_ref = refs.pop(0) if has_sum else None
    grad_ref, branch_ref, small_ref = refs
    sources, _, width = rows_ref.shape
    tokens = resid_ref.shape[0]
    codes = codes_ref[...]
    gates = [gates_ref[:, k : k + 1] for k in range(2)]
    slot = [col_ref[:, k : k + 1] for k in range(2)]
    pick = jnp.where(slot[0] == codes, gates[0], 0.0)
    pick = jnp.where(slot[1] == codes, gates[1], pick).astype(BF16)
    total = dot_nn(pick, rows_ref[:, 0:size, :].reshape(sources * size, width))
    if sum_ref is not None:
        total = total + sum_ref[...]
    scores = [jnp.zeros((tokens, 1), F32), jnp.zeros((tokens, 1), F32)]
    for e in range(experts):
        line = rows_ref[e, size : size + PAYLOAD, :].astype(F32)
        line = line[0:1, 0:STRIDE] + line[0:1, STRIDE : 2 * STRIDE]
        place = iota((tokens, STRIDE), 1) + e * STRIDE
        for k in range(2):
            scores[k] = scores[k] + jnp.sum(jnp.where(slot[k] == place, line, 0.0), axis=1, keepdims=True)
    inner = gates[0] * scores[0] + gates[1] * scores[1]
    lanes = iota((tokens, experts), 1)
    logit_grad = jnp.zeros((tokens, experts), F32)
    for k in range(2):
        logit_grad = jnp.where(ids_ref[:, k : k + 1] == lanes, gates[k] * (scores[k] - inner), logit_grad)
    logit_grad = logit_grad.astype(BF16)
    total = total + dot_nn(logit_grad, router_ref[...])
    normal, rate = norm_parts(resid_ref[...])
    grad = cot_ref[...].astype(F32) + norm_back(normal, rate, norms_ref[2:3, :], total)
    grad_ref[...] = grad
    branch_ref[...] = grad.astype(BF16)
    small_ref[0:1, :] = jnp.sum(total * normal, axis=0, keepdims=True)
    small_ref[1:2, :] = jnp.sum(total, axis=0, keepdims=True)
    small_ref[2 : 2 + experts, :] = dot_tn(logit_grad, normed_ref[...])


def attend_back_body(half, has_sum, where_ref, *refs):
    refs = list(refs)
    (q_ref, k_ref, v_ref, log_ref, mixed_own, mixed_other, branch_own, branch_other, own_ref, other_ref,
     w_ref) = refs[:11]
    del refs[:11]
    sums = (refs.pop(0), refs.pop(0)) if has_sum else None
    weight_ref, mine_ref, theirs_ref, rows, branch, grads, mixed, keys, vals, dq, dk, dv, joined, pile = refs
    core = where_ref[0]
    mine = pl.multiple_of(core * half, half)
    theirs = pl.multiple_of((1 - core) * half, half)
    rows[pl.ds(mine, half), :] = own_ref[...]
    rows[pl.ds(theirs, half), :] = other_ref[...]
    branch[pl.ds(mine, half), :] = branch_own[...]
    branch[pl.ds(theirs, half), :] = branch_other[...]
    mixed[pl.ds(mine, half), :] = mixed_own[...]
    mixed[pl.ds(theirs, half), :] = mixed_other[...]
    length, width = q_ref.shape
    grads[...] = dot_nt(branch[...], w_ref[3 * width :, :]).astype(BF16)
    heads = width // HD
    lane = iota((1, width), 1)
    triangle = iota((QUERY_ROWS, QUERY_ROWS), 0) >= iota((QUERY_ROWS, QUERY_ROWS), 1)
    qt = q_ref[...].astype(F32).T.astype(BF16)
    gt = grads[...].astype(F32).T.astype(BF16)
    dk[...] = jnp.zeros(dk.shape, F32)
    dv[...] = jnp.zeros(dv.shape, F32)
    for h in range(heads):
        keep = (lane >= h * HD) & (lane < (h + 1) * HD)
        keys[...] = jnp.where(keep, k_ref[...], 0)
        vals[...] = jnp.where(keep, v_ref[...], 0)
        head = slice(h * HD, (h + 1) * HD)
        for block in range(length // QUERY_ROWS):
            low = block * QUERY_ROWS
            here = slice(low, low + QUERY_ROWS)
            query, grad, log = q_ref[here, :], grads[here, :], log_ref[here, h : h + 1]
            spans = [slice(0, low)] if block else []
            spans.append(here)
            probs, outer = [], []
            inner = None
            for span in spans:
                score = dot_nt(query, keys[span, :])
                if span is here:
                    score = jnp.where(triangle, score, MASKED_SCORE)
                prob = jnp.exp(score - log)
                grad_prob = dot_nt(grad, vals[span, :])
                part = jnp.sum(prob * grad_prob, axis=1, keepdims=True)
                inner = part if inner is None else inner + part
                probs.append(prob)
                outer.append(grad_prob)
            query_grad = None
            for span, prob, grad_prob in zip(spans, probs, outer):
                score_grad = (prob * (grad_prob - inner)).astype(BF16)
                part = dot_nn(score_grad, keys[span, :])
                query_grad = part if query_grad is None else query_grad + part
                dv[head, span] = dv[head, span] + dot_nn(gt[head, here], prob.astype(BF16))
                dk[head, span] = dk[head, span] + dot_nn(qt[head, here], score_grad)
            if h:
                query_grad = query_grad + dq[here, :]
            dq[here, :] = query_grad
    query_grads = dq[...].astype(BF16).astype(F32) * HD ** (-0.5)
    joined[0:width, :] = query_grads.T.astype(BF16)
    joined[width : 2 * width, :] = dk[...].astype(BF16)
    joined[2 * width : 3 * width, :] = dv[...].astype(BF16)
    total = dot_nn(query_grads.astype(BF16), w_ref[0:width, :])
    total = total + dot_nn(dk[...].T.astype(BF16), w_ref[width : 2 * width, :])
    total = total + dot_nn(dv[...].T.astype(BF16), w_ref[2 * width : 3 * width, :])
    pile[...] = total
    one, two = pile[pl.ds(mine, half), :], pile[pl.ds(theirs, half), :]
    if sums is not None:
        one, two = one + sums[0][...], two + sums[1][...]
    mine_ref[...] = one.astype(mine_ref.dtype)
    theirs_ref[...] = two.astype(theirs_ref.dtype)
    weight_ref[0 : 3 * width, :] = dot_nn(joined[...], rows[...]).astype(weight_ref.dtype)
    turned = mixed[...].astype(F32).T.astype(BF16)
    weight_ref[3 * width :, :] = dot_nn(turned, branch[...]).astype(weight_ref.dtype)


def first_back_body(x_ref, norms_ref, mine_ref, other_ref, resid_ref, out_ref, small_ref):
    grad = mine_ref[...] + other_ref[...].astype(F32)
    normal, rate = norm_parts(x_ref[...].astype(F32))
    out_ref[...] = resid_ref[...] + norm_back(normal, rate, norms_ref[0:1, :], grad)
    small_ref[0:1, :] = jnp.sum(grad * normal, axis=0, keepdims=True)
    small_ref[1:2, :] = jnp.sum(grad, axis=0, keepdims=True)


def block_out_body(rows_ref, codes_ref, col_ref, gates_ref, resid_ref, out_ref):
    sources, size, width = rows_ref.shape
    codes = codes_ref[...]
    pick = jnp.where(col_ref[:, 0:1] == codes, gates_ref[:, 0:1], 0.0)
    pick = jnp.where(col_ref[:, 1:2] == codes, gates_ref[:, 1:2], pick).astype(BF16)
    moe = dot_nn(pick, rows_ref[...].reshape(sources * size, width))
    out_ref[...] = (resid_ref[...] + moe).astype(BF16)


def split_body(where_ref, near_ref, far_ref, *out_refs):
    side = len(out_refs)
    rows = out_refs[0].shape[1]
    here = where_ref[1]
    for j, ref in enumerate(out_refs):
        for place, block in enumerate((here ^ j, (here ^ j) ^ side)):
            part = pl.ds(pl.multiple_of(block * rows, rows), rows)
            ref[place] = (near_ref[part, :] + far_ref[part, :].astype(F32)).astype(BF16)


def half_sum_body(*refs):
    keep_ref, send_ref = refs[-2:]
    for place, out in enumerate((keep_ref, send_ref)):
        total = refs[0][place].astype(F32)
        for ref in refs[1:-2]:
            total = total + ref[place].astype(F32)
        out[...] = total.astype(out.dtype)


def final_body(where_ref, *refs):
    all_rows = refs[-1]
    pairs, outs = refs[:-5], refs[-5:-1]
    side = len(pairs)
    rows = pairs[0].shape[1]
    here = where_ref[1]
    for j in range(side):
        for place, block in enumerate((here ^ j, (here ^ j) ^ side)):
            part = pl.ds(pl.multiple_of(block * rows, rows), rows)
            all_rows[part, :] = pairs[j][place].astype(F32)
    count = outs[0].shape[0]
    for index, ref in enumerate(outs):
        ref[...] = all_rows[index * count : (index + 1) * count, :]


def swap(value, axis, step):
    size = lax.axis_size(axis)
    return lax.ppermute(value, axis, [(i, i ^ step) for i in range(size)])


def exchange(value):
    return lax.all_to_all(value, "dp", split_axis=0, concat_axis=0, tiled=True)


def after(value, *others):
    return lax.optimization_barrier((value,) + others)[0]


def codes_of(experts, start, size):
    table = np.arange(experts)[:, None] * STRIDE + start + np.arange(size)[None, :]
    return jnp.asarray(table.reshape(1, -1).astype(np.int32))


def per_device(activations, first_gain, first_shift, query_weight, key_weight, value_weight, output_weight,
               second_gain, second_shift, router_weight, expert_in, expert_out, expert_ids, capacity, new_mask,
               cotangent):
    kernel = functools.partial(call, pins=[activations, output_weight, cotangent])
    tokens, width = activations.shape
    local = query_weight.shape[1]
    heads = local // HD
    experts = router_weight.shape[1]
    sources = lax.axis_size("dp")
    shards = lax.axis_size("head")
    slots = 3 * tokens // experts
    sizes = (slots // 32 * 16, slots - slots // 32 * 16) if slots % 16 == 0 and slots >= 32 else (slots,)
    starts = tuple(sum(sizes[:i]) for i in range(len(sizes)))
    length, half, side = LENGTH, tokens, sources // 2
    where = jnp.stack([lax.axis_index("head") % 2, lax.axis_index("dp")]).astype(jnp.int32)
    last_rows = pl.BlockSpec((local, width), lambda i: (3, 0))

    attn_w = jnp.concatenate([query_weight.T, key_weight.T, value_weight.T, output_weight], axis=0)
    far_w = swap(attn_w, "head", 2)
    norms = jnp.stack([first_gain, first_shift, second_gain, second_shift])
    router = router_weight.T

    normed_first = kernel(first_norm_body, [sds((tokens, width), BF16)], "norm_first", (activations, norms), vmem=16)[0]
    normed_other = swap(normed_first, "head", 1)

    ids_row = expert_ids.T
    extra = jnp.pad(ids_row.astype(BF16), ((0, PAYLOAD - 2), (0, width - tokens)))
    mirror_grad = swap(jnp.concatenate([cotangent, extra], axis=0), "dp", side)
    routed = kernel(
        functools.partial(route_body, slots),
        [sds((tokens, 2), jnp.int32), sds((tokens, 2), jnp.int32), sds((2, tokens), jnp.int32)]
        + [sds((slots, width), BF16)] * side,
        "route", (where, ids_row, capacity, cotangent), smem=(0, 2))
    ids_col, slot_col, slot_row = routed[:3]
    grad_own = [routed[3]] + [swap(routed[3 + j], "dp", j) for j in range(1, side)]

    def attend(weight):
        return kernel(
            functools.partial(attend_body, half),
            [sds((length, local), BF16)] * 3 + [sds((length, heads), F32)] + [sds((half, local), BF16)] * 2,
            "attend", (where, normed_first, normed_other, weight), smem=(0,),
            scratch=[pltpu.VMEM((length, width), BF16), pltpu.VMEM((length, local), F32),
                     pltpu.VMEM((length, local), BF16), pltpu.VMEM((length, local), BF16)])

    near = attend(attn_w)
    mixed = {0: near[4], 1: swap(near[5], "head", 1)}
    far_w = after(far_w, near[4], slot_row)
    away = attend(far_w)
    mixed[2], mixed[3] = away[4], swap(away[5], "head", 1)
    out_w = {1: swap(output_weight, "head", 1), 3: swap(far_w[3 * local :], "head", 1)}

    weights = {0: jnp.stack([expert_in[0], expert_out[0]])}
    weights[1] = swap(weights[0], "head", 1)
    weights[2] = swap(after(weights[0], far_w), "head", 2)
    weights[3] = swap(weights[2], "head", 1)
    inner = weights[0].shape[2]

    mirror_send = kernel(
        functools.partial(mirror_body, slots, len(sizes)),
        [sds((size, width), BF16) for size in sizes for _ in range(side)], "mirror",
        (where, capacity, mirror_grad), smem=(0, 1))
    grad_mirror = []
    for index in range(len(sizes)):
        group = mirror_send[index * side : (index + 1) * side]
        grad_mirror.append([group[0]] + [swap(group[j], "dp", j) for j in range(1, side)])

    first_size = sizes[0] if len(sizes) > 1 else 0
    residual, normed_second, sent = kernel(
        functools.partial(post_body, experts, first_size),
        [sds((tokens, width), F32), sds((tokens, width), BF16), sds((experts, max(first_size, 16), width), BF16)],
        "post_attend",
        (activations, mixed[0], mixed[1], mixed[2], mixed[3], output_weight, out_w[1], far_w, out_w[3], norms,
         after(slot_row, mirror_send[0], *grad_own[1:])), blocks={7: last_rows}, vmem=32)
    gates, sent_last = kernel(
        functools.partial(gate_body, experts, starts[-1], sizes[-1]),
        [sds((tokens, 2), F32), sds((experts, sizes[-1] + PAYLOAD, width), BF16)],
        "gates", (normed_second, router, ids_col, slot_col, slot_row))
    rows_in = []
    if first_size:
        rows_in.append(exchange(sent))
    sent_last = after(sent_last, weights[2], *(rows_in + grad_mirror[0][1:]))
    rows_in.append(exchange(sent_last))

    hidden, pre, back = [], [], []
    carry = ()
    for index, size in enumerate(sizes):
        last = index == len(sizes) - 1
        rows = sources * size
        kept = slots if last else size
        outs = [sds((shards, rows, inner), BF16), sds((shards, rows, inner), BF16),
                sds((sources, size + (PAYLOAD if last else 0), width), BF16), sds((sources, kept, width), BF16)]
        ins = (where, rows_in[index]) + tuple(grad_own) + tuple(grad_mirror[index])
        first = len(ins)
        ins = ins + tuple(weights[r] for r in range(shards)) + carry
        if not last:
            outs.append(sds((sources, STRIDE), F32))
        result = kernel(
            functools.partial(expert_body, shards, sources, starts[index], size, last), outs, "expert", ins,
            vmem=60 if rows <= 768 else 62, smem=(0,), hbm=tuple(range(2, first + shards)), free=(2,),
            out_hbm=(0, 1),
            scratch=[pltpu.VMEM((shards, width, inner), BF16), pltpu.VMEM((shards, width, inner), BF16),
                     pltpu.VMEM((shards, rows, inner), BF16), pltpu.VMEM((shards, rows, inner), BF16),
                     pltpu.VMEM((sources, size, width), BF16), pltpu.SemaphoreType.DMA((2 * shards,)),
                     pltpu.SemaphoreType.DMA((2 * shards,)), pltpu.SemaphoreType.DMA((sources,))])
        hidden.append(result[0])
        pre.append(result[1])
        back.append(result[2])
        expert_rows = result[3]
        if not last:
            carry = (result[4], result[3])
    returned, done = [], rows_in[-1]
    for index, part in enumerate(back):
        done = exchange(after(part, done, *(grad_mirror[-1][1:] if index == 0 else ())))
        returned.append(done)

    partial_sums = ()
    if first_size:
        partial_sums = tuple(kernel(
            gather_body, [sds((tokens, width), F32)], "gather_back",
            (returned[0], codes_of(experts, 0, first_size), slot_col, gates)))

    keep = jnp.sum(jnp.where(jnp.arange(experts) == lax.axis_index("dp"), new_mask, 0)).astype(F32).reshape(1, 1)
    all_rows = sources * slots
    picks = tuple(range(1, shards, 2)) + tuple(range(0, shards, 2))
    skip = 1 + len(sizes)
    grads_home, grads_send = kernel(
        functools.partial(expert_grad_body, picks, shards, sources, sizes),
        [sds((shards // 2, 2, width, inner), BF16)] * 2, "expert_grads",
        (after(where, *partial_sums),) + tuple(rows_in) + tuple(grad_own) + sum(map(tuple, grad_mirror), ()) + tuple(hidden) + tuple(pre), vmem=60,
        smem=(0,), hbm=tuple(range(skip, skip + side * (1 + len(sizes)) + 2 * len(sizes))), out_hbm=(0, 1),
        scratch=[pltpu.VMEM((width, all_rows), BF16), pltpu.VMEM((width, all_rows), BF16),
                 pltpu.VMEM((shards, all_rows, inner), BF16), pltpu.VMEM((shards, all_rows, inner), BF16),
                 pltpu.VMEM((shards, 2, width, inner), BF16), pltpu.VMEM((sources, slots, width), BF16),
                 pltpu.SemaphoreType.DMA((4 * shards,)), pltpu.SemaphoreType.DMA((2 * shards,)),
                 pltpu.SemaphoreType.DMA((len(sizes), sources))])
    grads_got = swap(after(grads_send, returned[-1]), "head", 1)

    grad_residual, grad_branch, small_two = kernel(
        functools.partial(second_back_body, experts, sizes[-1], bool(partial_sums)),
        [sds((tokens, width), F32), sds((tokens, width), BF16), sds((2 + experts, width), F32)], "second_back",
        (returned[-1], codes_of(experts, starts[-1], sizes[-1]), slot_col, gates, ids_col, residual,
         normed_second, cotangent, norms, router) + partial_sums, free=(1, 2))
    branch_other = swap(grad_branch, "head", 1)

    def attend_back(parts, mixed_other, weight, sums, weight_type, types):
        return kernel(
            functools.partial(attend_back_body, half, bool(sums)),
            [sds((4 * local, width), weight_type), sds((half, width), types[0]), sds((half, width), types[1])],
            "attend_back",
            (where,) + tuple(parts[:4]) + (parts[4], parts[5], grad_branch, branch_other, normed_first, normed_other,
                                           weight) + tuple(sums),
            smem=(0,), vmem=32, free=(0, 1, 2),
            scratch=[pltpu.VMEM((length, width), BF16), pltpu.VMEM((length, width), BF16),
                     pltpu.VMEM((length, local), BF16), pltpu.VMEM((length, local), BF16),
                     pltpu.VMEM((length, local), BF16), pltpu.VMEM((length, local), BF16),
                     pltpu.VMEM((length, local), F32), pltpu.VMEM((local, length), F32),
                     pltpu.VMEM((local, length), F32), pltpu.VMEM((3 * local, length), BF16),
                     pltpu.VMEM((length, width), F32)])

    far_grad, far_mine, far_theirs = attend_back(away, mixed[3], far_w, (), BF16, (F32, F32))
    far_got = swap(far_grad, "head", 2)
    near_grad, near_mine, near_theirs = attend_back(near, mixed[1], attn_w, (far_mine, far_theirs), F32, (F32, BF16))
    rows_back = exchange(after(expert_rows, returned[-1], grads_home, *partial_sums))
    block_out = kernel(
        block_out_body, [sds((tokens, width), BF16)], "block_out",
        (rows_back, codes_of(experts, 0, slots), slot_col, gates, residual))[0]

    passed = (grads_home[1].astype(F32) + grads_got[1].astype(F32)).astype(BF16)
    near_grad = after(near_grad, passed)
    passed = swap(after(passed, far_got, near_grad), "head", 2)
    block_rows = 4 * local // sources
    split = kernel(
        split_body, [sds((2, block_rows, width), BF16)] * side, "split", (where, near_grad, far_got), smem=(0,))
    split = [split[0]] + [swap(split[j], "dp", j) for j in range(1, side)]
    first_got = swap(near_theirs, "head", 1)
    grad_input, small_one = kernel(
        first_back_body, [sds((tokens, width), F32), sds((2, width), F32)], "first_back",
        (activations, norms, after(near_mine, split[0]), first_got, grad_residual))
    small = jnp.concatenate([small_one, small_two], axis=0)
    small = jnp.pad(small, ((0, -small.shape[0] % 8), (0, 0)))
    small = small + swap(small, "head", 1)
    own_sum, cross_sum = kernel(
        half_sum_body, [sds((block_rows, width), F32), sds((block_rows, width), BF16)], "half_sum",
        (after(split[0], small, block_out),) + tuple(split[1:]))
    cross_got = swap(cross_sum, "dp", side)
    small = small + swap(small, "dp", 1)
    reduced = (after(own_sum, small) + cross_got.astype(F32)).astype(BF16)
    small = small + swap(small, "dp", 2)
    pair = jnp.stack([reduced, after(swap(reduced, "dp", side), small)])
    pairs = [pair] + [swap(pair, "dp", j) for j in range(1, side)]
    step = 4
    while step < sources:
        small = small + swap(small, "dp", step)
        step *= 2

    part = pl.BlockSpec((1, 2, width, inner), lambda i: (0, 0, 0, 0))
    grad_in, grad_out = kernel(
        grad_sum_body, [sds((width, inner), F32), sds((width, inner), F32)], "grad_sum",
        (keep, grads_home, grads_got, passed), smem=(0,), vmem=40, blocks={1: part, 2: part})

    small = small + swap(after(small, passed), "head", 2)
    pairs[0] = after(pairs[0], grad_in)
    final = kernel(
        final_body, [sds((local, width), F32)] * 4, "final", (where,) + tuple(pairs), smem=(0,),
        scratch=[pltpu.VMEM((4 * local, width), F32)])
    mask = new_mask.astype(F32)[None, :]
    return (
        block_out,
        grad_input,
        small[0],
        small[1],
        final[0].T,
        final[1].T,
        final[2].T,
        final[3],
        small[2],
        small[3],
        small[4 : 4 + experts].T * mask,
        grad_in[None],
        grad_out[None],
    )


def solution(mesh):
    placed = (
        P(("dp", "head"), None),
        P(),
        P(),
        P(None, "head"),
        P(None, "head"),
        P(None, "head"),
        P("head", None),
        P(),
        P(),
        P(),
        P("dp", None, "head"),
        P("dp", None, "head"),
        P(("dp", "head"), None),
        P(),
        P(),
        P(("dp", "head"), None),
    )
    return jax.shard_map(
        per_device,
        mesh=mesh,
        in_specs=placed,
        out_specs=(
            P(("dp", "head"), None),
            P(("dp", "head"), None),
            P(),
            P(),
            P(None, "head"),
            P(None, "head"),
            P(None, "head"),
            P("head", None),
            P(),
            P(),
            P(),
            P("dp", None, "head"),
            P("dp", None, "head"),
        ),
        check_vma=False,
    )
```

```python
import functools

import jax
import jax.numpy as jnp
import numpy as np
from jax import lax
from jax.experimental import pallas as pl
from jax.experimental.pallas import tpu as pltpu
from jax.sharding import PartitionSpec as P

HD = 64
LENGTH = 1024
NORM_EPSILON = 1e-05
MASKED_SCORE = -1e30
QUERY_ROWS = 256
STRIDE = 256
PAYLOAD = 8
MIB = 1 << 20
F32 = jnp.float32
BF16 = jnp.bfloat16
GELU_A = 0.7978845608028654
GELU_B = 0.044715


def dot_nn(left, right):
    return lax.dot_general(left, right, (((1,), (0,)), ((), ())), preferred_element_type=F32)


def dot_nt(left, right):
    return lax.dot_general(left, right, (((1,), (1,)), ((), ())), preferred_element_type=F32)


def dot_tn(left, right):
    return lax.dot_general(left, right, (((0,), (0,)), ((), ())), preferred_element_type=F32)


def iota(shape, axis):
    return lax.broadcasted_iota(jnp.int32, shape, axis)


def call(body, outs, name, ins, vmem=24, scratch=(), smem=(), hbm=(), free=(), out_hbm=(), pins=None, blocks=None):
    specs, given = [], []
    blocks = blocks or {}
    for index, value in enumerate(ins):
        if index in smem:
            specs.append(pl.BlockSpec(memory_space=pltpu.SMEM))
        elif index in hbm:
            specs.append(pl.BlockSpec(memory_space=pltpu.HBM))
        elif index in blocks:
            specs.append(blocks[index])
        else:
            specs.append(pl.BlockSpec())
        if index not in smem and any(value is p for p in pins):
            value = pltpu.with_memory_space_constraint(value, pltpu.HBM)
        given.append(value)
    results = pl.pallas_call(
        body,
        grid=(1,) if blocks else (),
        out_shape=[o if i in free else pltpu.HBM(o.shape, o.dtype) for i, o in enumerate(outs)],
        in_specs=specs,
        out_specs=[pl.BlockSpec(memory_space=pltpu.HBM) if i in out_hbm else pl.BlockSpec() for i in range(len(outs))],
        scratch_shapes=list(scratch),
        compiler_params=pltpu.CompilerParams(vmem_limit_bytes=vmem * MIB),
        cost_estimate=pl.CostEstimate(flops=1, bytes_accessed=1, transcendentals=0),
        name=name,
    )(*given)
    pins.extend(r for i, r in enumerate(results) if i not in free)
    return results


def sds(shape, dtype):
    return jax.ShapeDtypeStruct(shape, dtype)


def norm_parts(values):
    center = jnp.mean(values, axis=1, keepdims=True)
    centered = values - center
    rate = lax.rsqrt(jnp.mean(centered * centered, axis=1, keepdims=True) + NORM_EPSILON)
    return centered * rate, rate


def norm_back(normal, rate, gain, grad):
    scaled = grad * gain
    first = jnp.mean(scaled, axis=1, keepdims=True)
    second = jnp.mean(scaled * normal, axis=1, keepdims=True)
    return rate * (scaled - first - normal * second)


def first_norm_body(x_ref, norms_ref, out_ref):
    normal, _ = norm_parts(x_ref[...].astype(F32))
    out_ref[...] = (normal * norms_ref[0:1, :] + norms_ref[1:2, :]).astype(BF16)


def slot_hits(slot_row, experts, start, count):
    tokens = slot_row.shape[1]
    parts = []
    for e in range(experts):
        codes = iota((count, tokens), 0) + (e * STRIDE + start)
        hit = (slot_row[0:1] == codes) | (slot_row[1:2] == codes)
        parts.append(jnp.where(hit, 1.0, 0.0))
    return jnp.concatenate(parts, axis=0).astype(BF16)


def slots_of(ids, cap_ref):
    tokens = ids.shape[1]
    experts = cap_ref.shape[0]
    upper = jnp.where(iota((tokens, tokens), 0) < iota((tokens, tokens), 1), 1.0, 0.0).astype(BF16)
    rows_e = iota((experts, tokens), 0)
    hot = [jnp.where(ids[k : k + 1] == rows_e, 1.0, 0.0) for k in range(2)]
    earlier = dot_nn((hot[0] + hot[1]).astype(BF16), upper)
    column = iota((experts, 1), 0)
    limit = jnp.zeros((experts, 1), jnp.int32)
    for e in range(experts):
        limit = jnp.where(column == e, cap_ref[e], limit)
    limit = limit.astype(F32)
    rows = []
    for k in range(2):
        place = jnp.sum(hot[k] * earlier, axis=0, keepdims=True)
        top = jnp.sum(hot[k] * limit, axis=0, keepdims=True)
        rows.append(jnp.where(place < top, ids[k : k + 1] * STRIDE + place.astype(jnp.int32), -1))
    return jnp.concatenate(rows, axis=0)


def block_hits(slot_row, block, count):
    codes = iota((count, slot_row.shape[1]), 0) + block * STRIDE
    return jnp.where((slot_row[0:1] == codes) | (slot_row[1:2] == codes), 1.0, 0.0).astype(BF16)


def sort_rows(slots, here, slot_row, rows, send_refs):
    hits = [block_hits(slot_row, here ^ j, slots) for j in range(len(send_refs))]
    sent = dot_nn(jnp.concatenate(hits, axis=0), rows).astype(BF16)
    for j, refs in enumerate(send_refs):
        start = j * slots
        for ref in refs:
            ref[...] = sent[start : start + ref.shape[0]]
            start += ref.shape[0]


def route_body(slots, where_ref, ids_row_ref, cap_ref, grad_ref, ids_ref, col_ref, row_ref, *send_refs):
    ids = ids_row_ref[...]
    slot_row = slots_of(ids, cap_ref)
    row_ref[...] = slot_row
    col_ref[...] = slot_row.astype(F32).T.astype(jnp.int32)
    ids_ref[...] = ids.astype(F32).T.astype(jnp.int32)
    sort_rows(slots, where_ref[1], slot_row, grad_ref[...], [[ref] for ref in send_refs])


def mirror_body(slots, parts, where_ref, cap_ref, grad_ref, *send_refs):
    tokens = grad_ref.shape[0] - PAYLOAD
    ids = grad_ref[tokens:, 0:tokens].astype(F32)[0:2].astype(jnp.int32)
    side = len(send_refs) // parts
    groups = [send_refs[j::side] for j in range(side)]
    sort_rows(slots, where_ref[1], slots_of(ids, cap_ref), grad_ref[0:tokens, :], groups)


def attend_body(half, where_ref, own_ref, other_ref, w_ref,
                q_ref, k_ref, v_ref, log_ref, mine_ref, theirs_ref, rows, mixed, keys, vals):
    core = where_ref[0]
    mine = pl.multiple_of(core * half, half)
    theirs = pl.multiple_of((1 - core) * half, half)
    rows[pl.ds(mine, half), :] = own_ref[...]
    rows[pl.ds(theirs, half), :] = other_ref[...]
    length, width = q_ref.shape
    for part in range(2):
        block = slice(part * half, (part + 1) * half)
        source = rows[block, :]
        q_ref[block, :] = (dot_nt(source, w_ref[0:width, :]) * HD ** (-0.5)).astype(BF16)
        k_ref[block, :] = dot_nt(source, w_ref[width : 2 * width, :]).astype(BF16)
        v_ref[block, :] = dot_nt(source, w_ref[2 * width : 3 * width, :]).astype(BF16)
    heads = width // HD
    lane = iota((1, width), 1)
    triangle = iota((QUERY_ROWS, QUERY_ROWS), 0) >= iota((QUERY_ROWS, QUERY_ROWS), 1)
    for h in range(heads):
        keep = (lane >= h * HD) & (lane < (h + 1) * HD)
        keys[...] = jnp.where(keep, k_ref[...], 0)
        vals[...] = jnp.where(keep, v_ref[...], 0)
        for block in range(length // QUERY_ROWS):
            low = block * QUERY_ROWS
            here = slice(low, low + QUERY_ROWS)
            query = q_ref[here, :]
            diag = jnp.where(triangle, dot_nt(query, keys[here, :]), MASKED_SCORE)
            top = jnp.max(diag, axis=1, keepdims=True)
            if block:
                wide = dot_nt(query, keys[0:low, :])
                top = jnp.maximum(top, jnp.max(wide, axis=1, keepdims=True))
            diag = jnp.exp(diag - top)
            total = jnp.sum(diag, axis=1, keepdims=True)
            result = dot_nn(diag.astype(BF16), vals[here, :])
            if block:
                wide = jnp.exp(wide - top)
                total = total + jnp.sum(wide, axis=1, keepdims=True)
                result = result + dot_nn(wide.astype(BF16), vals[0:low, :])
            result = result / total
            log_ref[here, h : h + 1] = top + jnp.log(total)
            if h:
                result = result + mixed[here, :]
            mixed[here, :] = result
    mine_ref[...] = mixed[pl.ds(mine, half), :].astype(BF16)
    theirs_ref[...] = mixed[pl.ds(theirs, half), :].astype(BF16)


def gates_of(logits, ids_ref, lanes):
    hot = [ids_ref[:, k : k + 1] == lanes for k in range(2)]
    pair = [jnp.sum(jnp.where(hot[k], logits, 0.0), axis=1, keepdims=True) for k in range(2)]
    top = jnp.maximum(pair[0], pair[1])
    raised = [jnp.exp(p - top) for p in pair]
    total = raised[0] + raised[1]
    return [r / total for r in raised]


def split_rows(row, lines):
    high = row.astype(BF16).astype(F32)
    low = row - high
    both = jnp.concatenate([high, low], axis=1)
    return jnp.where(iota((lines, both.shape[1]), 0) == 0, both, 0.0).astype(BF16)


def post_body(experts, size, x_ref, m0, m1, m2, m3, near_ref, w1, far_ref, w3, norms_ref, row_ref,
              resid_ref, normed_ref, send_ref):
    branch = dot_nn(m0[...], near_ref[...]) + dot_nn(m1[...], w1[...])
    branch = branch + (dot_nn(m2[...], far_ref[...]) + dot_nn(m3[...], w3[...]))
    residual = x_ref[...].astype(F32) + branch
    resid_ref[...] = residual
    normal, _ = norm_parts(residual)
    normed = (normal * norms_ref[2:3, :] + norms_ref[3:4, :]).astype(BF16)
    normed_ref[...] = normed
    if size:
        hits = slot_hits(row_ref[...], experts, 0, size)
        send_ref[...] = dot_nn(hits, normed).astype(BF16).reshape(send_ref.shape)


def gate_body(experts, start, size, normed_ref, router_ref, ids_ref, col_ref, row_ref, gates_ref, send_ref):
    normed = normed_ref[...]
    tokens, width = normed.shape
    logits = dot_nt(normed, router_ref[...])
    gates = gates_of(logits, ids_ref, iota((tokens, experts), 1))
    gates_ref[:, 0:1] = gates[0]
    gates_ref[:, 1:2] = gates[1]
    hits = slot_hits(row_ref[...], experts, start, size)
    send_ref[:, 0:size, :] = dot_nn(hits, normed).astype(BF16).reshape(experts, size, width)
    for e in range(experts):
        codes = iota((tokens, STRIDE), 1) + e * STRIDE
        picked = [jnp.where(col_ref[:, k : k + 1] == codes, gates[k], 0.0) for k in range(2)]
        row = jnp.sum(picked[0] + picked[1], axis=0, keepdims=True)
        send_ref[e, size : size + PAYLOAD, 0 : 2 * STRIDE] = split_rows(row, PAYLOAD)
        send_ref[e, size : size + PAYLOAD, 2 * STRIDE :] = jnp.zeros((PAYLOAD, width - 2 * STRIDE), BF16)


def gelu_pair(values):
    square = values * values
    inner = values * (GELU_A + (GELU_A * GELU_B) * square)
    tanh = jnp.tanh(inner)
    half = 0.5 * tanh + 0.5
    slope = half + 0.5 * values * (1.0 - tanh * tanh) * (GELU_A + (3.0 * GELU_A * GELU_B) * square)
    return values * half, slope


def fetch_grads(here, own, mirror, start, size, target, first, sems):
    side = len(own)
    copies = []
    for j in range(side):
        own_part = own[j].at[pl.ds(start, size)]
        for place, ref in ((here ^ j, own_part), ((here ^ j) ^ side, mirror[j])):
            copies.append(pltpu.make_async_copy(ref, target.at[place, pl.ds(first, size)], sems.at[len(copies)]))
    for copy in copies:
        copy.start()
    return copies


def expert_body(shards, sources, start, size, last, where_ref, x_ref, *refs):
    refs = list(refs)
    side = sources // 2

    def take(count):
        taken = refs[:count]
        del refs[:count]
        return taken

    g_own, g_mirror, weights = take(side), take(side), take(shards)
    carry_ref, prior_ref = take(2) if last and start else (None, None)
    hidden_ref, pre_ref, back_ref, rows_ref = take(4)
    carry_out = None if last else take(1)[0]
    win_v, wout_v, hid_v, pre_v, g_v, in_sems, out_sems, g_sems = refs
    arriving = fetch_grads(where_ref[1], g_own, g_mirror, start, size, g_v, 0, g_sems)
    copies = []
    for r in range(shards):
        pair = (pltpu.make_async_copy(weights[r].at[0], win_v.at[r], in_sems.at[2 * r]),
                pltpu.make_async_copy(weights[r].at[1], wout_v.at[r], in_sems.at[2 * r + 1]))
        for copy in pair:
            copy.start()
        copies.append(pair)
    width = x_ref.shape[2]
    rows = sources * size
    x = x_ref[:, 0:size, :].reshape(rows, width)
    for copy in arriving:
        copy.wait()
    g = g_v[...].reshape(rows, width)
    inner = win_v.shape[2]
    step = 256 if inner % 256 == 0 else inner
    score = jnp.zeros((rows, 1), F32)
    total, result = None, None
    outgoing = []
    for r in range(shards):
        for copy in copies[r]:
            copy.wait()
        for f in range(inner // step):
            cols = slice(f * step, (f + 1) * step)
            hid, slope = gelu_pair(dot_nn(x, win_v[r, :, cols]))
            grad = dot_nn(g, wout_v[r, :, cols])
            hid = hid.astype(BF16)
            score = score + jnp.sum(grad * hid.astype(F32), axis=1, keepdims=True)
            hid_v[r, :, cols] = hid
            pre_v[r, :, cols] = (grad * slope).astype(BF16)
        for source, target in ((hid_v, hidden_ref), (pre_v, pre_ref)):
            copy = pltpu.make_async_copy(source.at[r], target.at[r], out_sems.at[len(outgoing)])
            copy.start()
            outgoing.append(copy)
        part, out = dot_nt(pre_v[r], win_v[r]), dot_nt(hid_v[r], wout_v[r])
        total = part if total is None else total + part
        result = out if result is None else result + out
    back = total.astype(BF16).reshape(sources, size, width)
    result = result.astype(BF16).reshape(sources, size, width)
    eye = iota((size, STRIDE), 1) == iota((size, STRIDE), 0) + start
    if last:
        back_ref[:, 0:size, :] = back
        rows_ref[:, start:, :] = result
        if prior_ref is not None:
            rows_ref[:, 0:start, :] = prior_ref[...]
    else:
        back_ref[...] = back
        rows_ref[...] = result
    for s in range(sources):
        row = jnp.sum(jnp.where(eye, score[s * size : (s + 1) * size], 0.0), axis=0, keepdims=True)
        if last:
            if carry_ref is not None:
                row = row + carry_ref[s : s + 1, :]
            back_ref[s, size : size + PAYLOAD, 0 : 2 * STRIDE] = split_rows(row, PAYLOAD)
            back_ref[s, size : size + PAYLOAD, 2 * STRIDE :] = jnp.zeros((PAYLOAD, width - 2 * STRIDE), BF16)
        else:
            carry_out[s : s + 1, :] = row
    for copy in outgoing:
        copy.wait()


def expert_grad_body(picks, shards, sources, sizes, where_ref, *refs):
    refs = list(refs)
    count = len(sizes)

    def take(number):
        taken = refs[:number]
        del refs[:number]
        return taken

    side = sources // 2
    x_refs, g_own, g_mirror = take(count), take(side), [take(side) for _ in range(count)]
    hidden, pre = take(count), take(count)
    home_ref, send_ref = take(2)
    xt, gt, hid_v, pre_v, out_v, g_v, in_sems, out_sems, g_sems = refs
    arriving = []
    for index, size in enumerate(sizes):
        first = sum(sizes[:index])
        arriving += fetch_grads(where_ref[1], g_own, g_mirror[index], first, size, g_v, first, g_sems.at[index])
    copies = []
    for place, r in enumerate(picks):
        base = 0
        group = []
        for index, size in enumerate(sizes):
            rows = sources * size
            for which, (source, target) in enumerate(((pre[index], pre_v), (hidden[index], hid_v))):
                copy = pltpu.make_async_copy(source.at[r], target.at[place, pl.ds(base, rows)],
                                             in_sems.at[(place * count + index) * 2 + which])
                group.append(copy)
            base += rows
        copies.append(group)
    for copy in copies[0]:
        copy.start()
    width = x_refs[0].shape[2]
    last = x_refs[-1]
    for copy in arriving:
        copy.wait()
    start, base = 0, 0
    for ref, size in zip(x_refs, sizes):
        rows = sources * size
        eye = iota((size, STRIDE), 1) == iota((size, STRIDE), 0) + start
        gate = []
        for s in range(sources):
            row = last[s, sizes[-1] : sizes[-1] + PAYLOAD, :].astype(F32)
            row = row[0:1, 0:STRIDE] + row[0:1, STRIDE : 2 * STRIDE]
            gate.append(jnp.sum(jnp.where(eye, row, 0.0), axis=1, keepdims=True))
        gate = jnp.concatenate(gate, axis=0)
        x = ref[:, 0:size, :].reshape(rows, width).astype(F32) * gate
        g = g_v[:, start : start + size, :].reshape(rows, width).astype(F32) * gate
        xt[:, base : base + rows] = x.T.astype(BF16)
        gt[:, base : base + rows] = g.T.astype(BF16)
        start += size
        base += rows
    outgoing = []
    for place, r in enumerate(picks):
        for copy in copies[place]:
            copy.wait()
        for copy in copies[place + 1] if place + 1 < len(picks) else ():
            copy.start()
        for which, (left, right) in enumerate(((xt, pre_v), (gt, hid_v))):
            out_v[place, which] = dot_nn(left[...], right[place]).astype(BF16)
            target = (send_ref if r % 2 else home_ref).at[r // 2, which]
            copy = pltpu.make_async_copy(out_v.at[place, which], target, out_sems.at[2 * place + which])
            copy.start()
            outgoing.append(copy)
    for copy in outgoing:
        copy.wait()


def grad_sum_body(keep_ref, home_ref, got_ref, passed_ref, *out_refs):
    for index, ref in enumerate(out_refs):
        total = home_ref[0, index].astype(F32) + got_ref[0, index].astype(F32)
        ref[...] = (total + passed_ref[index].astype(F32)) * keep_ref[0, 0]


def gather_body(rows_ref, codes_ref, col_ref, gates_ref, sum_ref):
    sources, size, width = rows_ref.shape
    codes = codes_ref[...]
    pick = jnp.where(col_ref[:, 0:1] == codes, gates_ref[:, 0:1], 0.0)
    pick = jnp.where(col_ref[:, 1:2] == codes, gates_ref[:, 1:2], pick).astype(BF16)
    sum_ref[...] = dot_nn(pick, rows_ref[...].reshape(sources * size, width))


def second_back_body(experts, size, has_sum, *refs):
    refs = list(refs)
    (rows_ref, codes_ref, col_ref, gates_ref, ids_ref, resid_ref, normed_ref, cot_ref, norms_ref, router_ref) = refs[:10]
    del refs[:10]
    sum_ref = refs.pop(0) if has_sum else None
    grad_ref, branch_ref, small_ref = refs
    sources, _, width = rows_ref.shape
    tokens = resid_ref.shape[0]
    codes = codes_ref[...]
    gates = [gates_ref[:, k : k + 1] for k in range(2)]
    slot = [col_ref[:, k : k + 1] for k in range(2)]
    pick = jnp.where(slot[0] == codes, gates[0], 0.0)
    pick = jnp.where(slot[1] == codes, gates[1], pick).astype(BF16)
    total = dot_nn(pick, rows_ref[:, 0:size, :].reshape(sources * size, width))
    if sum_ref is not None:
        total = total + sum_ref[...]
    scores = [jnp.zeros((tokens, 1), F32), jnp.zeros((tokens, 1), F32)]
    for e in range(experts):
        line = rows_ref[e, size : size + PAYLOAD, :].astype(F32)
        line = line[0:1, 0:STRIDE] + line[0:1, STRIDE : 2 * STRIDE]
        place = iota((tokens, STRIDE), 1) + e * STRIDE
        for k in range(2):
            scores[k] = scores[k] + jnp.sum(jnp.where(slot[k] == place, line, 0.0), axis=1, keepdims=True)
    inner = gates[0] * scores[0] + gates[1] * scores[1]
    lanes = iota((tokens, experts), 1)
    logit_grad = jnp.zeros((tokens, experts), F32)
    for k in range(2):
        logit_grad = jnp.where(ids_ref[:, k : k + 1] == lanes, gates[k] * (scores[k] - inner), logit_grad)
    logit_grad = logit_grad.astype(BF16)
    total = total + dot_nn(logit_grad, router_ref[...])
    normal, rate = norm_parts(resid_ref[...])
    grad = cot_ref[...].astype(F32) + norm_back(normal, rate, norms_ref[2:3, :], total)
    grad_ref[...] = grad
    branch_ref[...] = grad.astype(BF16)
    small_ref[0:1, :] = jnp.sum(total * normal, axis=0, keepdims=True)
    small_ref[1:2, :] = jnp.sum(total, axis=0, keepdims=True)
    small_ref[2 : 2 + experts, :] = dot_tn(logit_grad, normed_ref[...])


def attend_back_body(half, has_sum, where_ref, *refs):
    refs = list(refs)
    (q_ref, k_ref, v_ref, log_ref, mixed_own, mixed_other, branch_own, branch_other, own_ref, other_ref,
     w_ref) = refs[:11]
    del refs[:11]
    sums = (refs.pop(0), refs.pop(0)) if has_sum else None
    weight_ref, mine_ref, theirs_ref, rows, branch, grads, mixed, keys, vals, dq, dk, dv, joined, pile = refs
    core = where_ref[0]
    mine = pl.multiple_of(core * half, half)
    theirs = pl.multiple_of((1 - core) * half, half)
    rows[pl.ds(mine, half), :] = own_ref[...]
    rows[pl.ds(theirs, half), :] = other_ref[...]
    branch[pl.ds(mine, half), :] = branch_own[...]
    branch[pl.ds(theirs, half), :] = branch_other[...]
    mixed[pl.ds(mine, half), :] = mixed_own[...]
    mixed[pl.ds(theirs, half), :] = mixed_other[...]
    length, width = q_ref.shape
    grads[...] = dot_nt(branch[...], w_ref[3 * width :, :]).astype(BF16)
    heads = width // HD
    lane = iota((1, width), 1)
    triangle = iota((QUERY_ROWS, QUERY_ROWS), 0) >= iota((QUERY_ROWS, QUERY_ROWS), 1)
    qt = q_ref[...].astype(F32).T.astype(BF16)
    gt = grads[...].astype(F32).T.astype(BF16)
    dk[...] = jnp.zeros(dk.shape, F32)
    dv[...] = jnp.zeros(dv.shape, F32)
    for h in range(heads):
        keep = (lane >= h * HD) & (lane < (h + 1) * HD)
        keys[...] = jnp.where(keep, k_ref[...], 0)
        vals[...] = jnp.where(keep, v_ref[...], 0)
        head = slice(h * HD, (h + 1) * HD)
        for block in range(length // QUERY_ROWS):
            low = block * QUERY_ROWS
            here = slice(low, low + QUERY_ROWS)
            query, grad, log = q_ref[here, :], grads[here, :], log_ref[here, h : h + 1]
            spans = [slice(0, low)] if block else []
            spans.append(here)
            probs, outer = [], []
            inner = None
            for span in spans:
                score = dot_nt(query, keys[span, :])
                if span is here:
                    score = jnp.where(triangle, score, MASKED_SCORE)
                prob = jnp.exp(score - log)
                grad_prob = dot_nt(grad, vals[span, :])
                part = jnp.sum(prob * grad_prob, axis=1, keepdims=True)
                inner = part if inner is None else inner + part
                probs.append(prob)
                outer.append(grad_prob)
            query_grad = None
            for span, prob, grad_prob in zip(spans, probs, outer):
                score_grad = (prob * (grad_prob - inner)).astype(BF16)
                part = dot_nn(score_grad, keys[span, :])
                query_grad = part if query_grad is None else query_grad + part
                dv[head, span] = dv[head, span] + dot_nn(gt[head, here], prob.astype(BF16))
                dk[head, span] = dk[head, span] + dot_nn(qt[head, here], score_grad)
            if h:
                query_grad = query_grad + dq[here, :]
            dq[here, :] = query_grad
    query_grads = dq[...].astype(BF16).astype(F32) * HD ** (-0.5)
    joined[0:width, :] = query_grads.T.astype(BF16)
    joined[width : 2 * width, :] = dk[...].astype(BF16)
    joined[2 * width : 3 * width, :] = dv[...].astype(BF16)
    total = dot_nn(query_grads.astype(BF16), w_ref[0:width, :])
    total = total + dot_nn(dk[...].T.astype(BF16), w_ref[width : 2 * width, :])
    total = total + dot_nn(dv[...].T.astype(BF16), w_ref[2 * width : 3 * width, :])
    pile[...] = total
    one, two = pile[pl.ds(mine, half), :], pile[pl.ds(theirs, half), :]
    if sums is not None:
        one, two = one + sums[0][...], two + sums[1][...]
    mine_ref[...] = one.astype(mine_ref.dtype)
    theirs_ref[...] = two.astype(theirs_ref.dtype)
    weight_ref[0 : 3 * width, :] = dot_nn(joined[...], rows[...]).astype(weight_ref.dtype)
    turned = mixed[...].astype(F32).T.astype(BF16)
    weight_ref[3 * width :, :] = dot_nn(turned, branch[...]).astype(weight_ref.dtype)


def first_back_body(x_ref, norms_ref, mine_ref, other_ref, resid_ref, out_ref, small_ref):
    grad = mine_ref[...] + other_ref[...].astype(F32)
    normal, rate = norm_parts(x_ref[...].astype(F32))
    out_ref[...] = resid_ref[...] + norm_back(normal, rate, norms_ref[0:1, :], grad)
    small_ref[0:1, :] = jnp.sum(grad * normal, axis=0, keepdims=True)
    small_ref[1:2, :] = jnp.sum(grad, axis=0, keepdims=True)


def block_out_body(rows_ref, codes_ref, col_ref, gates_ref, resid_ref, out_ref):
    sources, size, width = rows_ref.shape
    codes = codes_ref[...]
    pick = jnp.where(col_ref[:, 0:1] == codes, gates_ref[:, 0:1], 0.0)
    pick = jnp.where(col_ref[:, 1:2] == codes, gates_ref[:, 1:2], pick).astype(BF16)
    moe = dot_nn(pick, rows_ref[...].reshape(sources * size, width))
    out_ref[...] = (resid_ref[...] + moe).astype(BF16)


def split_body(where_ref, near_ref, far_ref, *out_refs):
    side = len(out_refs)
    rows = out_refs[0].shape[1]
    here = where_ref[1]
    for j, ref in enumerate(out_refs):
        for place, block in enumerate((here ^ j, (here ^ j) ^ side)):
            part = pl.ds(pl.multiple_of(block * rows, rows), rows)
            ref[place] = (near_ref[part, :] + far_ref[part, :].astype(F32)).astype(BF16)


def half_sum_body(*refs):
    keep_ref, send_ref = refs[-2:]
    for place, out in enumerate((keep_ref, send_ref)):
        total = refs[0][place].astype(F32)
        for ref in refs[1:-2]:
            total = total + ref[place].astype(F32)
        out[...] = total.astype(out.dtype)


def final_body(where_ref, *refs):
    all_rows = refs[-1]
    pairs, outs = refs[:-5], refs[-5:-1]
    side = len(pairs)
    rows = pairs[0].shape[1]
    here = where_ref[1]
    for j in range(side):
        for place, block in enumerate((here ^ j, (here ^ j) ^ side)):
            part = pl.ds(pl.multiple_of(block * rows, rows), rows)
            all_rows[part, :] = pairs[j][place].astype(F32)
    count = outs[0].shape[0]
    for index, ref in enumerate(outs):
        ref[...] = all_rows[index * count : (index + 1) * count, :]


def swap(value, axis, step):
    size = lax.axis_size(axis)
    return lax.ppermute(value, axis, [(i, i ^ step) for i in range(size)])


def exchange(value):
    return lax.all_to_all(value, "dp", split_axis=0, concat_axis=0, tiled=True)


def after(value, *others):
    return lax.optimization_barrier((value,) + others)[0]


def codes_of(experts, start, size):
    table = np.arange(experts)[:, None] * STRIDE + start + np.arange(size)[None, :]
    return jnp.asarray(table.reshape(1, -1).astype(np.int32))


def per_device(activations, first_gain, first_shift, query_weight, key_weight, value_weight, output_weight,
               second_gain, second_shift, router_weight, expert_in, expert_out, expert_ids, capacity, new_mask,
               cotangent):
    kernel = functools.partial(call, pins=[activations, output_weight, cotangent])
    tokens, width = activations.shape
    local = query_weight.shape[1]
    heads = local // HD
    experts = router_weight.shape[1]
    sources = lax.axis_size("dp")
    shards = lax.axis_size("head")
    slots = 3 * tokens // experts
    sizes = (slots // 32 * 16, slots - slots // 32 * 16) if slots % 16 == 0 and slots >= 32 else (slots,)
    starts = tuple(sum(sizes[:i]) for i in range(len(sizes)))
    length, half, side = LENGTH, tokens, sources // 2
    where = jnp.stack([lax.axis_index("head") % 2, lax.axis_index("dp")]).astype(jnp.int32)
    last_rows = pl.BlockSpec((local, width), lambda i: (3, 0))

    attn_w = jnp.concatenate([query_weight.T, key_weight.T, value_weight.T, output_weight], axis=0)
    far_w = swap(attn_w, "head", 2)
    norms = jnp.stack([first_gain, first_shift, second_gain, second_shift])
    router = router_weight.T

    normed_first = kernel(first_norm_body, [sds((tokens, width), BF16)], "norm_first", (activations, norms), vmem=16)[0]
    normed_other = swap(normed_first, "head", 1)

    ids_row = expert_ids.T
    extra = jnp.pad(ids_row.astype(BF16), ((0, PAYLOAD - 2), (0, width - tokens)))
    mirror_grad = swap(jnp.concatenate([cotangent, extra], axis=0), "dp", side)
    routed = kernel(
        functools.partial(route_body, slots),
        [sds((tokens, 2), jnp.int32), sds((tokens, 2), jnp.int32), sds((2, tokens), jnp.int32)]
        + [sds((slots, width), BF16)] * side,
        "route", (where, ids_row, capacity, cotangent), smem=(0, 2))
    ids_col, slot_col, slot_row = routed[:3]
    grad_own = [routed[3]] + [swap(routed[3 + j], "dp", j) for j in range(1, side)]

    def attend(weight):
        return kernel(
            functools.partial(attend_body, half),
            [sds((length, local), BF16)] * 3 + [sds((length, heads), F32)] + [sds((half, local), BF16)] * 2,
            "attend", (where, normed_first, normed_other, weight), smem=(0,),
            scratch=[pltpu.VMEM((length, width), BF16), pltpu.VMEM((length, local), F32),
                     pltpu.VMEM((length, local), BF16), pltpu.VMEM((length, local), BF16)])

    near = attend(attn_w)
    mixed = {0: near[4], 1: swap(near[5], "head", 1)}
    far_w = after(far_w, near[4], slot_row)
    away = attend(far_w)
    mixed[2], mixed[3] = away[4], swap(away[5], "head", 1)
    out_w = {1: swap(output_weight, "head", 1), 3: swap(far_w[3 * local :], "head", 1)}

    weights = {0: jnp.stack([expert_in[0], expert_out[0]])}
    weights[1] = swap(weights[0], "head", 1)
    weights[2] = swap(after(weights[0], far_w), "head", 2)
    inner = weights[0].shape[2]

    mirror_send = kernel(
        functools.partial(mirror_body, slots, len(sizes)),
        [sds((size, width), BF16) for size in sizes for _ in range(side)], "mirror",
        (where, capacity, mirror_grad), smem=(0, 1))
    grad_mirror = []
    for index in range(len(sizes)):
        group = mirror_send[index * side : (index + 1) * side]
        grad_mirror.append([group[0]] + [swap(group[j], "dp", j) for j in range(1, side)])

    first_size = sizes[0] if len(sizes) > 1 else 0
    residual, normed_second, sent = kernel(
        functools.partial(post_body, experts, first_size),
        [sds((tokens, width), F32), sds((tokens, width), BF16), sds((experts, max(first_size, 16), width), BF16)],
        "post_attend",
        (activations, mixed[0], mixed[1], mixed[2], mixed[3], output_weight, out_w[1], far_w, out_w[3], norms,
         after(slot_row, mirror_grad, *grad_own[1:])), blocks={7: last_rows}, vmem=32)
    gates, sent_last = kernel(
        functools.partial(gate_body, experts, starts[-1], sizes[-1]),
        [sds((tokens, 2), F32), sds((experts, sizes[-1] + PAYLOAD, width), BF16)],
        "gates", (normed_second, router, ids_col, slot_col, slot_row))
    weights[3] = swap(after(weights[2], sent_last), "head", 1)
    rows_in = []
    if first_size:
        rows_in.append(exchange(sent))
    sent_last = after(sent_last, weights[2], *(rows_in + grad_mirror[0][1:]))
    rows_in.append(exchange(sent_last))

    hidden, pre, back = [], [], []
    carry = ()
    for index, size in enumerate(sizes):
        last = index == len(sizes) - 1
        rows = sources * size
        kept = slots if last else size
        outs = [sds((shards, rows, inner), BF16), sds((shards, rows, inner), BF16),
                sds((sources, size + (PAYLOAD if last else 0), width), BF16), sds((sources, kept, width), BF16)]
        ins = (where, rows_in[index]) + tuple(grad_own) + tuple(grad_mirror[index])
        first = len(ins)
        ins = ins + tuple(weights[r] for r in range(shards)) + carry
        if not last:
            outs.append(sds((sources, STRIDE), F32))
        result = kernel(
            functools.partial(expert_body, shards, sources, starts[index], size, last), outs, "expert", ins,
            vmem=60 if rows <= 768 else 62, smem=(0,), hbm=tuple(range(2, first + shards)), free=(2,),
            out_hbm=(0, 1),
            scratch=[pltpu.VMEM((shards, width, inner), BF16), pltpu.VMEM((shards, width, inner), BF16),
                     pltpu.VMEM((shards, rows, inner), BF16), pltpu.VMEM((shards, rows, inner), BF16),
                     pltpu.VMEM((sources, size, width), BF16), pltpu.SemaphoreType.DMA((2 * shards,)),
                     pltpu.SemaphoreType.DMA((2 * shards,)), pltpu.SemaphoreType.DMA((sources,))])
        hidden.append(result[0])
        pre.append(result[1])
        back.append(result[2])
        expert_rows = result[3]
        if not last:
            carry = (result[4], result[3])
    returned, done = [], rows_in[-1]
    for index, part in enumerate(back):
        done = exchange(after(part, done, *(grad_mirror[-1][1:] if index == 0 else ())))
        returned.append(done)

    partial_sums = ()
    if first_size:
        partial_sums = tuple(kernel(
            gather_body, [sds((tokens, width), F32)], "gather_back",
            (returned[0], codes_of(experts, 0, first_size), slot_col, gates)))

    keep = jnp.sum(jnp.where(jnp.arange(experts) == lax.axis_index("dp"), new_mask, 0)).astype(F32).reshape(1, 1)
    all_rows = sources * slots
    picks = tuple(range(1, shards, 2)) + tuple(range(0, shards, 2))
    skip = 1 + len(sizes)
    grads_home, grads_send = kernel(
        functools.partial(expert_grad_body, picks, shards, sources, sizes),
        [sds((shards // 2, 2, width, inner), BF16)] * 2, "expert_grads",
        (after(where, *partial_sums),) + tuple(rows_in) + tuple(grad_own) + sum(map(tuple, grad_mirror), ()) + tuple(hidden) + tuple(pre), vmem=60,
        smem=(0,), hbm=tuple(range(skip, skip + side * (1 + len(sizes)) + 2 * len(sizes))), out_hbm=(0, 1),
        scratch=[pltpu.VMEM((width, all_rows), BF16), pltpu.VMEM((width, all_rows), BF16),
                 pltpu.VMEM((shards, all_rows, inner), BF16), pltpu.VMEM((shards, all_rows, inner), BF16),
                 pltpu.VMEM((shards, 2, width, inner), BF16), pltpu.VMEM((sources, slots, width), BF16),
                 pltpu.SemaphoreType.DMA((4 * shards,)), pltpu.SemaphoreType.DMA((2 * shards,)),
                 pltpu.SemaphoreType.DMA((len(sizes), sources))])
    grads_got = swap(after(grads_send, returned[-1]), "head", 1)

    grad_residual, grad_branch, small_two = kernel(
        functools.partial(second_back_body, experts, sizes[-1], bool(partial_sums)),
        [sds((tokens, width), F32), sds((tokens, width), BF16), sds((2 + experts, width), F32)], "second_back",
        (returned[-1], codes_of(experts, starts[-1], sizes[-1]), slot_col, gates, ids_col, residual,
         normed_second, cotangent, norms, router) + partial_sums, free=(1, 2))
    branch_other = swap(grad_branch, "head", 1)

    def attend_back(parts, mixed_other, weight, sums, weight_type, types):
        return kernel(
            functools.partial(attend_back_body, half, bool(sums)),
            [sds((4 * local, width), weight_type), sds((half, width), types[0]), sds((half, width), types[1])],
            "attend_back",
            (where,) + tuple(parts[:4]) + (parts[4], parts[5], grad_branch, branch_other, normed_first, normed_other,
                                           weight) + tuple(sums),
            smem=(0,), vmem=32, free=(0, 1, 2),
            scratch=[pltpu.VMEM((length, width), BF16), pltpu.VMEM((length, width), BF16),
                     pltpu.VMEM((length, local), BF16), pltpu.VMEM((length, local), BF16),
                     pltpu.VMEM((length, local), BF16), pltpu.VMEM((length, local), BF16),
                     pltpu.VMEM((length, local), F32), pltpu.VMEM((local, length), F32),
                     pltpu.VMEM((local, length), F32), pltpu.VMEM((3 * local, length), BF16),
                     pltpu.VMEM((length, width), F32)])

    far_grad, far_mine, far_theirs = attend_back(away, mixed[3], far_w, (), BF16, (F32, F32))
    far_got = swap(far_grad, "head", 2)
    near_grad, near_mine, near_theirs = attend_back(near, mixed[1], attn_w, (far_mine, far_theirs), F32, (F32, BF16))
    rows_back = exchange(after(expert_rows, returned[-1], grads_home, *partial_sums))
    block_out = kernel(
        block_out_body, [sds((tokens, width), BF16)], "block_out",
        (rows_back, codes_of(experts, 0, slots), slot_col, gates, residual))[0]

    passed = (grads_home[1].astype(F32) + grads_got[1].astype(F32)).astype(BF16)
    near_grad = after(near_grad, passed)
    passed = swap(after(passed, far_got, near_grad), "head", 2)
    block_rows = 4 * local // sources
    split = kernel(
        split_body, [sds((2, block_rows, width), BF16)] * side, "split", (where, near_grad, far_got), smem=(0,))
    split = [split[0]] + [swap(split[j], "dp", j) for j in range(1, side)]
    first_got = swap(near_theirs, "head", 1)
    grad_input, small_one = kernel(
        first_back_body, [sds((tokens, width), F32), sds((2, width), F32)], "first_back",
        (activations, norms, after(near_mine, split[0]), first_got, grad_residual))
    small = jnp.concatenate([small_one, small_two], axis=0)
    small = jnp.pad(small, ((0, -small.shape[0] % 8), (0, 0)))
    small = small + swap(small, "head", 1)
    own_sum, cross_sum = kernel(
        half_sum_body, [sds((block_rows, width), F32), sds((block_rows, width), BF16)], "half_sum",
        (after(split[0], small, block_out),) + tuple(split[1:]))
    cross_got = swap(cross_sum, "dp", side)
    small = small + swap(small, "dp", 1)
    reduced = (after(own_sum, small) + cross_got.astype(F32)).astype(BF16)
    small = small + swap(small, "dp", 2)
    pair = jnp.stack([reduced, after(swap(reduced, "dp", side), small)])
    pairs = [pair] + [swap(pair, "dp", j) for j in range(1, side)]
    step = 4
    while step < sources:
        small = small + swap(small, "dp", step)
        step *= 2

    part = pl.BlockSpec((1, 2, width, inner), lambda i: (0, 0, 0, 0))
    grad_in, grad_out = kernel(
        grad_sum_body, [sds((width, inner), F32), sds((width, inner), F32)], "grad_sum",
        (keep, grads_home, grads_got, passed), smem=(0,), vmem=40, blocks={1: part, 2: part})

    small = small + swap(after(small, passed), "head", 2)
    pairs[0] = after(pairs[0], grad_in)
    final = kernel(
        final_body, [sds((local, width), F32)] * 4, "final", (where,) + tuple(pairs), smem=(0,),
        scratch=[pltpu.VMEM((4 * local, width), F32)])
    mask = new_mask.astype(F32)[None, :]
    return (
        block_out,
        grad_input,
        small[0],
        small[1],
        final[0].T,
        final[1].T,
        final[2].T,
        final[3],
        small[2],
        small[3],
        small[4 : 4 + experts].T * mask,
        grad_in[None],
        grad_out[None],
    )


def solution(mesh):
    placed = (
        P(("dp", "head"), None),
        P(),
        P(),
        P(None, "head"),
        P(None, "head"),
        P(None, "head"),
        P("head", None),
        P(),
        P(),
        P(),
        P("dp", None, "head"),
        P("dp", None, "head"),
        P(("dp", "head"), None),
        P(),
        P(),
        P(("dp", "head"), None),
    )
    return jax.shard_map(
        per_device,
        mesh=mesh,
        in_specs=placed,
        out_specs=(
            P(("dp", "head"), None),
            P(("dp", "head"), None),
            P(),
            P(),
            P(None, "head"),
            P(None, "head"),
            P(None, "head"),
            P("head", None),
            P(),
            P(),
            P(),
            P("dp", None, "head"),
            P("dp", None, "head"),
        ),
        check_vma=False,
    )
```

```python
import functools

import jax
import jax.numpy as jnp
import numpy as np
from jax import lax
from jax.experimental import pallas as pl
from jax.experimental.pallas import tpu as pltpu
from jax.sharding import PartitionSpec as P

HD = 64
LENGTH = 1024
NORM_EPSILON = 1e-05
MASKED_SCORE = -1e30
QUERY_ROWS = 256
STRIDE = 256
PAYLOAD = 8
MIB = 1 << 20
F32 = jnp.float32
BF16 = jnp.bfloat16
GELU_A = 0.7978845608028654
GELU_B = 0.044715


def dot_nn(left, right):
    return lax.dot_general(left, right, (((1,), (0,)), ((), ())), preferred_element_type=F32)


def dot_nt(left, right):
    return lax.dot_general(left, right, (((1,), (1,)), ((), ())), preferred_element_type=F32)


def dot_tn(left, right):
    return lax.dot_general(left, right, (((0,), (0,)), ((), ())), preferred_element_type=F32)


def iota(shape, axis):
    return lax.broadcasted_iota(jnp.int32, shape, axis)


def call(body, outs, name, ins, vmem=24, scratch=(), smem=(), hbm=(), free=(), out_hbm=(), pins=None, blocks=None):
    specs, given = [], []
    blocks = blocks or {}
    for index, value in enumerate(ins):
        if index in smem:
            specs.append(pl.BlockSpec(memory_space=pltpu.SMEM))
        elif index in hbm:
            specs.append(pl.BlockSpec(memory_space=pltpu.HBM))
        elif index in blocks:
            specs.append(blocks[index])
        else:
            specs.append(pl.BlockSpec())
        if index not in smem and any(value is p for p in pins):
            value = pltpu.with_memory_space_constraint(value, pltpu.HBM)
        given.append(value)
    results = pl.pallas_call(
        body,
        grid=(1,) if blocks else (),
        out_shape=[o if i in free else pltpu.HBM(o.shape, o.dtype) for i, o in enumerate(outs)],
        in_specs=specs,
        out_specs=[pl.BlockSpec(memory_space=pltpu.HBM) if i in out_hbm else pl.BlockSpec() for i in range(len(outs))],
        scratch_shapes=list(scratch),
        compiler_params=pltpu.CompilerParams(vmem_limit_bytes=vmem * MIB),
        cost_estimate=pl.CostEstimate(flops=1, bytes_accessed=1, transcendentals=0),
        name=name,
    )(*given)
    pins.extend(r for i, r in enumerate(results) if i not in free)
    return results


def sds(shape, dtype):
    return jax.ShapeDtypeStruct(shape, dtype)


def norm_parts(values):
    center = jnp.mean(values, axis=1, keepdims=True)
    centered = values - center
    rate = lax.rsqrt(jnp.mean(centered * centered, axis=1, keepdims=True) + NORM_EPSILON)
    return centered * rate, rate


def norm_back(normal, rate, gain, grad):
    scaled = grad * gain
    first = jnp.mean(scaled, axis=1, keepdims=True)
    second = jnp.mean(scaled * normal, axis=1, keepdims=True)
    return rate * (scaled - first - normal * second)


def first_norm_body(x_ref, norms_ref, out_ref):
    normal, _ = norm_parts(x_ref[...].astype(F32))
    out_ref[...] = (normal * norms_ref[0:1, :] + norms_ref[1:2, :]).astype(BF16)


def slot_hits(slot_row, experts, start, count):
    tokens = slot_row.shape[1]
    parts = []
    for e in range(experts):
        codes = iota((count, tokens), 0) + (e * STRIDE + start)
        hit = (slot_row[0:1] == codes) | (slot_row[1:2] == codes)
        parts.append(jnp.where(hit, 1.0, 0.0))
    return jnp.concatenate(parts, axis=0).astype(BF16)


def slots_of(ids, cap_ref):
    tokens = ids.shape[1]
    experts = cap_ref.shape[0]
    upper = jnp.where(iota((tokens, tokens), 0) < iota((tokens, tokens), 1), 1.0, 0.0).astype(BF16)
    rows_e = iota((experts, tokens), 0)
    hot = [jnp.where(ids[k : k + 1] == rows_e, 1.0, 0.0) for k in range(2)]
    earlier = dot_nn((hot[0] + hot[1]).astype(BF16), upper)
    column = iota((experts, 1), 0)
    limit = jnp.zeros((experts, 1), jnp.int32)
    for e in range(experts):
        limit = jnp.where(column == e, cap_ref[e], limit)
    limit = limit.astype(F32)
    rows = []
    for k in range(2):
        place = jnp.sum(hot[k] * earlier, axis=0, keepdims=True)
        top = jnp.sum(hot[k] * limit, axis=0, keepdims=True)
        rows.append(jnp.where(place < top, ids[k : k + 1] * STRIDE + place.astype(jnp.int32), -1))
    return jnp.concatenate(rows, axis=0)


def block_hits(slot_row, block, count):
    codes = iota((count, slot_row.shape[1]), 0) + block * STRIDE
    return jnp.where((slot_row[0:1] == codes) | (slot_row[1:2] == codes), 1.0, 0.0).astype(BF16)


def sort_rows(slots, here, slot_row, rows, send_refs):
    hits = [block_hits(slot_row, here ^ j, slots) for j in range(len(send_refs))]
    sent = dot_nn(jnp.concatenate(hits, axis=0), rows).astype(BF16)
    for j, refs in enumerate(send_refs):
        start = j * slots
        for ref in refs:
            ref[...] = sent[start : start + ref.shape[0]]
            start += ref.shape[0]


def route_body(slots, where_ref, ids_row_ref, cap_ref, grad_ref, ids_ref, col_ref, row_ref, *send_refs):
    ids = ids_row_ref[...]
    slot_row = slots_of(ids, cap_ref)
    row_ref[...] = slot_row
    col_ref[...] = slot_row.astype(F32).T.astype(jnp.int32)
    ids_ref[...] = ids.astype(F32).T.astype(jnp.int32)
    sort_rows(slots, where_ref[1], slot_row, grad_ref[...], [[ref] for ref in send_refs])


def mirror_body(slots, parts, where_ref, cap_ref, grad_ref, *send_refs):
    tokens = grad_ref.shape[0] - PAYLOAD
    ids = grad_ref[tokens:, 0:tokens].astype(F32)[0:2].astype(jnp.int32)
    side = len(send_refs) // parts
    groups = [send_refs[j::side] for j in range(side)]
    sort_rows(slots, where_ref[1], slots_of(ids, cap_ref), grad_ref[0:tokens, :], groups)


def attend_body(half, where_ref, own_ref, other_ref, w_ref,
                q_ref, k_ref, v_ref, log_ref, mine_ref, theirs_ref, rows, mixed, keys, vals):
    core = where_ref[0]
    mine = pl.multiple_of(core * half, half)
    theirs = pl.multiple_of((1 - core) * half, half)
    rows[pl.ds(mine, half), :] = own_ref[...]
    rows[pl.ds(theirs, half), :] = other_ref[...]
    length, width = q_ref.shape
    for part in range(2):
        block = slice(part * half, (part + 1) * half)
        source = rows[block, :]
        q_ref[block, :] = (dot_nt(source, w_ref[0:width, :]) * HD ** (-0.5)).astype(BF16)
        k_ref[block, :] = dot_nt(source, w_ref[width : 2 * width, :]).astype(BF16)
        v_ref[block, :] = dot_nt(source, w_ref[2 * width : 3 * width, :]).astype(BF16)
    heads = width // HD
    lane = iota((1, width), 1)
    triangle = iota((QUERY_ROWS, QUERY_ROWS), 0) >= iota((QUERY_ROWS, QUERY_ROWS), 1)
    for h in range(heads):
        keep = (lane >= h * HD) & (lane < (h + 1) * HD)
        keys[...] = jnp.where(keep, k_ref[...], 0)
        vals[...] = jnp.where(keep, v_ref[...], 0)
        for block in range(length // QUERY_ROWS):
            low = block * QUERY_ROWS
            here = slice(low, low + QUERY_ROWS)
            query = q_ref[here, :]
            diag = jnp.where(triangle, dot_nt(query, keys[here, :]), MASKED_SCORE)
            top = jnp.max(diag, axis=1, keepdims=True)
            if block:
                wide = dot_nt(query, keys[0:low, :])
                top = jnp.maximum(top, jnp.max(wide, axis=1, keepdims=True))
            diag = jnp.exp(diag - top)
            total = jnp.sum(diag, axis=1, keepdims=True)
            result = dot_nn(diag.astype(BF16), vals[here, :])
            if block:
                wide = jnp.exp(wide - top)
                total = total + jnp.sum(wide, axis=1, keepdims=True)
                result = result + dot_nn(wide.astype(BF16), vals[0:low, :])
            result = result / total
            log_ref[here, h : h + 1] = top + jnp.log(total)
            if h:
                result = result + mixed[here, :]
            mixed[here, :] = result
    mine_ref[...] = mixed[pl.ds(mine, half), :].astype(BF16)
    theirs_ref[...] = mixed[pl.ds(theirs, half), :].astype(BF16)


def gates_of(logits, ids_ref, lanes):
    hot = [ids_ref[:, k : k + 1] == lanes for k in range(2)]
    pair = [jnp.sum(jnp.where(hot[k], logits, 0.0), axis=1, keepdims=True) for k in range(2)]
    top = jnp.maximum(pair[0], pair[1])
    raised = [jnp.exp(p - top) for p in pair]
    total = raised[0] + raised[1]
    return [r / total for r in raised]


def split_rows(row, lines):
    high = row.astype(BF16).astype(F32)
    low = row - high
    both = jnp.concatenate([high, low], axis=1)
    return jnp.where(iota((lines, both.shape[1]), 0) == 0, both, 0.0).astype(BF16)


def post_body(experts, size, x_ref, m0, m1, m2, m3, near_ref, w1, far_ref, w3, norms_ref, row_ref,
              resid_ref, normed_ref, send_ref):
    branch = dot_nn(m0[...], near_ref[...]) + dot_nn(m1[...], w1[...])
    branch = branch + (dot_nn(m2[...], far_ref[...]) + dot_nn(m3[...], w3[...]))
    residual = x_ref[...].astype(F32) + branch
    resid_ref[...] = residual
    normal, _ = norm_parts(residual)
    normed = (normal * norms_ref[2:3, :] + norms_ref[3:4, :]).astype(BF16)
    normed_ref[...] = normed
    if size:
        hits = slot_hits(row_ref[...], experts, 0, size)
        send_ref[...] = dot_nn(hits, normed).astype(BF16).reshape(send_ref.shape)


def gate_body(experts, start, size, normed_ref, router_ref, ids_ref, col_ref, row_ref, gates_ref, send_ref):
    normed = normed_ref[...]
    tokens, width = normed.shape
    logits = dot_nt(normed, router_ref[...])
    gates = gates_of(logits, ids_ref, iota((tokens, experts), 1))
    gates_ref[:, 0:1] = gates[0]
    gates_ref[:, 1:2] = gates[1]
    hits = slot_hits(row_ref[...], experts, start, size)
    send_ref[:, 0:size, :] = dot_nn(hits, normed).astype(BF16).reshape(experts, size, width)
    for e in range(experts):
        codes = iota((tokens, STRIDE), 1) + e * STRIDE
        picked = [jnp.where(col_ref[:, k : k + 1] == codes, gates[k], 0.0) for k in range(2)]
        row = jnp.sum(picked[0] + picked[1], axis=0, keepdims=True)
        send_ref[e, size : size + PAYLOAD, 0 : 2 * STRIDE] = split_rows(row, PAYLOAD)
        send_ref[e, size : size + PAYLOAD, 2 * STRIDE :] = jnp.zeros((PAYLOAD, width - 2 * STRIDE), BF16)


def gelu_pair(values):
    square = values * values
    inner = values * (GELU_A + (GELU_A * GELU_B) * square)
    tanh = jnp.tanh(inner)
    half = 0.5 * tanh + 0.5
    slope = half + 0.5 * values * (1.0 - tanh * tanh) * (GELU_A + (3.0 * GELU_A * GELU_B) * square)
    return values * half, slope


def fetch_grads(here, own, mirror, start, size, target, first, sems):
    side = len(own)
    copies = []
    for j in range(side):
        own_part = own[j].at[pl.ds(start, size)]
        for place, ref in ((here ^ j, own_part), ((here ^ j) ^ side, mirror[j])):
            copies.append(pltpu.make_async_copy(ref, target.at[place, pl.ds(first, size)], sems.at[len(copies)]))
    for copy in copies:
        copy.start()
    return copies


def expert_body(shards, sources, start, size, last, where_ref, x_ref, *refs):
    refs = list(refs)
    side = sources // 2

    def take(count):
        taken = refs[:count]
        del refs[:count]
        return taken

    g_own, g_mirror, weights = take(side), take(side), take(shards)
    carry_ref, prior_ref = take(2) if last and start else (None, None)
    hidden_ref, pre_ref, back_ref, rows_ref = take(4)
    carry_out = None if last else take(1)[0]
    win_v, wout_v, hid_v, pre_v, g_v, in_sems, out_sems, g_sems = refs
    arriving = fetch_grads(where_ref[1], g_own, g_mirror, start, size, g_v, 0, g_sems)
    copies = []
    for r in range(shards):
        pair = (pltpu.make_async_copy(weights[r].at[0], win_v.at[r], in_sems.at[2 * r]),
                pltpu.make_async_copy(weights[r].at[1], wout_v.at[r], in_sems.at[2 * r + 1]))
        for copy in pair:
            copy.start()
        copies.append(pair)
    width = x_ref.shape[2]
    rows = sources * size
    x = x_ref[:, 0:size, :].reshape(rows, width)
    for copy in arriving:
        copy.wait()
    g = g_v[...].reshape(rows, width)
    inner = win_v.shape[2]
    step = 256 if inner % 256 == 0 else inner
    score = jnp.zeros((rows, 1), F32)
    total, result = None, None
    outgoing = []
    for r in range(shards):
        for copy in copies[r]:
            copy.wait()
        for f in range(inner // step):
            cols = slice(f * step, (f + 1) * step)
            hid, slope = gelu_pair(dot_nn(x, win_v[r, :, cols]))
            grad = dot_nn(g, wout_v[r, :, cols])
            hid = hid.astype(BF16)
            score = score + jnp.sum(grad * hid.astype(F32), axis=1, keepdims=True)
            hid_v[r, :, cols] = hid
            pre_v[r, :, cols] = (grad * slope).astype(BF16)
        for source, target in ((hid_v, hidden_ref), (pre_v, pre_ref)):
            copy = pltpu.make_async_copy(source.at[r], target.at[r], out_sems.at[len(outgoing)])
            copy.start()
            outgoing.append(copy)
        part, out = dot_nt(pre_v[r], win_v[r]), dot_nt(hid_v[r], wout_v[r])
        total = part if total is None else total + part
        result = out if result is None else result + out
    back = total.astype(BF16).reshape(sources, size, width)
    result = result.astype(BF16).reshape(sources, size, width)
    eye = iota((size, STRIDE), 1) == iota((size, STRIDE), 0) + start
    if last:
        back_ref[:, 0:size, :] = back
        rows_ref[:, start:, :] = result
        if prior_ref is not None:
            rows_ref[:, 0:start, :] = prior_ref[...]
    else:
        back_ref[...] = back
        rows_ref[...] = result
    for s in range(sources):
        row = jnp.sum(jnp.where(eye, score[s * size : (s + 1) * size], 0.0), axis=0, keepdims=True)
        if last:
            if carry_ref is not None:
                row = row + carry_ref[s : s + 1, :]
            back_ref[s, size : size + PAYLOAD, 0 : 2 * STRIDE] = split_rows(row, PAYLOAD)
            back_ref[s, size : size + PAYLOAD, 2 * STRIDE :] = jnp.zeros((PAYLOAD, width - 2 * STRIDE), BF16)
        else:
            carry_out[s : s + 1, :] = row
    for copy in outgoing:
        copy.wait()


def expert_grad_body(picks, shards, sources, sizes, where_ref, *refs):
    refs = list(refs)
    count = len(sizes)

    def take(number):
        taken = refs[:number]
        del refs[:number]
        return taken

    side = sources // 2
    x_refs, g_own, g_mirror = take(count), take(side), [take(side) for _ in range(count)]
    hidden, pre = take(count), take(count)
    home_ref, send_ref = take(2)
    xt, gt, hid_v, pre_v, out_v, g_v, in_sems, out_sems, g_sems = refs
    arriving = []
    for index, size in enumerate(sizes):
        first = sum(sizes[:index])
        arriving += fetch_grads(where_ref[1], g_own, g_mirror[index], first, size, g_v, first, g_sems.at[index])
    copies = []
    for place, r in enumerate(picks):
        base = 0
        group = []
        for index, size in enumerate(sizes):
            rows = sources * size
            for which, (source, target) in enumerate(((pre[index], pre_v), (hidden[index], hid_v))):
                copy = pltpu.make_async_copy(source.at[r], target.at[place, pl.ds(base, rows)],
                                             in_sems.at[(place * count + index) * 2 + which])
                group.append(copy)
            base += rows
        copies.append(group)
    for copy in copies[0]:
        copy.start()
    width = x_refs[0].shape[2]
    last = x_refs[-1]
    for copy in arriving:
        copy.wait()
    start, base = 0, 0
    for ref, size in zip(x_refs, sizes):
        rows = sources * size
        eye = iota((size, STRIDE), 1) == iota((size, STRIDE), 0) + start
        gate = []
        for s in range(sources):
            row = last[s, sizes[-1] : sizes[-1] + PAYLOAD, :].astype(F32)
            row = row[0:1, 0:STRIDE] + row[0:1, STRIDE : 2 * STRIDE]
            gate.append(jnp.sum(jnp.where(eye, row, 0.0), axis=1, keepdims=True))
        gate = jnp.concatenate(gate, axis=0)
        x = ref[:, 0:size, :].reshape(rows, width).astype(F32) * gate
        g = g_v[:, start : start + size, :].reshape(rows, width).astype(F32) * gate
        xt[:, base : base + rows] = x.T.astype(BF16)
        gt[:, base : base + rows] = g.T.astype(BF16)
        start += size
        base += rows
    outgoing = []
    for place, r in enumerate(picks):
        for copy in copies[place]:
            copy.wait()
        for copy in copies[place + 1] if place + 1 < len(picks) else ():
            copy.start()
        for which, (left, right) in enumerate(((xt, pre_v), (gt, hid_v))):
            out_v[place, which] = dot_nn(left[...], right[place]).astype(BF16)
            target = (send_ref if r % 2 else home_ref).at[r // 2, which]
            copy = pltpu.make_async_copy(out_v.at[place, which], target, out_sems.at[2 * place + which])
            copy.start()
            outgoing.append(copy)
    for copy in outgoing:
        copy.wait()


def grad_sum_body(keep_ref, home_ref, got_ref, early_ref, late_ref, *out_refs):
    early, width = early_ref.shape[0], out_refs[0].shape[0]
    spans = [(0, 0, early, early_ref, 0), (0, early, width, late_ref, 0), (1, 0, width, late_ref, width - early)]
    for index, start, stop, ref, first in spans:
        total = home_ref[0, index, start:stop].astype(F32) + got_ref[0, index, start:stop].astype(F32)
        last = ref[first : first + stop - start, :].astype(F32)
        out_refs[index][start:stop, :] = (total + last) * keep_ref[0, 0]


def gather_body(rows_ref, codes_ref, col_ref, gates_ref, sum_ref):
    sources, size, width = rows_ref.shape
    codes = codes_ref[...]
    pick = jnp.where(col_ref[:, 0:1] == codes, gates_ref[:, 0:1], 0.0)
    pick = jnp.where(col_ref[:, 1:2] == codes, gates_ref[:, 1:2], pick).astype(BF16)
    sum_ref[...] = dot_nn(pick, rows_ref[...].reshape(sources * size, width))


def second_back_body(experts, size, has_sum, *refs):
    refs = list(refs)
    (rows_ref, codes_ref, col_ref, gates_ref, ids_ref, resid_ref, normed_ref, cot_ref, norms_ref, router_ref) = refs[:10]
    del refs[:10]
    sum_ref = refs.pop(0) if has_sum else None
    grad_ref, branch_ref, small_ref = refs
    sources, _, width = rows_ref.shape
    tokens = resid_ref.shape[0]
    codes = codes_ref[...]
    gates = [gates_ref[:, k : k + 1] for k in range(2)]
    slot = [col_ref[:, k : k + 1] for k in range(2)]
    pick = jnp.where(slot[0] == codes, gates[0], 0.0)
    pick = jnp.where(slot[1] == codes, gates[1], pick).astype(BF16)
    total = dot_nn(pick, rows_ref[:, 0:size, :].reshape(sources * size, width))
    if sum_ref is not None:
        total = total + sum_ref[...]
    scores = [jnp.zeros((tokens, 1), F32), jnp.zeros((tokens, 1), F32)]
    for e in range(experts):
        line = rows_ref[e, size : size + PAYLOAD, :].astype(F32)
        line = line[0:1, 0:STRIDE] + line[0:1, STRIDE : 2 * STRIDE]
        place = iota((tokens, STRIDE), 1) + e * STRIDE
        for k in range(2):
            scores[k] = scores[k] + jnp.sum(jnp.where(slot[k] == place, line, 0.0), axis=1, keepdims=True)
    inner = gates[0] * scores[0] + gates[1] * scores[1]
    lanes = iota((tokens, experts), 1)
    logit_grad = jnp.zeros((tokens, experts), F32)
    for k in range(2):
        logit_grad = jnp.where(ids_ref[:, k : k + 1] == lanes, gates[k] * (scores[k] - inner), logit_grad)
    logit_grad = logit_grad.astype(BF16)
    total = total + dot_nn(logit_grad, router_ref[...])
    normal, rate = norm_parts(resid_ref[...])
    grad = cot_ref[...].astype(F32) + norm_back(normal, rate, norms_ref[2:3, :], total)
    grad_ref[...] = grad
    branch_ref[...] = grad.astype(BF16)
    small_ref[0:1, :] = jnp.sum(total * normal, axis=0, keepdims=True)
    small_ref[1:2, :] = jnp.sum(total, axis=0, keepdims=True)
    small_ref[2 : 2 + experts, :] = dot_tn(logit_grad, normed_ref[...])


def attend_back_body(half, has_sum, where_ref, *refs):
    refs = list(refs)
    (q_ref, k_ref, v_ref, log_ref, mixed_own, mixed_other, branch_own, branch_other, own_ref, other_ref,
     w_ref) = refs[:11]
    del refs[:11]
    sums = (refs.pop(0), refs.pop(0)) if has_sum else None
    weight_ref, mine_ref, theirs_ref, rows, branch, grads, mixed, keys, vals, dq, dk, dv, joined, pile = refs
    core = where_ref[0]
    mine = pl.multiple_of(core * half, half)
    theirs = pl.multiple_of((1 - core) * half, half)
    rows[pl.ds(mine, half), :] = own_ref[...]
    rows[pl.ds(theirs, half), :] = other_ref[...]
    branch[pl.ds(mine, half), :] = branch_own[...]
    branch[pl.ds(theirs, half), :] = branch_other[...]
    mixed[pl.ds(mine, half), :] = mixed_own[...]
    mixed[pl.ds(theirs, half), :] = mixed_other[...]
    length, width = q_ref.shape
    grads[...] = dot_nt(branch[...], w_ref[3 * width :, :]).astype(BF16)
    heads = width // HD
    lane = iota((1, width), 1)
    triangle = iota((QUERY_ROWS, QUERY_ROWS), 0) >= iota((QUERY_ROWS, QUERY_ROWS), 1)
    qt = q_ref[...].astype(F32).T.astype(BF16)
    gt = grads[...].astype(F32).T.astype(BF16)
    dk[...] = jnp.zeros(dk.shape, F32)
    dv[...] = jnp.zeros(dv.shape, F32)
    for h in range(heads):
        keep = (lane >= h * HD) & (lane < (h + 1) * HD)
        keys[...] = jnp.where(keep, k_ref[...], 0)
        vals[...] = jnp.where(keep, v_ref[...], 0)
        head = slice(h * HD, (h + 1) * HD)
        for block in range(length // QUERY_ROWS):
            low = block * QUERY_ROWS
            here = slice(low, low + QUERY_ROWS)
            query, grad, log = q_ref[here, :], grads[here, :], log_ref[here, h : h + 1]
            spans = [slice(0, low)] if block else []
            spans.append(here)
            probs, outer = [], []
            inner = None
            for span in spans:
                score = dot_nt(query, keys[span, :])
                if span is here:
                    score = jnp.where(triangle, score, MASKED_SCORE)
                prob = jnp.exp(score - log)
                grad_prob = dot_nt(grad, vals[span, :])
                part = jnp.sum(prob * grad_prob, axis=1, keepdims=True)
                inner = part if inner is None else inner + part
                probs.append(prob)
                outer.append(grad_prob)
            query_grad = None
            for span, prob, grad_prob in zip(spans, probs, outer):
                score_grad = (prob * (grad_prob - inner)).astype(BF16)
                part = dot_nn(score_grad, keys[span, :])
                query_grad = part if query_grad is None else query_grad + part
                dv[head, span] = dv[head, span] + dot_nn(gt[head, here], prob.astype(BF16))
                dk[head, span] = dk[head, span] + dot_nn(qt[head, here], score_grad)
            if h:
                query_grad = query_grad + dq[here, :]
            dq[here, :] = query_grad
    query_grads = dq[...].astype(BF16).astype(F32) * HD ** (-0.5)
    joined[0:width, :] = query_grads.T.astype(BF16)
    joined[width : 2 * width, :] = dk[...].astype(BF16)
    joined[2 * width : 3 * width, :] = dv[...].astype(BF16)
    total = dot_nn(query_grads.astype(BF16), w_ref[0:width, :])
    total = total + dot_nn(dk[...].T.astype(BF16), w_ref[width : 2 * width, :])
    total = total + dot_nn(dv[...].T.astype(BF16), w_ref[2 * width : 3 * width, :])
    pile[...] = total
    one, two = pile[pl.ds(mine, half), :], pile[pl.ds(theirs, half), :]
    if sums is not None:
        one, two = one + sums[0][...], two + sums[1][...]
    mine_ref[...] = one.astype(mine_ref.dtype)
    theirs_ref[...] = two.astype(theirs_ref.dtype)
    weight_ref[0 : 3 * width, :] = dot_nn(joined[...], rows[...]).astype(weight_ref.dtype)
    turned = mixed[...].astype(F32).T.astype(BF16)
    weight_ref[3 * width :, :] = dot_nn(turned, branch[...]).astype(weight_ref.dtype)


def first_back_body(x_ref, norms_ref, mine_ref, other_ref, resid_ref, out_ref, small_ref):
    grad = mine_ref[...] + other_ref[...].astype(F32)
    normal, rate = norm_parts(x_ref[...].astype(F32))
    out_ref[...] = resid_ref[...] + norm_back(normal, rate, norms_ref[0:1, :], grad)
    small_ref[0:1, :] = jnp.sum(grad * normal, axis=0, keepdims=True)
    small_ref[1:2, :] = jnp.sum(grad, axis=0, keepdims=True)


def block_out_body(rows_ref, codes_ref, col_ref, gates_ref, resid_ref, out_ref):
    sources, size, width = rows_ref.shape
    codes = codes_ref[...]
    pick = jnp.where(col_ref[:, 0:1] == codes, gates_ref[:, 0:1], 0.0)
    pick = jnp.where(col_ref[:, 1:2] == codes, gates_ref[:, 1:2], pick).astype(BF16)
    moe = dot_nn(pick, rows_ref[...].reshape(sources * size, width))
    out_ref[...] = (resid_ref[...] + moe).astype(BF16)


def split_body(where_ref, near_ref, far_ref, *out_refs):
    side = len(out_refs)
    rows = out_refs[0].shape[1]
    here = where_ref[1]
    for j, ref in enumerate(out_refs):
        for place, block in enumerate((here ^ j, (here ^ j) ^ side)):
            part = pl.ds(pl.multiple_of(block * rows, rows), rows)
            ref[place] = (near_ref[part, :] + far_ref[part, :].astype(F32)).astype(BF16)


def half_sum_body(*refs):
    keep_ref, send_ref = refs[-2:]
    for place, out in enumerate((keep_ref, send_ref)):
        total = refs[0][place].astype(F32)
        for ref in refs[1:-2]:
            total = total + ref[place].astype(F32)
        out[...] = total.astype(out.dtype)


def final_body(where_ref, *refs):
    all_rows = refs[-1]
    pairs, outs = refs[:-5], refs[-5:-1]
    side = len(pairs)
    rows = pairs[0].shape[1]
    here = where_ref[1]
    for j in range(side):
        for place, block in enumerate((here ^ j, (here ^ j) ^ side)):
            part = pl.ds(pl.multiple_of(block * rows, rows), rows)
            all_rows[part, :] = pairs[j][place].astype(F32)
    count = outs[0].shape[0]
    for index, ref in enumerate(outs):
        ref[...] = all_rows[index * count : (index + 1) * count, :]


def swap(value, axis, step):
    size = lax.axis_size(axis)
    return lax.ppermute(value, axis, [(i, i ^ step) for i in range(size)])


def exchange(value):
    return lax.all_to_all(value, "dp", split_axis=0, concat_axis=0, tiled=True)


def after(value, *others):
    return lax.optimization_barrier((value,) + others)[0]


def codes_of(experts, start, size):
    table = np.arange(experts)[:, None] * STRIDE + start + np.arange(size)[None, :]
    return jnp.asarray(table.reshape(1, -1).astype(np.int32))


def per_device(activations, first_gain, first_shift, query_weight, key_weight, value_weight, output_weight,
               second_gain, second_shift, router_weight, expert_in, expert_out, expert_ids, capacity, new_mask,
               cotangent):
    kernel = functools.partial(call, pins=[activations, output_weight, cotangent])
    tokens, width = activations.shape
    local = query_weight.shape[1]
    heads = local // HD
    experts = router_weight.shape[1]
    sources = lax.axis_size("dp")
    shards = lax.axis_size("head")
    slots = 3 * tokens // experts
    sizes = (slots // 32 * 16, slots - slots // 32 * 16) if slots % 16 == 0 and slots >= 32 else (slots,)
    starts = tuple(sum(sizes[:i]) for i in range(len(sizes)))
    length, half, side = LENGTH, tokens, sources // 2
    where = jnp.stack([lax.axis_index("head") % 2, lax.axis_index("dp")]).astype(jnp.int32)
    last_rows = pl.BlockSpec((local, width), lambda i: (3, 0))

    attn_w = jnp.concatenate([query_weight.T, key_weight.T, value_weight.T, output_weight], axis=0)
    far_w = swap(attn_w, "head", 2)
    norms = jnp.stack([first_gain, first_shift, second_gain, second_shift])
    router = router_weight.T

    normed_first = kernel(first_norm_body, [sds((tokens, width), BF16)], "norm_first", (activations, norms), vmem=16)[0]
    normed_other = swap(normed_first, "head", 1)

    ids_row = expert_ids.T
    extra = jnp.pad(ids_row.astype(BF16), ((0, PAYLOAD - 2), (0, width - tokens)))
    mirror_grad = swap(jnp.concatenate([cotangent, extra], axis=0), "dp", side)
    routed = kernel(
        functools.partial(route_body, slots),
        [sds((tokens, 2), jnp.int32), sds((tokens, 2), jnp.int32), sds((2, tokens), jnp.int32)]
        + [sds((slots, width), BF16)] * side,
        "route", (where, ids_row, capacity, cotangent), smem=(0, 2))
    ids_col, slot_col, slot_row = routed[:3]
    grad_own = [routed[3]] + [swap(routed[3 + j], "dp", j) for j in range(1, side)]

    def attend(weight):
        return kernel(
            functools.partial(attend_body, half),
            [sds((length, local), BF16)] * 3 + [sds((length, heads), F32)] + [sds((half, local), BF16)] * 2,
            "attend", (where, normed_first, normed_other, weight), smem=(0,),
            scratch=[pltpu.VMEM((length, width), BF16), pltpu.VMEM((length, local), F32),
                     pltpu.VMEM((length, local), BF16), pltpu.VMEM((length, local), BF16)])

    near = attend(attn_w)
    mixed = {0: near[4], 1: swap(near[5], "head", 1)}
    far_w = after(far_w, near[4], slot_row)
    away = attend(far_w)
    mixed[2], mixed[3] = away[4], swap(away[5], "head", 1)
    out_w = {1: swap(output_weight, "head", 1), 3: swap(far_w[3 * local :], "head", 1)}

    weights = {0: jnp.stack([expert_in[0], expert_out[0]])}
    weights[1] = swap(weights[0], "head", 1)
    weights[2] = swap(after(weights[0], far_w), "head", 2)
    inner = weights[0].shape[2]

    mirror_send = kernel(
        functools.partial(mirror_body, slots, len(sizes)),
        [sds((size, width), BF16) for size in sizes for _ in range(side)], "mirror",
        (where, capacity, mirror_grad), smem=(0, 1))
    grad_mirror = []
    for index in range(len(sizes)):
        group = mirror_send[index * side : (index + 1) * side]
        grad_mirror.append([group[0]] + [swap(group[j], "dp", j) for j in range(1, side)])

    first_size = sizes[0] if len(sizes) > 1 else 0
    residual, normed_second, sent = kernel(
        functools.partial(post_body, experts, first_size),
        [sds((tokens, width), F32), sds((tokens, width), BF16), sds((experts, max(first_size, 16), width), BF16)],
        "post_attend",
        (activations, mixed[0], mixed[1], mixed[2], mixed[3], output_weight, out_w[1], far_w, out_w[3], norms,
         after(slot_row, mirror_grad, *grad_own[1:])), blocks={7: last_rows}, vmem=32)
    gates, sent_last = kernel(
        functools.partial(gate_body, experts, starts[-1], sizes[-1]),
        [sds((tokens, 2), F32), sds((experts, sizes[-1] + PAYLOAD, width), BF16)],
        "gates", (normed_second, router, ids_col, slot_col, slot_row))
    weights[3] = swap(after(weights[2], sent_last), "head", 1)
    rows_in = []
    if first_size:
        rows_in.append(exchange(sent))
    sent_last = after(sent_last, weights[2], *(rows_in + grad_mirror[0][1:]))
    rows_in.append(exchange(sent_last))

    hidden, pre, back = [], [], []
    carry = ()
    for index, size in enumerate(sizes):
        last = index == len(sizes) - 1
        rows = sources * size
        kept = slots if last else size
        outs = [sds((shards, rows, inner), BF16), sds((shards, rows, inner), BF16),
                sds((sources, size + (PAYLOAD if last else 0), width), BF16), sds((sources, kept, width), BF16)]
        ins = (where, rows_in[index]) + tuple(grad_own) + tuple(grad_mirror[index])
        first = len(ins)
        ins = ins + tuple(weights[r] for r in range(shards)) + carry
        if not last:
            outs.append(sds((sources, STRIDE), F32))
        result = kernel(
            functools.partial(expert_body, shards, sources, starts[index], size, last), outs, "expert", ins,
            vmem=60 if rows <= 768 else 62, smem=(0,), hbm=tuple(range(2, first + shards)), free=(2,),
            out_hbm=(0, 1),
            scratch=[pltpu.VMEM((shards, width, inner), BF16), pltpu.VMEM((shards, width, inner), BF16),
                     pltpu.VMEM((shards, rows, inner), BF16), pltpu.VMEM((shards, rows, inner), BF16),
                     pltpu.VMEM((sources, size, width), BF16), pltpu.SemaphoreType.DMA((2 * shards,)),
                     pltpu.SemaphoreType.DMA((2 * shards,)), pltpu.SemaphoreType.DMA((sources,))])
        hidden.append(result[0])
        pre.append(result[1])
        back.append(result[2])
        expert_rows = result[3]
        if not last:
            carry = (result[4], result[3])
    returned, done = [], rows_in[-1]
    for index, part in enumerate(back):
        done = exchange(after(part, done, *(grad_mirror[-1][1:] if index == 0 else ())))
        returned.append(done)

    partial_sums = ()
    if first_size:
        partial_sums = tuple(kernel(
            gather_body, [sds((tokens, width), F32)], "gather_back",
            (returned[0], codes_of(experts, 0, first_size), slot_col, gates)))

    keep = jnp.sum(jnp.where(jnp.arange(experts) == lax.axis_index("dp"), new_mask, 0)).astype(F32).reshape(1, 1)
    all_rows = sources * slots
    picks = tuple(range(1, shards, 2)) + tuple(range(0, shards, 2))
    skip = 1 + len(sizes)
    grads_home, grads_send = kernel(
        functools.partial(expert_grad_body, picks, shards, sources, sizes),
        [sds((shards // 2, 2, width, inner), BF16)] * 2, "expert_grads",
        (after(where, *partial_sums),) + tuple(rows_in) + tuple(grad_own) + sum(map(tuple, grad_mirror), ()) + tuple(hidden) + tuple(pre), vmem=60,
        smem=(0,), hbm=tuple(range(skip, skip + side * (1 + len(sizes)) + 2 * len(sizes))), out_hbm=(0, 1),
        scratch=[pltpu.VMEM((width, all_rows), BF16), pltpu.VMEM((width, all_rows), BF16),
                 pltpu.VMEM((shards, all_rows, inner), BF16), pltpu.VMEM((shards, all_rows, inner), BF16),
                 pltpu.VMEM((shards, 2, width, inner), BF16), pltpu.VMEM((sources, slots, width), BF16),
                 pltpu.SemaphoreType.DMA((4 * shards,)), pltpu.SemaphoreType.DMA((2 * shards,)),
                 pltpu.SemaphoreType.DMA((len(sizes), sources))])
    grads_got = swap(after(grads_send, returned[-1]), "head", 1)

    grad_residual, grad_branch, small_two = kernel(
        functools.partial(second_back_body, experts, sizes[-1], bool(partial_sums)),
        [sds((tokens, width), F32), sds((tokens, width), BF16), sds((2 + experts, width), F32)], "second_back",
        (returned[-1], codes_of(experts, starts[-1], sizes[-1]), slot_col, gates, ids_col, residual,
         normed_second, cotangent, norms, router) + partial_sums, free=(1, 2))
    branch_other = swap(grad_branch, "head", 1)

    early = width // 2

    def pass_on(start, stop):
        parts = [g[1].reshape(2 * width, inner)[start:stop].astype(F32) for g in (grads_home, grads_got)]
        return (parts[0] + parts[1]).astype(BF16)

    passed_first = pass_on(0, early)
    branch_other = after(branch_other, passed_first)
    passed_first = swap(passed_first, "head", 2)

    def attend_back(parts, mixed_other, weight, sums, weight_type, types):
        return kernel(
            functools.partial(attend_back_body, half, bool(sums)),
            [sds((4 * local, width), weight_type), sds((half, width), types[0]), sds((half, width), types[1])],
            "attend_back",
            (where,) + tuple(parts[:4]) + (parts[4], parts[5], grad_branch, branch_other, normed_first, normed_other,
                                           weight) + tuple(sums),
            smem=(0,), vmem=32, free=(0, 1, 2),
            scratch=[pltpu.VMEM((length, width), BF16), pltpu.VMEM((length, width), BF16),
                     pltpu.VMEM((length, local), BF16), pltpu.VMEM((length, local), BF16),
                     pltpu.VMEM((length, local), BF16), pltpu.VMEM((length, local), BF16),
                     pltpu.VMEM((length, local), F32), pltpu.VMEM((local, length), F32),
                     pltpu.VMEM((local, length), F32), pltpu.VMEM((3 * local, length), BF16),
                     pltpu.VMEM((length, width), F32)])

    far_grad, far_mine, far_theirs = attend_back(away, mixed[3], far_w, (), BF16, (F32, F32))
    far_got = swap(far_grad, "head", 2)
    branch_other = after(branch_other, passed_first)
    near_grad, near_mine, near_theirs = attend_back(near, mixed[1], attn_w, (far_mine, far_theirs), F32, (F32, BF16))
    rows_back = exchange(after(expert_rows, returned[-1], grads_home, *partial_sums))
    block_out = kernel(
        block_out_body, [sds((tokens, width), BF16)], "block_out",
        (rows_back, codes_of(experts, 0, slots), slot_col, gates, residual))[0]

    passed = pass_on(early, 2 * width)
    near_grad = after(near_grad, passed)
    passed = swap(after(passed, far_got, near_grad), "head", 2)
    block_rows = 4 * local // sources
    split = kernel(
        split_body, [sds((2, block_rows, width), BF16)] * side, "split", (where, near_grad, far_got), smem=(0,))
    split = [split[0]] + [swap(split[j], "dp", j) for j in range(1, side)]
    first_got = swap(near_theirs, "head", 1)
    grad_input, small_one = kernel(
        first_back_body, [sds((tokens, width), F32), sds((2, width), F32)], "first_back",
        (activations, norms, after(near_mine, split[0]), first_got, grad_residual))
    small = jnp.concatenate([small_one, small_two], axis=0)
    small = jnp.pad(small, ((0, -small.shape[0] % 8), (0, 0)))
    small = small + swap(small, "head", 1)
    own_sum, cross_sum = kernel(
        half_sum_body, [sds((block_rows, width), F32), sds((block_rows, width), BF16)], "half_sum",
        (after(split[0], small, block_out),) + tuple(split[1:]))
    cross_got = swap(cross_sum, "dp", side)
    small = small + swap(small, "dp", 1)
    reduced = (after(own_sum, small) + cross_got.astype(F32)).astype(BF16)
    small = small + swap(small, "dp", 2)
    pair = jnp.stack([reduced, after(swap(reduced, "dp", side), small)])
    pairs = [pair] + [swap(pair, "dp", j) for j in range(1, side)]
    step = 4
    while step < sources:
        small = small + swap(small, "dp", step)
        step *= 2

    part = pl.BlockSpec((1, 2, width, inner), lambda i: (0, 0, 0, 0))
    grad_in, grad_out = kernel(
        grad_sum_body, [sds((width, inner), F32), sds((width, inner), F32)], "grad_sum",
        (keep, grads_home, grads_got, passed_first, passed), smem=(0,), vmem=40, blocks={1: part, 2: part})

    small = small + swap(after(small, passed), "head", 2)
    pairs[0] = after(pairs[0], grad_in)
    final = kernel(
        final_body, [sds((local, width), F32)] * 4, "final", (where,) + tuple(pairs), smem=(0,),
        scratch=[pltpu.VMEM((4 * local, width), F32)])
    mask = new_mask.astype(F32)[None, :]
    return (
        block_out,
        grad_input,
        small[0],
        small[1],
        final[0].T,
        final[1].T,
        final[2].T,
        final[3],
        small[2],
        small[3],
        small[4 : 4 + experts].T * mask,
        grad_in[None],
        grad_out[None],
    )


def solution(mesh):
    placed = (
        P(("dp", "head"), None),
        P(),
        P(),
        P(None, "head"),
        P(None, "head"),
        P(None, "head"),
        P("head", None),
        P(),
        P(),
        P(),
        P("dp", None, "head"),
        P("dp", None, "head"),
        P(("dp", "head"), None),
        P(),
        P(),
        P(("dp", "head"), None),
    )
    return jax.shard_map(
        per_device,
        mesh=mesh,
        in_specs=placed,
        out_specs=(
            P(("dp", "head"), None),
            P(("dp", "head"), None),
            P(),
            P(),
            P(None, "head"),
            P(None, "head"),
            P(None, "head"),
            P("head", None),
            P(),
            P(),
            P(),
            P("dp", None, "head"),
            P("dp", None, "head"),
        ),
        check_vma=False,
    )
```

```python
import functools

import jax
import jax.numpy as jnp
import numpy as np
from jax import lax
from jax.experimental import pallas as pl
from jax.experimental.pallas import tpu as pltpu
from jax.sharding import PartitionSpec as P

HD = 64
LENGTH = 1024
NORM_EPSILON = 1e-05
MASKED_SCORE = -1e30
QUERY_ROWS = 256
STRIDE = 256
PAYLOAD = 16
MIB = 1 << 20
F32 = jnp.float32
BF16 = jnp.bfloat16
GELU_A = 0.7978845608028654
GELU_B = 0.044715


def dot_nn(left, right):
    return lax.dot_general(left, right, (((1,), (0,)), ((), ())), preferred_element_type=F32)


def dot_nt(left, right):
    return lax.dot_general(left, right, (((1,), (1,)), ((), ())), preferred_element_type=F32)


def dot_tn(left, right):
    return lax.dot_general(left, right, (((0,), (0,)), ((), ())), preferred_element_type=F32)


def iota(shape, axis):
    return lax.broadcasted_iota(jnp.int32, shape, axis)


def call(body, outs, name, ins, vmem=24, scratch=(), smem=(), hbm=(), free=(), out_hbm=(), pins=None, blocks=None):
    specs, given = [], []
    blocks = blocks or {}
    for index, value in enumerate(ins):
        if index in smem:
            specs.append(pl.BlockSpec(memory_space=pltpu.SMEM))
        elif index in hbm:
            specs.append(pl.BlockSpec(memory_space=pltpu.HBM))
        elif index in blocks:
            specs.append(blocks[index])
        else:
            specs.append(pl.BlockSpec())
        if index not in smem and any(value is p for p in pins):
            value = pltpu.with_memory_space_constraint(value, pltpu.HBM)
        given.append(value)
    results = pl.pallas_call(
        body,
        grid=(1,) if blocks else (),
        out_shape=[o if i in free else pltpu.HBM(o.shape, o.dtype) for i, o in enumerate(outs)],
        in_specs=specs,
        out_specs=[pl.BlockSpec(memory_space=pltpu.HBM) if i in out_hbm else pl.BlockSpec() for i in range(len(outs))],
        scratch_shapes=list(scratch),
        compiler_params=pltpu.CompilerParams(vmem_limit_bytes=vmem * MIB),
        cost_estimate=pl.CostEstimate(flops=1, bytes_accessed=1, transcendentals=0),
        name=name,
    )(*given)
    pins.extend(r for i, r in enumerate(results) if i not in free)
    return results


def sds(shape, dtype):
    return jax.ShapeDtypeStruct(shape, dtype)


def norm_parts(values):
    center = jnp.mean(values, axis=1, keepdims=True)
    centered = values - center
    rate = lax.rsqrt(jnp.mean(centered * centered, axis=1, keepdims=True) + NORM_EPSILON)
    return centered * rate, rate


def norm_back(normal, rate, gain, grad):
    scaled = grad * gain
    first = jnp.mean(scaled, axis=1, keepdims=True)
    second = jnp.mean(scaled * normal, axis=1, keepdims=True)
    return rate * (scaled - first - normal * second)


def first_norm_body(x_ref, norms_ref, out_ref):
    normal, _ = norm_parts(x_ref[...].astype(F32))
    out_ref[...] = (normal * norms_ref[0:1, :] + norms_ref[1:2, :]).astype(BF16)


def slot_hits(slot_row, experts, start, count):
    tokens = slot_row.shape[1]
    parts = []
    for e in range(experts):
        codes = iota((count, tokens), 0) + (e * STRIDE + start)
        hit = (slot_row[0:1] == codes) | (slot_row[1:2] == codes)
        parts.append(jnp.where(hit, 1.0, 0.0))
    return jnp.concatenate(parts, axis=0).astype(BF16)


def slots_of(ids, cap_ref):
    tokens = ids.shape[1]
    experts = cap_ref.shape[0]
    upper = jnp.where(iota((tokens, tokens), 0) < iota((tokens, tokens), 1), 1.0, 0.0).astype(BF16)
    rows_e = iota((experts, tokens), 0)
    hot = [jnp.where(ids[k : k + 1] == rows_e, 1.0, 0.0) for k in range(2)]
    earlier = dot_nn((hot[0] + hot[1]).astype(BF16), upper)
    column = iota((experts, 1), 0)
    limit = jnp.zeros((experts, 1), jnp.int32)
    for e in range(experts):
        limit = jnp.where(column == e, cap_ref[e], limit)
    limit = limit.astype(F32)
    rows = []
    for k in range(2):
        place = jnp.sum(hot[k] * earlier, axis=0, keepdims=True)
        top = jnp.sum(hot[k] * limit, axis=0, keepdims=True)
        rows.append(jnp.where(place < top, ids[k : k + 1] * STRIDE + place.astype(jnp.int32), -1))
    return jnp.concatenate(rows, axis=0)


def block_hits(slot_row, block, count):
    codes = iota((count, slot_row.shape[1]), 0) + block * STRIDE
    return jnp.where((slot_row[0:1] == codes) | (slot_row[1:2] == codes), 1.0, 0.0).astype(BF16)


def sort_rows(slots, here, slot_row, rows, send_refs):
    hits = [block_hits(slot_row, here ^ j, slots) for j in range(len(send_refs))]
    sent = dot_nn(jnp.concatenate(hits, axis=0), rows).astype(BF16)
    for j, refs in enumerate(send_refs):
        start = j * slots
        for ref in refs:
            ref[...] = sent[start : start + ref.shape[0]]
            start += ref.shape[0]


def route_body(slots, where_ref, ids_row_ref, cap_ref, grad_ref, ids_ref, col_ref, row_ref, *send_refs):
    ids = ids_row_ref[...]
    slot_row = slots_of(ids, cap_ref)
    row_ref[...] = slot_row
    col_ref[...] = slot_row.astype(F32).T.astype(jnp.int32)
    ids_ref[...] = ids.astype(F32).T.astype(jnp.int32)
    sort_rows(slots, where_ref[1], slot_row, grad_ref[...], [[ref] for ref in send_refs])


def mirror_body(slots, parts, where_ref, cap_ref, grad_ref, *send_refs):
    tokens = grad_ref.shape[0] - PAYLOAD
    ids = grad_ref[tokens:, 0:tokens].astype(F32)[0:2].astype(jnp.int32)
    side = len(send_refs) // parts
    groups = [send_refs[j::side] for j in range(side)]
    sort_rows(slots, where_ref[1], slots_of(ids, cap_ref), grad_ref[0:tokens, :], groups)


def attend_body(half, where_ref, own_ref, other_ref, w_ref,
                q_ref, k_ref, v_ref, log_ref, mine_ref, theirs_ref, rows, mixed, keys, vals):
    core = where_ref[0]
    mine = pl.multiple_of(core * half, half)
    theirs = pl.multiple_of((1 - core) * half, half)
    rows[pl.ds(mine, half), :] = own_ref[...]
    rows[pl.ds(theirs, half), :] = other_ref[...]
    length, width = q_ref.shape
    for part in range(2):
        block = slice(part * half, (part + 1) * half)
        source = rows[block, :]
        q_ref[block, :] = (dot_nt(source, w_ref[0:width, :]) * HD ** (-0.5)).astype(BF16)
        k_ref[block, :] = dot_nt(source, w_ref[width : 2 * width, :]).astype(BF16)
        v_ref[block, :] = dot_nt(source, w_ref[2 * width : 3 * width, :]).astype(BF16)
    heads = width // HD
    lane = iota((1, width), 1)
    triangle = iota((QUERY_ROWS, QUERY_ROWS), 0) >= iota((QUERY_ROWS, QUERY_ROWS), 1)
    for h in range(heads):
        keep = (lane >= h * HD) & (lane < (h + 1) * HD)
        keys[...] = jnp.where(keep, k_ref[...], 0)
        vals[...] = jnp.where(keep, v_ref[...], 0)
        for block in range(length // QUERY_ROWS):
            low = block * QUERY_ROWS
            here = slice(low, low + QUERY_ROWS)
            query = q_ref[here, :]
            diag = jnp.where(triangle, dot_nt(query, keys[here, :]), MASKED_SCORE)
            top = jnp.max(diag, axis=1, keepdims=True)
            if block:
                wide = dot_nt(query, keys[0:low, :])
                top = jnp.maximum(top, jnp.max(wide, axis=1, keepdims=True))
            diag = jnp.exp(diag - top)
            total = jnp.sum(diag, axis=1, keepdims=True)
            result = dot_nn(diag.astype(BF16), vals[here, :])
            if block:
                wide = jnp.exp(wide - top)
                total = total + jnp.sum(wide, axis=1, keepdims=True)
                result = result + dot_nn(wide.astype(BF16), vals[0:low, :])
            result = result / total
            log_ref[here, h : h + 1] = top + jnp.log(total)
            if h:
                result = result + mixed[here, :]
            mixed[here, :] = result
    mine_ref[...] = mixed[pl.ds(mine, half), :].astype(BF16)
    theirs_ref[...] = mixed[pl.ds(theirs, half), :].astype(BF16)


def gates_of(logits, ids_ref, lanes):
    hot = [ids_ref[:, k : k + 1] == lanes for k in range(2)]
    pair = [jnp.sum(jnp.where(hot[k], logits, 0.0), axis=1, keepdims=True) for k in range(2)]
    top = jnp.maximum(pair[0], pair[1])
    raised = [jnp.exp(p - top) for p in pair]
    total = raised[0] + raised[1]
    return [r / total for r in raised]


def split_rows(row, lines):
    high = row.astype(BF16).astype(F32)
    low = row - high
    both = jnp.concatenate([high, low], axis=1)
    return jnp.where(iota((lines, both.shape[1]), 0) == 0, both, 0.0).astype(BF16)


def post_body(experts, size, x_ref, m0, m1, m2, m3, near_ref, w1, far_ref, w3, norms_ref, row_ref,
              resid_ref, normed_ref, send_ref):
    branch = dot_nn(m0[...], near_ref[...]) + dot_nn(m1[...], w1[...])
    branch = branch + (dot_nn(m2[...], far_ref[...]) + dot_nn(m3[...], w3[...]))
    residual = x_ref[...].astype(F32) + branch
    resid_ref[...] = residual
    normal, _ = norm_parts(residual)
    normed = (normal * norms_ref[2:3, :] + norms_ref[3:4, :]).astype(BF16)
    normed_ref[...] = normed
    if size:
        hits = slot_hits(row_ref[...], experts, 0, size)
        send_ref[...] = dot_nn(hits, normed).astype(BF16).reshape(send_ref.shape)


def gate_body(experts, start, size, normed_ref, router_ref, ids_ref, col_ref, row_ref, gates_ref, send_ref):
    normed = normed_ref[...]
    tokens, width = normed.shape
    logits = dot_nt(normed, router_ref[...])
    gates = gates_of(logits, ids_ref, iota((tokens, experts), 1))
    gates_ref[:, 0:1] = gates[0]
    gates_ref[:, 1:2] = gates[1]
    hits = slot_hits(row_ref[...], experts, start, size)
    send_ref[:, 0:size, :] = dot_nn(hits, normed).astype(BF16).reshape(experts, size, width)
    for e in range(experts):
        codes = iota((tokens, STRIDE), 1) + e * STRIDE
        picked = [jnp.where(col_ref[:, k : k + 1] == codes, gates[k], 0.0) for k in range(2)]
        row = jnp.sum(picked[0] + picked[1], axis=0, keepdims=True)
        send_ref[e, size : size + PAYLOAD, 0 : 2 * STRIDE] = split_rows(row, PAYLOAD)
        send_ref[e, size : size + PAYLOAD, 2 * STRIDE :] = jnp.zeros((PAYLOAD, width - 2 * STRIDE), BF16)


def gelu_pair(values):
    square = values * values
    inner = values * (GELU_A + (GELU_A * GELU_B) * square)
    tanh = jnp.tanh(inner)
    half = 0.5 * tanh + 0.5
    slope = half + 0.5 * values * (1.0 - tanh * tanh) * (GELU_A + (3.0 * GELU_A * GELU_B) * square)
    return values * half, slope


def fetch_grads(here, own, mirror, start, size, target, first, sems):
    side = len(own)
    copies = []
    for j in range(side):
        own_part = own[j].at[pl.ds(start, size)]
        for place, ref in ((here ^ j, own_part), ((here ^ j) ^ side, mirror[j])):
            copies.append(pltpu.make_async_copy(ref, target.at[place, pl.ds(first, size)], sems.at[len(copies)]))
    for copy in copies:
        copy.start()
    return copies


def expert_body(shards, sources, start, size, last, where_ref, x_ref, *refs):
    refs = list(refs)
    side = sources // 2

    def take(count):
        taken = refs[:count]
        del refs[:count]
        return taken

    g_own, g_mirror, weights = take(side), take(side), take(shards)
    carry_ref, prior_ref = take(2) if last and start else (None, None)
    hidden_ref, pre_ref, back_ref, rows_ref = take(4)
    carry_out = None if last else take(1)[0]
    win_v, wout_v, hid_v, pre_v, g_v, in_sems, out_sems, g_sems = refs
    arriving = fetch_grads(where_ref[1], g_own, g_mirror, start, size, g_v, 0, g_sems)
    copies = []
    for r in range(shards):
        pair = (pltpu.make_async_copy(weights[r].at[0], win_v.at[r], in_sems.at[2 * r]),
                pltpu.make_async_copy(weights[r].at[1], wout_v.at[r], in_sems.at[2 * r + 1]))
        for copy in pair:
            copy.start()
        copies.append(pair)
    width = x_ref.shape[2]
    rows = sources * size
    x = x_ref[:, 0:size, :].reshape(rows, width)
    for copy in arriving:
        copy.wait()
    g = g_v[...].reshape(rows, width)
    inner = win_v.shape[2]
    step = 256 if inner % 256 == 0 else inner
    score = jnp.zeros((rows, 1), F32)
    total, result = None, None
    outgoing = []
    for r in range(shards):
        for copy in copies[r]:
            copy.wait()
        for f in range(inner // step):
            cols = slice(f * step, (f + 1) * step)
            hid, slope = gelu_pair(dot_nn(x, win_v[r, :, cols]))
            grad = dot_nn(g, wout_v[r, :, cols])
            hid = hid.astype(BF16)
            score = score + jnp.sum(grad * hid.astype(F32), axis=1, keepdims=True)
            hid_v[r, :, cols] = hid
            pre_v[r, :, cols] = (grad * slope).astype(BF16)
        for source, target in ((hid_v, hidden_ref), (pre_v, pre_ref)):
            copy = pltpu.make_async_copy(source.at[r], target.at[r], out_sems.at[len(outgoing)])
            copy.start()
            outgoing.append(copy)
        part, out = dot_nt(pre_v[r], win_v[r]), dot_nt(hid_v[r], wout_v[r])
        total = part if total is None else total + part
        result = out if result is None else result + out
    back = total.astype(BF16).reshape(sources, size, width)
    result = result.astype(BF16).reshape(sources, size, width)
    eye = iota((size, STRIDE), 1) == iota((size, STRIDE), 0) + start
    if last:
        back_ref[:, 0:size, :] = back
        rows_ref[:, start:, :] = result
        if prior_ref is not None:
            rows_ref[:, 0:start, :] = prior_ref[...]
    else:
        back_ref[...] = back
        rows_ref[...] = result
    for s in range(sources):
        row = jnp.sum(jnp.where(eye, score[s * size : (s + 1) * size], 0.0), axis=0, keepdims=True)
        if last:
            if carry_ref is not None:
                row = row + carry_ref[s : s + 1, :]
            back_ref[s, size : size + PAYLOAD, 0 : 2 * STRIDE] = split_rows(row, PAYLOAD)
            back_ref[s, size : size + PAYLOAD, 2 * STRIDE :] = jnp.zeros((PAYLOAD, width - 2 * STRIDE), BF16)
        else:
            carry_out[s : s + 1, :] = row
    for copy in outgoing:
        copy.wait()


def expert_grad_body(picks, shards, sources, sizes, where_ref, *refs):
    refs = list(refs)
    count = len(sizes)

    def take(number):
        taken = refs[:number]
        del refs[:number]
        return taken

    side = sources // 2
    x_refs, g_own, g_mirror = take(count), take(side), [take(side) for _ in range(count)]
    hidden, pre = take(count), take(count)
    home_ref, send_ref = take(2)
    xt, gt, hid_v, pre_v, out_v, g_v, in_sems, out_sems, g_sems = refs
    arriving = []
    for index, size in enumerate(sizes):
        first = sum(sizes[:index])
        arriving += fetch_grads(where_ref[1], g_own, g_mirror[index], first, size, g_v, first, g_sems.at[index])
    copies = []
    for place, r in enumerate(picks):
        base = 0
        group = []
        for index, size in enumerate(sizes):
            rows = sources * size
            for which, (source, target) in enumerate(((pre[index], pre_v), (hidden[index], hid_v))):
                copy = pltpu.make_async_copy(source.at[r], target.at[place, pl.ds(base, rows)],
                                             in_sems.at[(place * count + index) * 2 + which])
                group.append(copy)
            base += rows
        copies.append(group)
    for copy in copies[0]:
        copy.start()
    width = x_refs[0].shape[2]
    last = x_refs[-1]
    for copy in arriving:
        copy.wait()
    start, base = 0, 0
    for ref, size in zip(x_refs, sizes):
        rows = sources * size
        eye = iota((size, STRIDE), 1) == iota((size, STRIDE), 0) + start
        gate = []
        for s in range(sources):
            row = last[s, sizes[-1] : sizes[-1] + PAYLOAD, :].astype(F32)
            row = row[0:1, 0:STRIDE] + row[0:1, STRIDE : 2 * STRIDE]
            gate.append(jnp.sum(jnp.where(eye, row, 0.0), axis=1, keepdims=True))
        gate = jnp.concatenate(gate, axis=0)
        x = ref[:, 0:size, :].reshape(rows, width).astype(F32) * gate
        g = g_v[:, start : start + size, :].reshape(rows, width).astype(F32) * gate
        xt[:, base : base + rows] = x.T.astype(BF16)
        gt[:, base : base + rows] = g.T.astype(BF16)
        start += size
        base += rows
    outgoing = []
    for place, r in enumerate(picks):
        for copy in copies[place]:
            copy.wait()
        for copy in copies[place + 1] if place + 1 < len(picks) else ():
            copy.start()
        for which, (left, right) in enumerate(((xt, pre_v), (gt, hid_v))):
            out_v[place, which] = dot_nn(left[...], right[place]).astype(BF16)
            target = (send_ref if r % 2 else home_ref).at[r // 2, which]
            copy = pltpu.make_async_copy(out_v.at[place, which], target, out_sems.at[2 * place + which])
            copy.start()
            outgoing.append(copy)
    for copy in outgoing:
        copy.wait()


def grad_sum_body(keep_ref, home_ref, got_ref, early_ref, late_ref, *out_refs):
    early, width = early_ref.shape[0], out_refs[0].shape[0]
    spans = [(0, 0, early, early_ref, 0), (0, early, width, late_ref, 0), (1, 0, width, late_ref, width - early)]
    for index, start, stop, ref, first in spans:
        total = home_ref[0, index, start:stop].astype(F32) + got_ref[0, index, start:stop].astype(F32)
        last = ref[first : first + stop - start, :].astype(F32)
        out_refs[index][start:stop, :] = (total + last) * keep_ref[0, 0]


def gather_body(rows_ref, codes_ref, col_ref, gates_ref, sum_ref):
    sources, size, width = rows_ref.shape
    codes = codes_ref[...]
    pick = jnp.where(col_ref[:, 0:1] == codes, gates_ref[:, 0:1], 0.0)
    pick = jnp.where(col_ref[:, 1:2] == codes, gates_ref[:, 1:2], pick).astype(BF16)
    sum_ref[...] = dot_nn(pick, rows_ref[...].reshape(sources * size, width))


def second_back_body(experts, size, has_sum, *refs):
    refs = list(refs)
    (rows_ref, codes_ref, col_ref, gates_ref, ids_ref, resid_ref, normed_ref, cot_ref, norms_ref, router_ref) = refs[:10]
    del refs[:10]
    sum_ref = refs.pop(0) if has_sum else None
    grad_ref, branch_ref, small_ref = refs
    sources, _, width = rows_ref.shape
    tokens = resid_ref.shape[0]
    codes = codes_ref[...]
    gates = [gates_ref[:, k : k + 1] for k in range(2)]
    slot = [col_ref[:, k : k + 1] for k in range(2)]
    pick = jnp.where(slot[0] == codes, gates[0], 0.0)
    pick = jnp.where(slot[1] == codes, gates[1], pick).astype(BF16)
    total = dot_nn(pick, rows_ref[:, 0:size, :].reshape(sources * size, width))
    if sum_ref is not None:
        total = total + sum_ref[...]
    scores = [jnp.zeros((tokens, 1), F32), jnp.zeros((tokens, 1), F32)]
    for e in range(experts):
        line = rows_ref[e, size : size + PAYLOAD, :].astype(F32)
        line = line[0:1, 0:STRIDE] + line[0:1, STRIDE : 2 * STRIDE]
        place = iota((tokens, STRIDE), 1) + e * STRIDE
        for k in range(2):
            scores[k] = scores[k] + jnp.sum(jnp.where(slot[k] == place, line, 0.0), axis=1, keepdims=True)
    inner = gates[0] * scores[0] + gates[1] * scores[1]
    lanes = iota((tokens, experts), 1)
    logit_grad = jnp.zeros((tokens, experts), F32)
    for k in range(2):
        logit_grad = jnp.where(ids_ref[:, k : k + 1] == lanes, gates[k] * (scores[k] - inner), logit_grad)
    logit_grad = logit_grad.astype(BF16)
    total = total + dot_nn(logit_grad, router_ref[...])
    normal, rate = norm_parts(resid_ref[...])
    grad = cot_ref[...].astype(F32) + norm_back(normal, rate, norms_ref[2:3, :], total)
    grad_ref[...] = grad
    branch_ref[...] = grad.astype(BF16)
    small_ref[0:1, :] = jnp.sum(total * normal, axis=0, keepdims=True)
    small_ref[1:2, :] = jnp.sum(total, axis=0, keepdims=True)
    small_ref[2 : 2 + experts, :] = dot_tn(logit_grad, normed_ref[...])


def attend_back_body(half, has_sum, where_ref, *refs):
    refs = list(refs)
    (q_ref, k_ref, v_ref, log_ref, mixed_own, mixed_other, branch_own, branch_other, own_ref, other_ref,
     w_ref) = refs[:11]
    del refs[:11]
    sums = (refs.pop(0), refs.pop(0)) if has_sum else None
    weight_ref, mine_ref, theirs_ref, rows, branch, grads, mixed, keys, vals, dq, dk, dv, joined, pile = refs
    core = where_ref[0]
    mine = pl.multiple_of(core * half, half)
    theirs = pl.multiple_of((1 - core) * half, half)
    rows[pl.ds(mine, half), :] = own_ref[...]
    rows[pl.ds(theirs, half), :] = other_ref[...]
    branch[pl.ds(mine, half), :] = branch_own[...]
    branch[pl.ds(theirs, half), :] = branch_other[...]
    mixed[pl.ds(mine, half), :] = mixed_own[...]
    mixed[pl.ds(theirs, half), :] = mixed_other[...]
    length, width = q_ref.shape
    grads[...] = dot_nt(branch[...], w_ref[3 * width :, :]).astype(BF16)
    heads = width // HD
    lane = iota((1, width), 1)
    triangle = iota((QUERY_ROWS, QUERY_ROWS), 0) >= iota((QUERY_ROWS, QUERY_ROWS), 1)
    qt = q_ref[...].astype(F32).T.astype(BF16)
    gt = grads[...].astype(F32).T.astype(BF16)
    dk[...] = jnp.zeros(dk.shape, F32)
    dv[...] = jnp.zeros(dv.shape, F32)
    for h in range(heads):
        keep = (lane >= h * HD) & (lane < (h + 1) * HD)
        keys[...] = jnp.where(keep, k_ref[...], 0)
        vals[...] = jnp.where(keep, v_ref[...], 0)
        head = slice(h * HD, (h + 1) * HD)
        for block in range(length // QUERY_ROWS):
            low = block * QUERY_ROWS
            here = slice(low, low + QUERY_ROWS)
            query, grad, log = q_ref[here, :], grads[here, :], log_ref[here, h : h + 1]
            spans = [slice(0, low)] if block else []
            spans.append(here)
            probs, outer = [], []
            inner = None
            for span in spans:
                score = dot_nt(query, keys[span, :])
                if span is here:
                    score = jnp.where(triangle, score, MASKED_SCORE)
                prob = jnp.exp(score - log)
                grad_prob = dot_nt(grad, vals[span, :])
                part = jnp.sum(prob * grad_prob, axis=1, keepdims=True)
                inner = part if inner is None else inner + part
                probs.append(prob)
                outer.append(grad_prob)
            query_grad = None
            for span, prob, grad_prob in zip(spans, probs, outer):
                score_grad = (prob * (grad_prob - inner)).astype(BF16)
                part = dot_nn(score_grad, keys[span, :])
                query_grad = part if query_grad is None else query_grad + part
                dv[head, span] = dv[head, span] + dot_nn(gt[head, here], prob.astype(BF16))
                dk[head, span] = dk[head, span] + dot_nn(qt[head, here], score_grad)
            if h:
                query_grad = query_grad + dq[here, :]
            dq[here, :] = query_grad
    query_grads = dq[...].astype(BF16).astype(F32) * HD ** (-0.5)
    joined[0:width, :] = query_grads.T.astype(BF16)
    joined[width : 2 * width, :] = dk[...].astype(BF16)
    joined[2 * width : 3 * width, :] = dv[...].astype(BF16)
    total = dot_nn(query_grads.astype(BF16), w_ref[0:width, :])
    total = total + dot_nn(dk[...].T.astype(BF16), w_ref[width : 2 * width, :])
    total = total + dot_nn(dv[...].T.astype(BF16), w_ref[2 * width : 3 * width, :])
    pile[...] = total
    one, two = pile[pl.ds(mine, half), :], pile[pl.ds(theirs, half), :]
    if sums is not None:
        one, two = one + sums[0][...], two + sums[1][...]
    mine_ref[...] = one.astype(mine_ref.dtype)
    theirs_ref[...] = two.astype(theirs_ref.dtype)
    weight_ref[0 : 3 * width, :] = dot_nn(joined[...], rows[...]).astype(weight_ref.dtype)
    turned = mixed[...].astype(F32).T.astype(BF16)
    weight_ref[3 * width :, :] = dot_nn(turned, branch[...]).astype(weight_ref.dtype)


def first_back_body(x_ref, norms_ref, mine_ref, other_ref, resid_ref, out_ref, small_ref):
    grad = mine_ref[...] + other_ref[...].astype(F32)
    normal, rate = norm_parts(x_ref[...].astype(F32))
    out_ref[...] = resid_ref[...] + norm_back(normal, rate, norms_ref[0:1, :], grad)
    small_ref[0:1, :] = jnp.sum(grad * normal, axis=0, keepdims=True)
    small_ref[1:2, :] = jnp.sum(grad, axis=0, keepdims=True)


def block_out_body(rows_ref, codes_ref, col_ref, gates_ref, resid_ref, out_ref):
    sources, size, width = rows_ref.shape
    codes = codes_ref[...]
    pick = jnp.where(col_ref[:, 0:1] == codes, gates_ref[:, 0:1], 0.0)
    pick = jnp.where(col_ref[:, 1:2] == codes, gates_ref[:, 1:2], pick).astype(BF16)
    moe = dot_nn(pick, rows_ref[...].reshape(sources * size, width))
    out_ref[...] = (resid_ref[...] + moe).astype(BF16)


def split_body(where_ref, near_ref, far_ref, *out_refs):
    side = len(out_refs)
    rows = out_refs[0].shape[1]
    here = where_ref[1]
    for j, ref in enumerate(out_refs):
        for place, block in enumerate((here ^ j, (here ^ j) ^ side)):
            part = pl.ds(pl.multiple_of(block * rows, rows), rows)
            ref[place] = (near_ref[part, :] + far_ref[part, :].astype(F32)).astype(BF16)


def half_sum_body(*refs):
    keep_ref, send_ref = refs[-2:]
    for place, out in enumerate((keep_ref, send_ref)):
        total = refs[0][place].astype(F32)
        for ref in refs[1:-2]:
            total = total + ref[place].astype(F32)
        out[...] = total.astype(out.dtype)


def final_body(where_ref, *refs):
    all_rows = refs[-1]
    pairs, outs = refs[:-5], refs[-5:-1]
    side = len(pairs)
    rows = pairs[0].shape[1]
    here = where_ref[1]
    for j in range(side):
        for place, block in enumerate((here ^ j, (here ^ j) ^ side)):
            part = pl.ds(pl.multiple_of(block * rows, rows), rows)
            all_rows[part, :] = pairs[j][place].astype(F32)
    count = outs[0].shape[0]
    for index, ref in enumerate(outs):
        ref[...] = all_rows[index * count : (index + 1) * count, :]


def swap(value, axis, step):
    size = lax.axis_size(axis)
    return lax.ppermute(value, axis, [(i, i ^ step) for i in range(size)])


def exchange(value):
    return lax.all_to_all(value, "dp", split_axis=0, concat_axis=0, tiled=True)


def after(value, *others):
    return lax.optimization_barrier((value,) + others)[0]


def codes_of(experts, start, size):
    table = np.arange(experts)[:, None] * STRIDE + start + np.arange(size)[None, :]
    return jnp.asarray(table.reshape(1, -1).astype(np.int32))


def per_device(activations, first_gain, first_shift, query_weight, key_weight, value_weight, output_weight,
               second_gain, second_shift, router_weight, expert_in, expert_out, expert_ids, capacity, new_mask,
               cotangent):
    kernel = functools.partial(call, pins=[activations, output_weight, cotangent])
    tokens, width = activations.shape
    local = query_weight.shape[1]
    heads = local // HD
    experts = router_weight.shape[1]
    sources = lax.axis_size("dp")
    shards = lax.axis_size("head")
    slots = 3 * tokens // experts
    sizes = (slots // 32 * 16, slots - slots // 32 * 16) if slots % 16 == 0 and slots >= 32 else (slots,)
    starts = tuple(sum(sizes[:i]) for i in range(len(sizes)))
    length, half, side = LENGTH, tokens, sources // 2
    where = jnp.stack([lax.axis_index("head") % 2, lax.axis_index("dp")]).astype(jnp.int32)
    last_rows = pl.BlockSpec((local, width), lambda i: (3, 0))

    attn_w = jnp.concatenate([query_weight.T, key_weight.T, value_weight.T, output_weight], axis=0)
    far_w = swap(attn_w, "head", 2)
    norms = jnp.stack([first_gain, first_shift, second_gain, second_shift])
    router = router_weight.T

    normed_first = kernel(first_norm_body, [sds((tokens, width), BF16)], "norm_first", (activations, norms), vmem=16)[0]
    normed_other = swap(normed_first, "head", 1)

    ids_row = expert_ids.T
    extra = jnp.pad(ids_row.astype(BF16), ((0, PAYLOAD - 2), (0, width - tokens)))
    mirror_grad = swap(jnp.concatenate([cotangent, extra], axis=0), "dp", side)
    routed = kernel(
        functools.partial(route_body, slots),
        [sds((tokens, 2), jnp.int32), sds((tokens, 2), jnp.int32), sds((2, tokens), jnp.int32)]
        + [sds((slots, width), BF16)] * side,
        "route", (where, ids_row, capacity, cotangent), smem=(0, 2))
    ids_col, slot_col, slot_row = routed[:3]
    grad_own = [routed[3]] + [swap(routed[3 + j], "dp", j) for j in range(1, side)]

    def attend(weight):
        return kernel(
            functools.partial(attend_body, half),
            [sds((length, local), BF16)] * 3 + [sds((length, heads), F32)] + [sds((half, local), BF16)] * 2,
            "attend", (where, normed_first, normed_other, weight), smem=(0,),
            scratch=[pltpu.VMEM((length, width), BF16), pltpu.VMEM((length, local), F32),
                     pltpu.VMEM((length, local), BF16), pltpu.VMEM((length, local), BF16)])

    near = attend(attn_w)
    mixed = {0: near[4], 1: swap(near[5], "head", 1)}
    far_w = after(far_w, near[4], slot_row)
    away = attend(far_w)
    mixed[2], mixed[3] = away[4], swap(away[5], "head", 1)
    out_w = {1: swap(output_weight, "head", 1), 3: swap(far_w[3 * local :], "head", 1)}

    weights = {0: jnp.stack([expert_in[0], expert_out[0]])}
    weights[1] = swap(weights[0], "head", 1)
    weights[2] = swap(after(weights[0], far_w), "head", 2)
    inner = weights[0].shape[2]

    mirror_send = kernel(
        functools.partial(mirror_body, slots, len(sizes)),
        [sds((size, width), BF16) for size in sizes for _ in range(side)], "mirror",
        (where, capacity, mirror_grad), smem=(0, 1))
    grad_mirror = []
    for index in range(len(sizes)):
        group = mirror_send[index * side : (index + 1) * side]
        grad_mirror.append([group[0]] + [swap(group[j], "dp", j) for j in range(1, side)])

    first_size = sizes[0] if len(sizes) > 1 else 0
    residual, normed_second, sent = kernel(
        functools.partial(post_body, experts, first_size),
        [sds((tokens, width), F32), sds((tokens, width), BF16), sds((experts, max(first_size, 16), width), BF16)],
        "post_attend",
        (activations, mixed[0], mixed[1], mixed[2], mixed[3], output_weight, out_w[1], far_w, out_w[3], norms,
         after(slot_row, mirror_grad, *grad_own[1:])), blocks={7: last_rows}, vmem=32)
    gates, sent_last = kernel(
        functools.partial(gate_body, experts, starts[-1], sizes[-1]),
        [sds((tokens, 2), F32), sds((experts, sizes[-1] + PAYLOAD, width), BF16)],
        "gates", (normed_second, router, ids_col, slot_col, slot_row))
    weights[3] = swap(after(weights[2], sent_last), "head", 1)
    rows_in = []
    if first_size:
        rows_in.append(exchange(sent))
    sent_last = after(sent_last, weights[2], *(rows_in + grad_mirror[0][1:]))
    rows_in.append(exchange(sent_last))

    hidden, pre, back = [], [], []
    carry = ()
    for index, size in enumerate(sizes):
        last = index == len(sizes) - 1
        rows = sources * size
        kept = slots if last else size
        outs = [sds((shards, rows, inner), BF16), sds((shards, rows, inner), BF16),
                sds((sources, size + (PAYLOAD if last else 0), width), BF16), sds((sources, kept, width), BF16)]
        ins = (where, rows_in[index]) + tuple(grad_own) + tuple(grad_mirror[index])
        first = len(ins)
        ins = ins + tuple(weights[r] for r in range(shards)) + carry
        if not last:
            outs.append(sds((sources, STRIDE), F32))
        result = kernel(
            functools.partial(expert_body, shards, sources, starts[index], size, last), outs, "expert", ins,
            vmem=60 if rows <= 768 else 62, smem=(0,), hbm=tuple(range(2, first + shards)), free=(2,),
            out_hbm=(0, 1),
            scratch=[pltpu.VMEM((shards, width, inner), BF16), pltpu.VMEM((shards, width, inner), BF16),
                     pltpu.VMEM((shards, rows, inner), BF16), pltpu.VMEM((shards, rows, inner), BF16),
                     pltpu.VMEM((sources, size, width), BF16), pltpu.SemaphoreType.DMA((2 * shards,)),
                     pltpu.SemaphoreType.DMA((2 * shards,)), pltpu.SemaphoreType.DMA((sources,))])
        hidden.append(result[0])
        pre.append(result[1])
        back.append(result[2])
        expert_rows = result[3]
        if not last:
            carry = (result[4], result[3])
    returned, done = [], rows_in[-1]
    for index, part in enumerate(back):
        done = exchange(after(part, done, *(grad_mirror[-1][1:] if index == 0 else ())))
        returned.append(done)

    partial_sums = ()
    if first_size:
        partial_sums = tuple(kernel(
            gather_body, [sds((tokens, width), F32)], "gather_back",
            (returned[0], codes_of(experts, 0, first_size), slot_col, gates)))

    keep = jnp.sum(jnp.where(jnp.arange(experts) == lax.axis_index("dp"), new_mask, 0)).astype(F32).reshape(1, 1)
    all_rows = sources * slots
    picks = tuple(range(1, shards, 2)) + tuple(range(0, shards, 2))
    skip = 1 + len(sizes)
    grads_home, grads_send = kernel(
        functools.partial(expert_grad_body, picks, shards, sources, sizes),
        [sds((shards // 2, 2, width, inner), BF16)] * 2, "expert_grads",
        (after(where, *partial_sums),) + tuple(rows_in) + tuple(grad_own) + sum(map(tuple, grad_mirror), ()) + tuple(hidden) + tuple(pre), vmem=60,
        smem=(0,), hbm=tuple(range(skip, skip + side * (1 + len(sizes)) + 2 * len(sizes))), out_hbm=(0, 1),
        scratch=[pltpu.VMEM((width, all_rows), BF16), pltpu.VMEM((width, all_rows), BF16),
                 pltpu.VMEM((shards, all_rows, inner), BF16), pltpu.VMEM((shards, all_rows, inner), BF16),
                 pltpu.VMEM((shards, 2, width, inner), BF16), pltpu.VMEM((sources, slots, width), BF16),
                 pltpu.SemaphoreType.DMA((4 * shards,)), pltpu.SemaphoreType.DMA((2 * shards,)),
                 pltpu.SemaphoreType.DMA((len(sizes), sources))])
    grads_got = swap(after(grads_send, returned[-1]), "head", 1)

    grad_residual, grad_branch, small_two = kernel(
        functools.partial(second_back_body, experts, sizes[-1], bool(partial_sums)),
        [sds((tokens, width), F32), sds((tokens, width), BF16), sds((2 + experts, width), F32)], "second_back",
        (returned[-1], codes_of(experts, starts[-1], sizes[-1]), slot_col, gates, ids_col, residual,
         normed_second, cotangent, norms, router) + partial_sums, free=(1, 2))
    branch_other = swap(grad_branch, "head", 1)

    early = width // 2

    def pass_on(start, stop):
        parts = [g[1].reshape(2 * width, inner)[start:stop].astype(F32) for g in (grads_home, grads_got)]
        return (parts[0] + parts[1]).astype(BF16)

    passed_first = pass_on(0, early)
    branch_other = after(branch_other, passed_first)
    passed_first = swap(passed_first, "head", 2)

    def attend_back(parts, mixed_other, weight, sums, weight_type, types):
        return kernel(
            functools.partial(attend_back_body, half, bool(sums)),
            [sds((4 * local, width), weight_type), sds((half, width), types[0]), sds((half, width), types[1])],
            "attend_back",
            (where,) + tuple(parts[:4]) + (parts[4], parts[5], grad_branch, branch_other, normed_first, normed_other,
                                           weight) + tuple(sums),
            smem=(0,), vmem=32, free=(0, 1, 2),
            scratch=[pltpu.VMEM((length, width), BF16), pltpu.VMEM((length, width), BF16),
                     pltpu.VMEM((length, local), BF16), pltpu.VMEM((length, local), BF16),
                     pltpu.VMEM((length, local), BF16), pltpu.VMEM((length, local), BF16),
                     pltpu.VMEM((length, local), F32), pltpu.VMEM((local, length), F32),
                     pltpu.VMEM((local, length), F32), pltpu.VMEM((3 * local, length), BF16),
                     pltpu.VMEM((length, width), F32)])

    far_grad, far_mine, far_theirs = attend_back(away, mixed[3], far_w, (), BF16, (F32, F32))
    far_got = swap(far_grad, "head", 2)
    branch_other = after(branch_other, passed_first)
    near_grad, near_mine, near_theirs = attend_back(near, mixed[1], attn_w, (far_mine, far_theirs), F32, (F32, BF16))
    rows_back = exchange(after(expert_rows, returned[-1], grads_home, *partial_sums))
    block_out = kernel(
        block_out_body, [sds((tokens, width), BF16)], "block_out",
        (rows_back, codes_of(experts, 0, slots), slot_col, gates, residual))[0]

    passed = pass_on(early, 2 * width)
    near_grad = after(near_grad, passed)
    passed = swap(after(passed, far_got, near_grad), "head", 2)
    block_rows = 4 * local // sources
    split = kernel(
        split_body, [sds((2, block_rows, width), BF16)] * side, "split", (where, near_grad, far_got), smem=(0,))
    split = [split[0]] + [swap(split[j], "dp", j) for j in range(1, side)]
    first_got = swap(near_theirs, "head", 1)
    grad_input, small_one = kernel(
        first_back_body, [sds((tokens, width), F32), sds((2, width), F32)], "first_back",
        (activations, norms, after(near_mine, split[0]), first_got, grad_residual))
    small = jnp.concatenate([small_one, small_two], axis=0)
    small = jnp.pad(small, ((0, -small.shape[0] % 8), (0, 0)))
    small = small + swap(small, "head", 1)
    own_sum, cross_sum = kernel(
        half_sum_body, [sds((block_rows, width), F32), sds((block_rows, width), BF16)], "half_sum",
        (after(split[0], small, block_out),) + tuple(split[1:]))
    cross_got = swap(cross_sum, "dp", side)
    small = small + swap(small, "dp", 1)
    reduced = (after(own_sum, small) + cross_got.astype(F32)).astype(BF16)
    small = small + swap(small, "dp", 2)
    pair = jnp.stack([reduced, after(swap(reduced, "dp", side), small)])
    pairs = [pair] + [swap(pair, "dp", j) for j in range(1, side)]
    step = 4
    while step < sources:
        small = small + swap(small, "dp", step)
        step *= 2

    part = pl.BlockSpec((1, 2, width, inner), lambda i: (0, 0, 0, 0))
    grad_in, grad_out = kernel(
        grad_sum_body, [sds((width, inner), F32), sds((width, inner), F32)], "grad_sum",
        (keep, grads_home, grads_got, passed_first, passed), smem=(0,), vmem=40, blocks={1: part, 2: part})

    small = small + swap(after(small, passed), "head", 2)
    pairs[0] = after(pairs[0], grad_in)
    final = kernel(
        final_body, [sds((local, width), F32)] * 4, "final", (where,) + tuple(pairs), smem=(0,),
        scratch=[pltpu.VMEM((4 * local, width), F32)])
    mask = new_mask.astype(F32)[None, :]
    return (
        block_out,
        grad_input,
        small[0],
        small[1],
        final[0].T,
        final[1].T,
        final[2].T,
        final[3],
        small[2],
        small[3],
        small[4 : 4 + experts].T * mask,
        grad_in[None],
        grad_out[None],
    )


def solution(mesh):
    placed = (
        P(("dp", "head"), None),
        P(),
        P(),
        P(None, "head"),
        P(None, "head"),
        P(None, "head"),
        P("head", None),
        P(),
        P(),
        P(),
        P("dp", None, "head"),
        P("dp", None, "head"),
        P(("dp", "head"), None),
        P(),
        P(),
        P(("dp", "head"), None),
    )
    return jax.shard_map(
        per_device,
        mesh=mesh,
        in_specs=placed,
        out_specs=(
            P(("dp", "head"), None),
            P(("dp", "head"), None),
            P(),
            P(),
            P(None, "head"),
            P(None, "head"),
            P(None, "head"),
            P("head", None),
            P(),
            P(),
            P(),
            P("dp", None, "head"),
            P("dp", None, "head"),
        ),
        check_vma=False,
    )
```
